128 devices in a mesh: wide: 8 (over z, core), narrow: 16 (over x, y).
Axes of the slice: x: 4, y: 4, z: 4, core: 2. Of those that a mesh axis runs over, the one named last changes fastest.
Arguments:
- hidden_states: float32 [4096, 4096], P('wide', 'narrow'), may hold values from -300 to 300
- out_cotangent: float32 [4096, 4096], P('wide', 'narrow'), may hold values from -6 to 6
- enc_table: float32 [128, 128, 896], P('wide', 'narrow'), may hold values from -6 to 6
- nbr_ids: int32 [64, 2], replicated, may hold values from 0 to 127, as said below
- owner_map: int32 [128], replicated, may hold values from 0 to 127, as said below
- w_query: float32 [4096, 4096], P(None, 'narrow'), may hold values from -0.09375 to 0.09375
- w_key: float32 [896, 4096], P(None, 'narrow'), may hold values from -0.1875 to 0.1875
- w_value: float32 [896, 4096], P(None, 'narrow'), may hold values from -0.1875 to 0.1875
- w_out: float32 [4096, 4096], P(None, 'narrow'), may hold values from -0.09375 to 0.09375
Outputs:
- grad_hidden: float32 [4096, 4096], P('wide', 'narrow')
- grad_query: float32 [4096, 4096], P('wide', 'narrow')
- grad_key: float32 [896, 4096], P('wide', 'narrow')
- grad_value: float32 [896, 4096], P('wide', 'narrow')
- grad_out: float32 [4096, 4096], P('wide', 'narrow')
- grad_table: float32 [128, 128, 896], P('wide', 'narrow')
The draws below stay inside these ranges and needn't reach their ends.
Inputs may be any that keep to these rules, and one draw needn't show every extreme that they name: A permutation: neighbour id n is stored in slot owner_map[n] of enc_table; slots o * 16 to (o + 1) * 16 - 1 belong to owner o. `nbr_ids`: of the 16 neighbour ids of the spans of one index of wide, at most 2 are stored with one owner, and exactly 2 with some owner. Ids may repeat.
All inputs are finite; a program needn't handle non-finite values.
Results may differ from the reference program's by a relative error of at most 0.0011.
Values sent between devices are 32-bit elements; how exact they have to be, the bound alone decides.
A program may use at most 192 MiB of HBM per device.

```python
import jax
import jax.numpy as jnp
from jax import lax

D = 4096
HEADS = 32
HEAD_DIM = 128
ENC = 896
SPAN = 64
NEIGH = 2
RET = 128
CH_DEV = 8
CAP = 2
NBW = 16
NB = 128
SPANS = 64
TOKENS = 4096


def shared_layout(key):
    placing = jax.random.permutation(jax.random.fold_in(key, 101), NB).astype(jnp.int32)
    owners_all = NB // NBW
    inst = NEIGH * CH_DEV
    blocks = SPANS // CH_DEV
    keys = jax.random.split(jax.random.fold_in(key, 202), 5)
    first = jax.random.randint(keys[0], (blocks,), 0, owners_all)
    second = jax.random.randint(keys[1], (blocks,), 0, owners_all)
    hot = first * second // owners_all
    rotation = jax.random.randint(keys[2], (blocks, 1), 0, owners_all - 1)
    position = jnp.arange(inst)[None, :]
    offset = jnp.maximum(position - CAP, 0)
    others = (hot[:, None] + 1 + (rotation + offset) % (owners_all - 1)) % owners_all
    base = jnp.where(position < CAP, hot[:, None], others)
    order = jax.vmap(lambda k: jax.random.permutation(k, inst))(jax.random.split(keys[3], blocks))
    owner = jnp.take_along_axis(base, order, axis=1)
    slot = owner * NBW + jax.random.randint(keys[4], (blocks, inst), 0, NBW)
    inverse = jnp.argsort(placing, stable=True).astype(jnp.int32)
    ids = inverse[slot.reshape(-1)].reshape(SPANS, NEIGH)
    return (placing, ids.astype(jnp.int32))


def draw_owner_map(key, part):
    layout = shared_layout(key)
    return layout[0]


def draw_nbr_ids(key, part):
    layout = shared_layout(key)
    return layout[1]


def draw_hidden_states(key, part):
    key = jax.random.fold_in(key, 7)
    return jnp.clip(jax.random.normal(key, (TOKENS, D), jnp.float32), -6.0, 6.0)


def steps_of(stream_key, dims, shards, least, top_value):
    def one(axis_at, shards_of):
        steps = jax.random.uniform(jax.random.fold_in(jax.random.fold_in(stream_key, 6), axis_at), (shards_of,), jnp.float32, least / len(shards), top_value / len(shards))
        return jnp.repeat(jnp.exp(steps), dims[axis_at] // shards_of).reshape((-1,) + (1,) * (len(dims) - axis_at - 1))

    level = one(*shards[0])
    for cut in shards[1:]:
        level = level * one(*cut)
    return level


def bell_draw(rng, shape, scale, reach, pieces=(), held_as=jnp.bfloat16):
    entries = jax.random.normal(rng, shape, jnp.float32) * scale
    if len(pieces) > 0:
        entries = steps_of(rng, shape, pieces, -0.22, 0.18) * entries
    return jnp.clip(entries, min=-reach, max=reach).astype(held_as)


def setup_inputs(seed: int = 0) -> dict:
    splits = jax.random.split(jax.random.key(seed), 10)
    hidden_states = draw_hidden_states(jax.random.fold_in(splits[9], 71), 0)
    out_cotangent = bell_draw(splits[1], (TOKENS, D), 1.0, 6.0, ((0, 8), (1, 16)), jnp.float32)
    enc_table = bell_draw(splits[2], (NB, RET, ENC), 1.0, 6.0, ((0, 8), (1, 16)), jnp.float32)
    nbr_ids = draw_nbr_ids(jax.random.fold_in(splits[9], 71), 0)
    owner_map = draw_owner_map(jax.random.fold_in(splits[9], 71), 0)
    w_query = bell_draw(splits[5], (D, D), D ** -0.5, 0.09375, ((1, 16),), jnp.float32)
    w_key = bell_draw(splits[6], (ENC, D), ENC ** -0.5, 0.1875, ((1, 16),), jnp.float32)
    w_value = bell_draw(splits[7], (ENC, D), ENC ** -0.5, 0.1875, ((1, 16),), jnp.float32)
    w_out = bell_draw(splits[8], (D, D), D ** -0.5, 0.09375, ((1, 16),), jnp.float32)
    return dict(hidden_states=hidden_states, out_cotangent=out_cotangent, enc_table=enc_table, nbr_ids=nbr_ids, owner_map=owner_map, w_query=w_query, w_key=w_key, w_value=w_value, w_out=w_out)


HIGH = lax.Precision.HIGHEST

def reference(hidden_states, out_cotangent, enc_table, nbr_ids, owner_map, w_query, w_key, w_value, w_out):
    slots = owner_map[nbr_ids]
    scale = HEAD_DIM ** (-0.5)

    def forward(inputs, wq, wk, wv, wo, table):
        neighbours = table[slots].reshape(SPANS, NEIGH * RET, ENC)
        query = jnp.dot(inputs, wq, precision=HIGH).reshape(SPANS, SPAN, HEADS, HEAD_DIM)
        keys = jnp.einsum('cne,ef->cnf', neighbours, wk, precision=HIGH).reshape(SPANS, NEIGH * RET, HEADS, HEAD_DIM)
        values = jnp.einsum('cne,ef->cnf', neighbours, wv, precision=HIGH).reshape(SPANS, NEIGH * RET, HEADS, HEAD_DIM)
        scores = jnp.einsum('cmhd,cnhd->chmn', query, keys, precision=HIGH) * scale
        probs = jax.nn.softmax(scores, axis=-1)
        attended = jnp.einsum('chmn,cnhd->cmhd', probs, values, precision=HIGH).reshape(TOKENS, D)
        return jnp.dot(attended, wo.T, precision=HIGH)
    _, pull = jax.vjp(forward, hidden_states, w_query, w_key, w_value, w_out, enc_table)
    grad_hidden, grad_query, grad_key, grad_value, grad_out, grad_table = pull(out_cotangent)
    return (grad_hidden, grad_query, grad_key, grad_value, grad_out, grad_table)
```

```python
import functools

import jax
import jax.numpy as jnp
from jax import lax
from jax.experimental import pallas as pl
from jax.experimental.pallas import tpu as pltpu
from jax.sharding import PartitionSpec as P

HEAD_DIM = 128
SPAN = 64
NEIGH = 2
SIDE = 4
VMEM_LIMIT = 60 * 1024 * 1024

HIGH = lax.Precision.HIGHEST
MID = lax.Precision.HIGH
MESH = pl.DeviceIdType.MESH


def wrap(value):
    return lax.rem(value + 2 * SIDE, SIDE)


class Place:
    def __init__(self):
        me = lax.axis_index("narrow")
        self.x = me // SIDE
        self.y = lax.rem(me, SIDE)

    def own(self, half):
        return (self.x, self.y) if half == 0 else (self.y, self.x)

    @staticmethod
    def block(half, first, second):
        return (first, second) if half == 0 else (second, first)

    def device(self, half, first, second):
        bx, by = self.block(half, first, second)
        return {"narrow": bx * SIDE + by}

    def line(self, half, turn, shift):
        first, second = self.own(half)
        if isinstance(turn, int) and turn == 0:
            return wrap(first + shift), second
        return first, wrap(second + shift)


def greet(place):
    groups = lax.axis_size("wide")
    group = lax.axis_index("wide")
    barrier = pltpu.get_barrier_semaphore()
    for half in (0, 1):
        for shift in (1, -1):
            pl.semaphore_signal(
                barrier,
                inc=1,
                device_id=place.device(half, *place.line(half, 0, shift)),
                device_id_type=MESH,
            )
    for step in range(1, groups):
        pl.semaphore_signal(
            barrier,
            inc=1,
            device_id={"wide": lax.rem(group + step, groups)},
            device_id_type=MESH,
        )
    pl.semaphore_wait(barrier, 4 + groups - 1)


def exchange(out_ref, in_ref, send, recv, local):
    groups = lax.axis_size("wide")
    group = lax.axis_index("wide")
    copies = []
    for step in range(1, groups):
        peer = lax.rem(group + step, groups)
        copy = pltpu.make_async_remote_copy(
            src_ref=out_ref.at[peer],
            dst_ref=in_ref.at[group],
            send_sem=send.at[step],
            recv_sem=recv.at[step],
            device_id={"wide": peer},
            device_id_type=MESH,
        )
        copy.start()
        copies.append(copy)
    mine = pltpu.make_async_copy(out_ref.at[group], in_ref.at[group], local)
    mine.start()
    copies.append(mine)
    return copies


class Gather:
    def __init__(self, place, buf, send, recv):
        self.place, self.buf, self.send, self.recv = place, buf, send, recv
        self.rows = buf.shape[2]

    def copy(self, half, turn, kind, block, dest):
        rows = self.rows // 2 if kind < 2 else self.rows // 4
        start = half * (self.rows // 2) + (self.rows // 4 if kind == 3 else 0)
        bx, by = self.place.block(half, *block)
        piece = self.buf.at[bx, by, pl.ds(start, rows)]
        slot = (half * 5 + turn) * 4 + kind
        return pltpu.make_async_remote_copy(
            src_ref=piece,
            dst_ref=piece,
            send_sem=self.send.at[slot],
            recv_sem=self.recv.at[slot],
            device_id=self.place.device(half, *dest),
            device_id_type=MESH,
        )

    def at(self, half, turn, shift):
        first, second = self.place.own(half)
        if isinstance(turn, int) and turn == 0:
            return wrap(first + shift), second
        return wrap(first + turn - 1), wrap(second + shift)

    def describe(self, half, turn, kind):
        shift = (0, 0, -1, 1)[kind]
        ahead = (1, -1, 1, -1)[kind]
        return self.copy(
            half, turn, kind, self.at(half, turn, shift), self.place.line(half, turn, ahead)
        )

    def arrival(self, half, turn, kind):
        shift = (-1, 1, 2, 2)[kind]
        ahead = (1, -1, 1, -1)[kind]
        return self.copy(
            half, turn, kind, self.at(half, turn, shift), self.place.line(half, turn, ahead)
        )

    def begin(self, half, turn):
        self.describe(half, turn, 0).start()
        self.describe(half, turn, 1).start()

    def forward(self, half, turn):
        for kind in (0, 1):
            self.arrival(half, turn, kind).wait_recv()
            self.describe(half, turn, kind + 2).start()

    def finish(self, half, turn):
        for kind in (2, 3):
            self.arrival(half, turn, kind).wait_recv()

    def drain(self):
        for half in (0, 1):
            for turn in range(5):
                for kind in range(4):
                    self.describe(half, turn, kind).wait_send()


def gather_kernel(
    hid_ref,
    cot_ref,
    going_ref,
    slot_ref,
    wq_ref,
    wo_ref,
    wk_ref,
    wv_ref,
    hid_out,
    cot_out,
    nei_out,
    q_ref,
    da_ref,
    keys_ref,
    values_ref,
    hid,
    cot,
    nei,
    wq,
    wo,
    wkv,
    came,
    hid_send,
    hid_recv,
    cot_send,
    cot_recv,
    nei_send,
    nei_recv,
    swap_send,
    swap_recv,
    load_sem,
    store_sem,
):
    place = Place()
    x, y = place.x, place.y
    width = q_ref.shape[1]
    tokens = q_ref.shape[0]
    piece_rows = going_ref.shape[2]
    inst = nei.shape[2] // piece_rows
    cap = going_ref.shape[1]
    own = [
        pltpu.make_async_copy(hid_ref, hid.at[x, y], load_sem.at[0]),
        pltpu.make_async_copy(cot_ref, cot.at[x, y], load_sem.at[1]),
    ]
    weights = [
        pltpu.make_async_copy(wq_ref, wq, load_sem.at[2]),
        pltpu.make_async_copy(wo_ref, wo, load_sem.at[3]),
        pltpu.make_async_copy(wk_ref, wkv.at[:, pl.ds(0, width)], load_sem.at[4]),
        pltpu.make_async_copy(wv_ref, wkv.at[:, pl.ds(width, width)], load_sem.at[5]),
    ]
    for copy in own:
        copy.start()
    greet(place)
    swaps = exchange(going_ref, came, swap_send, swap_recv, load_sem.at[6])
    for copy in own:
        copy.wait()
    gathers = [
        Gather(place, hid, hid_send, hid_recv),
        Gather(place, cot, cot_send, cot_recv),
        Gather(place, nei, nei_send, nei_recv),
    ]
    for turn in (0, 1):
        for gather in gathers[:2]:
            for half in (0, 1):
                gather.begin(half, turn)
    for copy in weights:
        copy.start()
    for copy in swaps:
        copy.wait()
    for i in range(inst):
        slot = slot_ref[i]
        nei[x, y, pl.ds(i * piece_rows, piece_rows), :] = came[slot // cap, lax.rem(slot, cap)]
    for turn in (0, 1):
        for half in (0, 1):
            gathers[2].begin(half, turn)
    for gather in gathers:
        for half in (0, 1):
            gather.forward(half, 0)
        for half in (0, 1):
            gather.begin(half, 2)
            gather.begin(half, 4)
    for gather in gathers:
        for half in (0, 1):
            gather.finish(half, 0)
            gather.begin(half, 3)
    for copy in weights:
        copy.wait()
    q_ref[...] = jnp.zeros_like(q_ref)
    da_ref[...] = jnp.zeros_like(da_ref)

    def turn_of(step):
        return step + (step // 2) * (1 - 2 * lax.rem(step, 2)) + 1

    def project(half, first):
        rows = pl.ds(half * (tokens // 2), tokens // 2)

        def column(second, carry):
            bx, by = place.block(half, first, second)
            part = pl.ds(pl.multiple_of((bx * SIDE + by) * width, width), width)
            q_ref[rows, :] += jnp.dot(
                hid[bx, by, rows, :], wq[part, :], precision=HIGH,
                preferred_element_type=jnp.float32,
            )
            da_ref[rows, :] += jnp.dot(
                cot[bx, by, rows, :], wo[part, :], precision=HIGH,
                preferred_element_type=jnp.float32,
            )
            return carry

        lax.fori_loop(0, SIDE, column, 0)
        few = nei.shape[2] // 2
        rows = pl.ds(half * few, few)
        if half == 0:
            blocks = nei[first, :, rows, :]
        else:
            blocks = nei[:, first, rows, :]
        both = jnp.dot(
            blocks.reshape(SIDE * few, nei.shape[3]), wkv[...], precision=HIGH,
            preferred_element_type=jnp.float32,
        ).reshape(SIDE, few, 2 * width)
        if half == 0:
            keys_ref[first, :, rows, :] = both[:, :, :width]
            values_ref[first, :, rows, :] = both[:, :, width:]
        else:
            keys_ref[:, first, rows, :] = both[:, :, :width]
            values_ref[:, first, rows, :] = both[:, :, width:]

    def keep(half, turn, first):
        copies = []
        for which, (buf, out) in enumerate(((hid, hid_out), (cot, cot_out), (nei, nei_out))):
            rows = pl.ds(half * (buf.shape[2] // 2), buf.shape[2] // 2)
            at = (first, slice(None), rows) if half == 0 else (slice(None), first, rows)
            copies.append(
                pltpu.make_async_copy(
                    buf.at[at], out.at[at], store_sem.at[(which * 2 + half) * 5 + turn]
                )
            )
        return copies

    def pass_on(turn):
        for gather in gathers:
            for half in (0, 1):
                gather.forward(half, turn)

    pass_on(turn_of(0))

    def main(step, carry):
        @pl.when(step < SIDE - 1)
        def _():
            pass_on(turn_of(step + 1))

        turn = turn_of(step)
        for half in (0, 1):
            for gather in gathers:
                gather.finish(half, turn)
            first = wrap(place.own(half)[0] + turn - 1)
            for copy in keep(half, turn, first):
                copy.start()
            project(half, first)
        return carry

    lax.fori_loop(0, SIDE, main, 0)
    for gather in gathers:
        gather.drain()

    def stored(turn, carry):
        for half in (0, 1):
            first = wrap(place.own(half)[0] + turn - 1)
            for copy in keep(half, turn, first):
                copy.wait()
        return carry

    lax.fori_loop(1, SIDE + 1, stored, 0)


class Reduce:
    def __init__(self, place, part, whole_in, quarter_in, send, recv):
        self.place, self.part = place, part
        self.whole_in, self.quarter_in = whole_in, quarter_in
        self.send, self.recv = send, recv
        self.rows = part.shape[2]

    def at(self, half, turn, shift):
        first, second = self.place.own(half)
        if isinstance(turn, int) and turn == 0:
            return wrap(first + shift), second
        return wrap(first + turn - 1), wrap(second + shift)

    def piece(self, half, block, kind):
        rows = self.rows // 2 if kind < 2 else self.rows // 4
        start = half * (self.rows // 2) + (self.rows // 4 if kind == 3 else 0)
        bx, by = self.place.block(half, *block)
        return bx, by, pl.ds(start, rows)

    def copy(self, half, turn, kind):
        ahead = (1, -1, 1, -1)[kind]
        shift = (1, -1, 2, 2)[kind]
        slot = (half * 5 + turn) * 2 + kind % 2
        landing = (self.whole_in if kind < 2 else self.quarter_in).at[slot]
        bx, by, rows = self.piece(half, self.at(half, turn, shift), kind)
        sem = (half * 5 + turn) * 4 + kind
        return pltpu.make_async_remote_copy(
            src_ref=self.part.at[bx, by, rows],
            dst_ref=landing,
            send_sem=self.send.at[sem],
            recv_sem=self.recv.at[sem],
            device_id=self.place.device(half, *self.place.line(half, turn, ahead)),
            device_id_type=MESH,
        )

    def begin(self, half, turn):
        for kind in (2, 3):
            self.copy(half, turn, kind).start()

    def middle(self, half, turn):
        for kind in (2, 3):
            self.copy(half, turn, kind).wait_recv()
            slot = (half * 5 + turn) * 2 + kind % 2
            shift = 1 if kind == 2 else -1
            bx, by, rows = self.piece(half, self.at(half, turn, shift), kind)
            self.part[bx, by, rows, :] += self.quarter_in[slot]
            self.copy(half, turn, kind - 2).start()

    def finish(self, half, turn):
        for kind in (0, 1):
            self.copy(half, turn, kind).wait_recv()
        slot = (half * 5 + turn) * 2
        bx, by, rows = self.piece(half, self.at(half, turn, 0), 0)
        self.part[bx, by, rows, :] += self.whole_in[slot] + self.whole_in[slot + 1]

    def drain(self):
        for half in (0, 1):
            for turn in range(5):
                for kind in range(4):
                    self.copy(half, turn, kind).wait_send()


TURNS = (3, 2, 4, 1)


def reduce_kernel(
    dq_ref,
    dk_ref,
    dv_ref,
    inst_ref,
    wq_ref,
    wk_ref,
    wv_ref,
    gh_ref,
    came_ref,
    gpart,
    dpart,
    ghalf,
    gquarter,
    dhalf,
    dquarter,
    wq,
    wk,
    wv,
    going,
    mine,
    g_send,
    g_recv,
    d_send,
    d_recv,
    swap_send,
    swap_recv,
    load_sem,
):
    place = Place()
    x, y = place.x, place.y
    tokens, width = dq_ref.shape
    groups, cap, piece_rows, _ = going.shape
    weights = [
        pltpu.make_async_copy(wq_ref, wq, load_sem.at[0]),
        pltpu.make_async_copy(wk_ref, wk, load_sem.at[1]),
        pltpu.make_async_copy(wv_ref, wv, load_sem.at[2]),
    ]
    for copy in weights:
        copy.start()
    greet(place)
    for copy in weights:
        copy.wait()
    wide_sum = Reduce(place, gpart, ghalf, gquarter, g_send, g_recv)
    near_sum = Reduce(place, dpart, dhalf, dquarter, d_send, d_recv)
    transposed = (((1,), (1,)), ((), ()))

    def hidden_part(half, block):
        bx, by = place.block(half, *block)
        rows = pl.ds(half * (tokens // 2), tokens // 2)
        part = pl.ds(pl.multiple_of((bx * SIDE + by) * width, width), width)
        gpart[bx, by, rows, :] = lax.dot_general(
            dq_ref[rows, :], wq[part, :], transposed, precision=HIGH,
            preferred_element_type=jnp.float32,
        )

    def order(step):
        return 3 - step + 3 * (step // 2) - 2 * (step // 3)

    def g_first(step, carry):
        turn = order(step)
        for half in (0, 1):
            hidden_part(half, wide_sum.at(half, turn, 2))
            wide_sum.begin(half, turn)
        return carry

    lax.fori_loop(0, SIDE, g_first, 0)

    def d_all(step, carry):
        bx, by = step // SIDE, lax.rem(step, SIDE)
        dpart[bx, by] = lax.dot_general(
            dk_ref[bx, by], wk[...], transposed, precision=HIGH,
            preferred_element_type=jnp.float32,
        ) + lax.dot_general(
            dv_ref[bx, by], wv[...], transposed, precision=HIGH,
            preferred_element_type=jnp.float32,
        )
        return carry

    lax.fori_loop(0, SIDE * SIDE, d_all, 0)
    for turn in TURNS:
        for half in (0, 1):
            near_sum.begin(half, turn)

    def g_second(step, carry):
        turn = order(step)
        for half in (0, 1):
            for shift in (1, -1):
                hidden_part(half, wide_sum.at(half, turn, shift))
            wide_sum.middle(half, turn)
        return carry

    lax.fori_loop(0, SIDE, g_second, 0)
    for turn in TURNS:
        for half in (0, 1):
            near_sum.middle(half, turn)
    def g_third(step, carry):
        turn = order(step)
        for half in (0, 1):
            hidden_part(half, wide_sum.at(half, turn, 0))
        return carry

    lax.fori_loop(0, SIDE, g_third, 0)
    for target in (wide_sum, near_sum):
        for half in (0, 1):
            target.finish(half, 3)
            target.begin(half, 0)
        for half in (0, 1):
            for turn in (2, 4):
                target.finish(half, turn)
            target.middle(half, 0)
        for half in (0, 1):
            target.finish(half, 1)
    for half in (0, 1):
        near_sum.finish(half, 0)
    for i in range(groups * cap):
        mine[i] = dpart[x, y, pl.ds(i * piece_rows, piece_rows), :]
    for slot in range(groups * cap):
        going[slot // cap, slot % cap] = mine[inst_ref[slot]]
    swaps = exchange(going, came_ref, swap_send, swap_recv, load_sem.at[3])
    for half in (0, 1):
        wide_sum.finish(half, 0)
    gh_ref[...] = gpart[x, y]
    for copy in swaps:
        copy.wait()
    wide_sum.drain()
    near_sum.drain()


def attention_kernel(q_ref, da_ref, keys_ref, values_ref, att_ref, dq_ref, dk_ref, dv_ref):
    scale = HEAD_DIM ** (-0.5)
    heads = q_ref.shape[1] // HEAD_DIM
    spans = q_ref.shape[0] // SPAN
    few = keys_ref.shape[2] // spans
    near = SIDE * SIDE * few

    def dot(a, b, ca, cb):
        return lax.dot_general(
            a, b, (((ca,), (cb,)), ((), ())), precision=HIGH, preferred_element_type=jnp.float32
        )

    def span(c, carry):
        rows = pl.ds(pl.multiple_of(c * SPAN, SPAN), SPAN)
        pieces = pl.ds(pl.multiple_of(c * few, few), few)
        for head in range(heads):
            cols = pl.ds(head * HEAD_DIM, HEAD_DIM)
            q = q_ref[rows, cols]
            da = da_ref[rows, cols]
            k = keys_ref[:, :, pieces, cols].reshape(near, HEAD_DIM)
            v = values_ref[:, :, pieces, cols].reshape(near, HEAD_DIM)
            scores = dot(q, k, 1, 1) * scale
            top = jnp.max(scores, axis=-1, keepdims=True)
            e = jnp.exp(scores - top)
            probs = e / jnp.sum(e, axis=-1, keepdims=True)
            att_ref[rows, cols] = dot(probs, v, 1, 0)
            dp = dot(da, v, 1, 1)
            ds = probs * (dp - jnp.sum(dp * probs, axis=-1, keepdims=True)) * scale
            dq_ref[rows, cols] = dot(ds, k, 1, 0)
            shape = (SIDE, SIDE, few, HEAD_DIM)
            dk_ref[:, :, pieces, cols] = dot(ds, q, 0, 0).reshape(shape)
            dv_ref[:, :, pieces, cols] = dot(probs, da, 0, 0).reshape(shape)
        return carry

    lax.fori_loop(0, spans, span, 0)


def vmem(n):
    return [pl.BlockSpec(memory_space=pltpu.VMEM)] * n


def hbm(n):
    return [pl.BlockSpec(memory_space=pl.ANY)] * n


def smem(n):
    return [pl.BlockSpec(memory_space=pltpu.SMEM)] * n


def f32(*shape):
    return jax.ShapeDtypeStruct(shape, jnp.float32)


def gather_call(hidden, cotangent, outgoing, slots, wq, wo, wk, wv):
    tokens, width = hidden.shape
    groups, cap, piece_rows, enc = outgoing.shape
    rows = slots.shape[0] * piece_rows
    dma = pltpu.SemaphoreType.DMA
    out_shape = [
        f32(SIDE, SIDE, tokens, width),
        f32(SIDE, SIDE, tokens, width),
        f32(SIDE, SIDE, rows, enc),
        f32(tokens, width),
        f32(tokens, width),
        f32(SIDE, SIDE, rows, width),
        f32(SIDE, SIDE, rows, width),
    ]
    scratch = [
        pltpu.VMEM((SIDE, SIDE, tokens, width), jnp.float32),
        pltpu.VMEM((SIDE, SIDE, tokens, width), jnp.float32),
        pltpu.VMEM((SIDE, SIDE, rows, enc), jnp.float32),
        pltpu.VMEM(wq.shape, jnp.float32),
        pltpu.VMEM(wo.shape, jnp.float32),
        pltpu.VMEM((enc, 2 * width), jnp.float32),
        pltpu.VMEM(outgoing.shape, jnp.float32),
    ]
    scratch += [dma((40,))] * 6 + [dma((groups,))] * 2 + [dma((8,)), dma((30,))]
    return pl.pallas_call(
        gather_kernel,
        out_shape=out_shape,
        in_specs=hbm(2) + vmem(1) + smem(1) + hbm(4),
        out_specs=hbm(3) + vmem(4),
        scratch_shapes=scratch,
        compiler_params=pltpu.CompilerParams(
            collective_id=0, has_side_effects=True, vmem_limit_bytes=VMEM_LIMIT
        ),
        cost_estimate=pl.CostEstimate(flops=24_000_000_000, bytes_accessed=60_000_000, transcendentals=0),
    )(hidden, cotangent, outgoing, slots, wq, wo, wk, wv)


def reduce_call(dq, dk, dv, inst_of, wq, wk, wv, groups):
    tokens, width = dq.shape
    rows = dk.shape[2]
    enc = wk.shape[0]
    slots = inst_of.shape[0]
    cap = slots // groups
    piece_rows = rows // slots
    dma = pltpu.SemaphoreType.DMA
    going = (groups, cap, piece_rows, enc)
    scratch = [
        pltpu.VMEM((SIDE, SIDE, tokens, width), jnp.float32),
        pltpu.VMEM((SIDE, SIDE, rows, enc), jnp.float32),
        pltpu.VMEM((20, tokens // 2, width), jnp.float32),
        pltpu.VMEM((20, tokens // 4, width), jnp.float32),
        pltpu.VMEM((20, rows // 2, enc), jnp.float32),
        pltpu.VMEM((20, rows // 4, enc), jnp.float32),
        pltpu.VMEM(wq.shape, jnp.float32),
        pltpu.VMEM(wk.shape, jnp.float32),
        pltpu.VMEM(wv.shape, jnp.float32),
        pltpu.VMEM(going, jnp.float32),
        pltpu.VMEM((slots, piece_rows, enc), jnp.float32),
    ]
    scratch += [dma((40,))] * 4 + [dma((groups,))] * 2 + [dma((4,))]
    return pl.pallas_call(
        reduce_kernel,
        out_shape=[f32(tokens, width), f32(*going)],
        in_specs=vmem(3) + smem(1) + hbm(3),
        out_specs=vmem(2),
        scratch_shapes=scratch,
        compiler_params=pltpu.CompilerParams(
            collective_id=1, has_side_effects=True, vmem_limit_bytes=VMEM_LIMIT
        ),
        cost_estimate=pl.CostEstimate(flops=50_000_000_000, bytes_accessed=60_000_000, transcendentals=0),
    )(dq, dk, dv, inst_of, wq, wk, wv)


def body(
    hidden_states, out_cotangent, enc_table, nbr_ids, owner_map, w_query, w_key, w_value, w_out
):
    groups = lax.axis_size("wide")
    group = lax.axis_index("wide")
    stored = enc_table.shape[0]
    table_size = owner_map.shape[0]
    tokens, width = hidden_states.shape
    inst = NEIGH * (tokens // SPAN)
    capacity = inst // groups
    match = nbr_ids[:, :, None] == jnp.arange(table_size, dtype=jnp.int32)[None, None, :]
    slots = jnp.sum(jnp.where(match, owner_map[None, None, :], 0), axis=-1)
    slots = slots.reshape(groups, inst)
    owners = slots // stored
    local_slot = slots - owners * stored
    earlier = jnp.arange(inst)[None, :] < jnp.arange(inst)[:, None]
    same = owners[:, :, None] == owners[:, None, :]
    rank = jnp.sum((same & earlier[None, :, :]).astype(jnp.int32), axis=-1)
    slot_range = jnp.arange(capacity, dtype=jnp.int32)
    pick = ((owners[:, None, :] == group) & (rank[:, None, :] == slot_range[None, :, None])).astype(
        jnp.float32
    )
    one_local = (
        local_slot[:, :, None] == jnp.arange(stored, dtype=jnp.int32)[None, None, :]
    ).astype(jnp.float32)
    place = jnp.einsum("bri,bis->brs", pick, one_local, precision=HIGH)
    outgoing = jnp.einsum("brs,sxe->brxe", place, enc_table, precision=HIGH)
    mine = lax.dynamic_index_in_dim(owners * capacity + rank, group, 0, keepdims=False)
    numbers = jnp.arange(inst, dtype=jnp.int32)
    inst_of = jnp.sum(jnp.where(mine[None, :] == numbers[:, None], numbers[None, :], 0), axis=1)

    hid, cot, nei, query, d_att, keys, values = gather_call(
        hidden_states, out_cotangent, outgoing, mine, w_query, w_out, w_key, w_value
    )
    rows, enc = nei.shape[2:]
    attended, d_query, d_keys, d_values = pl.pallas_call(
        attention_kernel,
        out_shape=[f32(*t.shape) for t in (query, query, keys, values)],
        in_specs=vmem(4),
        out_specs=vmem(4),
        compiler_params=pltpu.CompilerParams(vmem_limit_bytes=40 * 1024 * 1024),
    )(query, d_att, keys, values)

    def over_tokens(a, b):
        out = jnp.einsum("mtf,td->mfd", a.reshape(SIDE * SIDE, tokens, width), b, precision=MID)
        return lax.psum_scatter(
            out.reshape(-1, width), "wide", scatter_dimension=0, tiled=True
        )

    def over_rows(b):
        out = lax.dot_general(
            nei.reshape(-1, enc), b.reshape(-1, width), (((0,), (0,)), ((), ())), precision=MID
        )
        return lax.psum_scatter(out, "wide", scatter_dimension=0, tiled=True)

    grad_out = over_tokens(cot, attended)
    grad_query = over_tokens(hid, d_query)
    grad_key = over_rows(d_keys)
    grad_value = over_rows(d_values)
    grad_hidden, arrived = reduce_call(
        d_query, d_keys, d_values, inst_of, w_query, w_key, w_value, groups
    )
    grad_table = jnp.einsum("brs,brxe->sxe", place, arrived, precision=HIGH)
    return (grad_hidden, grad_query, grad_key, grad_value, grad_out, grad_table)


def solution(mesh):
    placed = (
        P("wide", "narrow"),
        P("wide", "narrow"),
        P("wide", "narrow", None),
        P(),
        P(),
        P(None, "narrow"),
        P(None, "narrow"),
        P(None, "narrow"),
        P(None, "narrow"),
    )
    return jax.shard_map(
        body,
        mesh=mesh,
        in_specs=placed,
        out_specs=(
            P("wide", "narrow"),
            P("wide", "narrow"),
            P("wide", "narrow"),
            P("wide", "narrow"),
            P("wide", "narrow"),
            P("wide", "narrow", None),
        ),
        check_vma=False,
    )
```

```python
import functools

import jax
import jax.numpy as jnp
from jax import lax
from jax.experimental import pallas as pl
from jax.experimental.pallas import tpu as pltpu
from jax.sharding import PartitionSpec as P

HEAD_DIM = 128
SPAN = 64
NEIGH = 2
SIDE = 4
VMEM_LIMIT = 60 * 1024 * 1024
REDUCE_LIMIT = 63 * 1024 * 1024

HIGH = lax.Precision.HIGHEST
MID = lax.Precision.HIGH
MESH = pl.DeviceIdType.MESH


def wrap(value):
    return lax.rem(value + 2 * SIDE, SIDE)


class Place:
    def __init__(self):
        me = lax.axis_index("narrow")
        self.x = me // SIDE
        self.y = lax.rem(me, SIDE)

    def own(self, half):
        return (self.x, self.y) if half == 0 else (self.y, self.x)

    @staticmethod
    def block(half, first, second):
        return (first, second) if half == 0 else (second, first)

    def device(self, half, first, second):
        bx, by = self.block(half, first, second)
        return {"narrow": bx * SIDE + by}

    def line(self, half, turn, shift):
        first, second = self.own(half)
        if isinstance(turn, int) and turn == 0:
            return wrap(first + shift), second
        return first, wrap(second + shift)


def greet(place):
    groups = lax.axis_size("wide")
    group = lax.axis_index("wide")
    barrier = pltpu.get_barrier_semaphore()
    for half in (0, 1):
        for shift in (1, -1):
            pl.semaphore_signal(
                barrier,
                inc=1,
                device_id=place.device(half, *place.line(half, 0, shift)),
                device_id_type=MESH,
            )
    for step in range(1, groups):
        pl.semaphore_signal(
            barrier,
            inc=1,
            device_id={"wide": lax.rem(group + step, groups)},
            device_id_type=MESH,
        )
    pl.semaphore_wait(barrier, 4 + groups - 1)


def exchange(out_ref, in_ref, send, recv, local):
    groups = lax.axis_size("wide")
    group = lax.axis_index("wide")
    copies = []
    for step in range(1, groups):
        peer = lax.rem(group + step, groups)
        copy = pltpu.make_async_remote_copy(
            src_ref=out_ref.at[peer],
            dst_ref=in_ref.at[group],
            send_sem=send.at[step],
            recv_sem=recv.at[step],
            device_id={"wide": peer},
            device_id_type=MESH,
        )
        copy.start()
        copies.append(copy)
    mine = pltpu.make_async_copy(out_ref.at[group], in_ref.at[group], local)
    mine.start()
    copies.append(mine)
    return copies


class Gather:
    def __init__(self, place, buf, send, recv):
        self.place, self.buf, self.send, self.recv = place, buf, send, recv
        self.rows = buf.shape[2]

    def copy(self, half, turn, kind, block, dest):
        rows = self.rows // 2 if kind < 2 else self.rows // 4
        start = half * (self.rows // 2) + (self.rows // 4 if kind == 3 else 0)
        bx, by = self.place.block(half, *block)
        piece = self.buf.at[bx, by, pl.ds(start, rows)]
        slot = (half * 5 + turn) * 4 + kind
        return pltpu.make_async_remote_copy(
            src_ref=piece,
            dst_ref=piece,
            send_sem=self.send.at[slot],
            recv_sem=self.recv.at[slot],
            device_id=self.place.device(half, *dest),
            device_id_type=MESH,
        )

    def at(self, half, turn, shift):
        first, second = self.place.own(half)
        if isinstance(turn, int) and turn == 0:
            return wrap(first + shift), second
        return wrap(first + turn - 1), wrap(second + shift)

    def describe(self, half, turn, kind):
        shift = (0, 0, -1, 1)[kind]
        ahead = (1, -1, 1, -1)[kind]
        return self.copy(
            half, turn, kind, self.at(half, turn, shift), self.place.line(half, turn, ahead)
        )

    def arrival(self, half, turn, kind):
        shift = (-1, 1, 2, 2)[kind]
        ahead = (1, -1, 1, -1)[kind]
        return self.copy(
            half, turn, kind, self.at(half, turn, shift), self.place.line(half, turn, ahead)
        )

    def begin(self, half, turn):
        self.describe(half, turn, 0).start()
        self.describe(half, turn, 1).start()

    def forward(self, half, turn):
        for kind in (0, 1):
            self.arrival(half, turn, kind).wait_recv()
            self.describe(half, turn, kind + 2).start()

    def finish(self, half, turn):
        for kind in (2, 3):
            self.arrival(half, turn, kind).wait_recv()

    def drain(self):
        for half in (0, 1):
            for turn in range(5):
                for kind in range(4):
                    self.describe(half, turn, kind).wait_send()


def attend(q_ref, da_ref, keys_ref, values_ref, att_ref, dq_ref, dk_ref, dv_ref):
    scale = HEAD_DIM ** (-0.5)
    heads = q_ref.shape[1] // HEAD_DIM
    spans = q_ref.shape[0] // SPAN
    few = keys_ref.shape[2] // spans
    near = SIDE * SIDE * few

    def dot(a, b, ca, cb, precision=MID):
        return lax.dot_general(
            a, b, (((ca,), (cb,)), ((), ())), precision=precision,
            preferred_element_type=jnp.float32,
        )

    def span(c, carry):
        rows = pl.ds(pl.multiple_of(c * SPAN, SPAN), SPAN)
        pieces = pl.ds(pl.multiple_of(c * few, few), few)
        for head in range(heads):
            cols = pl.ds(head * HEAD_DIM, HEAD_DIM)
            q = q_ref[rows, cols]
            da = da_ref[rows, cols]
            k = keys_ref[:, :, pieces, cols].reshape(near, HEAD_DIM)
            v = values_ref[:, :, pieces, cols].reshape(near, HEAD_DIM)
            scores = dot(q, k, 1, 1, HIGH) * scale
            dp = dot(da, v, 1, 1)
            top = jnp.max(scores, axis=-1, keepdims=True)
            e = jnp.exp(scores - top)
            probs = e / jnp.sum(e, axis=-1, keepdims=True)
            ds = probs * (dp - jnp.sum(dp * probs, axis=-1, keepdims=True)) * scale
            att_ref[rows, cols] = dot(probs, v, 1, 0)
            dq_ref[rows, cols] = dot(ds, k, 1, 0)
            shape = (SIDE, SIDE, few, HEAD_DIM)
            dk_ref[:, :, pieces, cols] = dot(ds, q, 0, 0).reshape(shape)
            dv_ref[:, :, pieces, cols] = dot(probs, da, 0, 0).reshape(shape)
        return carry

    lax.fori_loop(0, spans, span, 0)


def gather_kernel(
    hid_ref,
    cot_ref,
    going_ref,
    slot_ref,
    wq_ref,
    wo_ref,
    wk_ref,
    wv_ref,
    hid_out,
    cot_out,
    nei_out,
    att_ref,
    dq_ref,
    dk_ref,
    dv_ref,
    q_ref,
    da_ref,
    keys_ref,
    values_ref,
    hid,
    cot,
    nei,
    wq,
    wo,
    wkv,
    came,
    hid_send,
    hid_recv,
    cot_send,
    cot_recv,
    nei_send,
    nei_recv,
    swap_send,
    swap_recv,
    load_sem,
    store_sem,
):
    place = Place()
    x, y = place.x, place.y
    width = q_ref.shape[1]
    tokens = q_ref.shape[0]
    piece_rows = going_ref.shape[2]
    inst = nei.shape[2] // piece_rows
    cap = going_ref.shape[1]
    own = [
        pltpu.make_async_copy(hid_ref, hid.at[x, y], load_sem.at[0]),
        pltpu.make_async_copy(cot_ref, cot.at[x, y], load_sem.at[1]),
    ]
    weights = [
        pltpu.make_async_copy(wq_ref, wq, load_sem.at[2]),
        pltpu.make_async_copy(wo_ref, wo, load_sem.at[3]),
        pltpu.make_async_copy(wk_ref, wkv.at[:, pl.ds(0, width)], load_sem.at[4]),
        pltpu.make_async_copy(wv_ref, wkv.at[:, pl.ds(width, width)], load_sem.at[5]),
    ]
    for copy in own:
        copy.start()
    greet(place)
    swaps = exchange(going_ref, came, swap_send, swap_recv, load_sem.at[6])
    for copy in own:
        copy.wait()
    gathers = [
        Gather(place, hid, hid_send, hid_recv),
        Gather(place, cot, cot_send, cot_recv),
        Gather(place, nei, nei_send, nei_recv),
    ]
    for turn in (0, 1):
        for gather in gathers[:2]:
            for half in (0, 1):
                gather.begin(half, turn)
    for copy in weights:
        copy.start()
    for copy in swaps:
        copy.wait()
    for i in range(inst):
        slot = slot_ref[i]
        nei[x, y, pl.ds(i * piece_rows, piece_rows), :] = came[slot // cap, lax.rem(slot, cap)]
    for turn in (0, 1):
        for half in (0, 1):
            gathers[2].begin(half, turn)
    for gather in gathers:
        for half in (0, 1):
            gather.forward(half, 0)
        for half in (0, 1):
            gather.begin(half, 2)
            gather.begin(half, 4)
    for gather in gathers:
        for half in (0, 1):
            gather.finish(half, 0)
            gather.begin(half, 3)
    for copy in weights:
        copy.wait()
    q_ref[...] = jnp.zeros_like(q_ref)
    da_ref[...] = jnp.zeros_like(da_ref)

    def turn_of(step):
        return step + (step // 2) * (1 - 2 * lax.rem(step, 2)) + 1

    def project(half, first):
        rows = pl.ds(half * (tokens // 2), tokens // 2)

        def column(second, carry):
            bx, by = place.block(half, first, second)
            part = pl.ds(pl.multiple_of((bx * SIDE + by) * width, width), width)
            q_ref[rows, :] += jnp.dot(
                hid[bx, by, rows, :], wq[part, :], precision=HIGH,
                preferred_element_type=jnp.float32,
            )
            da_ref[rows, :] += jnp.dot(
                cot[bx, by, rows, :], wo[part, :], precision=MID,
                preferred_element_type=jnp.float32,
            )
            return carry

        lax.fori_loop(0, SIDE, column, 0)
        few = nei.shape[2] // 2
        rows = pl.ds(half * few, few)
        if half == 0:
            blocks = nei[first, :, rows, :]
        else:
            blocks = nei[:, first, rows, :]
        both = jnp.dot(
            blocks.reshape(SIDE * few, nei.shape[3]), wkv[...], precision=HIGH,
            preferred_element_type=jnp.float32,
        ).reshape(SIDE, few, 2 * width)
        if half == 0:
            keys_ref[first, :, rows, :] = both[:, :, :width]
            values_ref[first, :, rows, :] = both[:, :, width:]
        else:
            keys_ref[:, first, rows, :] = both[:, :, :width]
            values_ref[:, first, rows, :] = both[:, :, width:]

    def keep(half, turn, first):
        copies = []
        for which, (buf, out) in enumerate(((hid, hid_out), (cot, cot_out), (nei, nei_out))):
            rows = pl.ds(half * (buf.shape[2] // 2), buf.shape[2] // 2)
            at = (first, slice(None), rows) if half == 0 else (slice(None), first, rows)
            copies.append(
                pltpu.make_async_copy(
                    buf.at[at], out.at[at], store_sem.at[(which * 2 + half) * 5 + turn]
                )
            )
        return copies

    def pass_on(turn):
        for gather in gathers:
            for half in (0, 1):
                gather.forward(half, turn)

    pass_on(turn_of(0))

    def main(step, carry):
        @pl.when(step < SIDE - 1)
        def _():
            pass_on(turn_of(step + 1))

        turn = turn_of(step)
        for half in (0, 1):
            for gather in gathers:
                gather.finish(half, turn)
            first = wrap(place.own(half)[0] + turn - 1)
            for copy in keep(half, turn, first):
                copy.start()
            project(half, first)
        return carry

    lax.fori_loop(0, SIDE, main, 0)
    attend(q_ref, da_ref, keys_ref, values_ref, att_ref, dq_ref, dk_ref, dv_ref)
    for gather in gathers:
        gather.drain()

    def stored(turn, carry):
        for half in (0, 1):
            first = wrap(place.own(half)[0] + turn - 1)
            for copy in keep(half, turn, first):
                copy.wait()
        return carry

    lax.fori_loop(1, SIDE + 1, stored, 0)


class Reduce:
    def __init__(self, place, part, whole_in, quarter_in, send, recv):
        self.place, self.part = place, part
        self.whole_in, self.quarter_in = whole_in, quarter_in
        self.send, self.recv = send, recv
        self.rows = part.shape[2]

    def at(self, half, turn, shift):
        first, second = self.place.own(half)
        if isinstance(turn, int) and turn == 0:
            return wrap(first + shift), second
        return wrap(first + turn - 1), wrap(second + shift)

    def piece(self, half, block, kind):
        rows = self.rows // 2 if kind < 2 else self.rows // 4
        start = half * (self.rows // 2) + (self.rows // 4 if kind == 3 else 0)
        bx, by = self.place.block(half, *block)
        return bx, by, pl.ds(start, rows)

    def copy(self, half, turn, kind):
        ahead = (1, -1, 1, -1)[kind]
        shift = (1, -1, 2, 2)[kind]
        slot = (half * 5 + turn) * 2 + kind % 2
        landing = (self.whole_in if kind < 2 else self.quarter_in).at[slot]
        bx, by, rows = self.piece(half, self.at(half, turn, shift), kind)
        sem = (half * 5 + turn) * 4 + kind
        return pltpu.make_async_remote_copy(
            src_ref=self.part.at[bx, by, rows],
            dst_ref=landing,
            send_sem=self.send.at[sem],
            recv_sem=self.recv.at[sem],
            device_id=self.place.device(half, *self.place.line(half, turn, ahead)),
            device_id_type=MESH,
        )

    def begin(self, half, turn):
        for kind in (2, 3):
            self.copy(half, turn, kind).start()

    def middle(self, half, turn):
        for kind in (2, 3):
            self.copy(half, turn, kind).wait_recv()
            slot = (half * 5 + turn) * 2 + kind % 2
            shift = 1 if kind == 2 else -1
            bx, by, rows = self.piece(half, self.at(half, turn, shift), kind)
            self.part[bx, by, rows, :] += self.quarter_in[slot]
            self.copy(half, turn, kind - 2).start()

    def finish(self, half, turn):
        for kind in (0, 1):
            self.copy(half, turn, kind).wait_recv()
        slot = (half * 5 + turn) * 2
        bx, by, rows = self.piece(half, self.at(half, turn, 0), 0)
        self.part[bx, by, rows, :] += self.whole_in[slot] + self.whole_in[slot + 1]

    def drain(self):
        for half in (0, 1):
            for turn in range(5):
                for kind in range(4):
                    self.copy(half, turn, kind).wait_send()


class Ring:
    def __init__(self, w, near_in, whole_in, half_in, send, recv):
        group = lax.axis_index("wide")
        self.z, self.core = group // 2, lax.rem(group, 2)
        self.w, self.near_in, self.whole_in, self.half_in = w, near_in, whole_in, half_in
        self.send, self.recv = send, recv
        self.half_rows = w.shape[1] // 2

    def index(self, shift):
        return wrap(self.z + shift) * 2 + self.core

    def swap(self, turn, shift):
        to = wrap(self.z + shift)
        return pltpu.make_async_remote_copy(
            src_ref=self.w.at[to * 2 + 1 - self.core],
            dst_ref=self.near_in.at[to],
            send_sem=self.send.at[4 + turn],
            recv_sem=self.recv.at[4 + turn],
            device_id={"wide": self.z * 2 + 1 - self.core},
            device_id_type=MESH,
        )

    def take(self, turn, shift):
        self.swap(turn, shift).wait_recv()
        self.w[self.index(shift)] += self.near_in[wrap(self.z + shift)]

    def copy(self, kind):
        ahead = (1, -1, 1, -1)[kind]
        shift = (1, -1, 2, 2)[kind]
        source = self.w.at[self.index(shift)]
        landing = self.whole_in
        if kind >= 2:
            source = self.w.at[self.index(shift), pl.ds((kind - 2) * self.half_rows, self.half_rows)]
            landing = self.half_in
        return pltpu.make_async_remote_copy(
            src_ref=source,
            dst_ref=landing.at[kind % 2],
            send_sem=self.send.at[kind],
            recv_sem=self.recv.at[kind],
            device_id={"wide": self.index(ahead)},
            device_id_type=MESH,
        )

    def begin(self):
        self.take(0, 2)
        for kind in (2, 3):
            self.copy(kind).start()

    def middle(self):
        for kind in (2, 3):
            shift = 1 if kind == 2 else -1
            self.take(kind - 1, shift)
            self.copy(kind).wait_recv()
            rows = pl.ds((kind - 2) * self.half_rows, self.half_rows)
            self.w[self.index(shift), rows, :] += self.half_in[kind - 2]
            self.copy(kind - 2).start()
        self.take(3, 0)

    def finish(self):
        for kind in (0, 1):
            self.copy(kind).wait_recv()
        return self.w[self.index(0)] + self.whole_in[0] + self.whole_in[1]

    def drain(self):
        for kind in range(4):
            self.copy(kind).wait_send()
        for turn, shift in enumerate((2, 1, 3, 0)):
            self.swap(turn, shift).wait_send()


TURNS = (3, 2, 4, 1)


def shift_of(step):
    return 2 - step + 3 * (step // 2) - 2 * (step // 3)


def stream(count, loads, work):
    for copy in loads(0, 0):
        copy.start()

    def one(i, carry):
        slot = lax.rem(i, 2)

        @pl.when(i + 1 < count)
        def _():
            for copy in loads(i + 1, 1 - slot):
                copy.start()

        for copy in loads(i, slot):
            copy.wait()
        work(i, slot)
        return carry

    lax.fori_loop(0, count, one, 0)


def reduce_kernel(
    dq_ref,
    att_ref,
    inst_ref,
    dk_hbm,
    dv_hbm,
    hid_hbm,
    cot_hbm,
    nei_hbm,
    wq_hbm,
    wk_hbm,
    wv_hbm,
    gh_ref,
    came_ref,
    gq_ref,
    go_ref,
    gk_ref,
    gv_ref,
    gpart,
    dpart,
    ghalf,
    gquarter,
    dhalf,
    dquarter,
    tile,
    near_tile,
    dk_tile,
    dv_tile,
    wk,
    wv,
    going,
    mine,
    out_w,
    out_near,
    out_whole,
    out_half,
    in_w,
    in_near,
    in_whole,
    in_half,
    kv_w,
    kv_near,
    kv_whole,
    kv_half,
    g_send,
    g_recv,
    d_send,
    d_recv,
    out_send,
    out_recv,
    in_send,
    in_recv,
    kv_send,
    kv_recv,
    swap_send,
    swap_recv,
    load_sem,
    tile_sem,
    near_sem,
):
    place = Place()
    x, y = place.x, place.y
    width = dq_ref.shape[1]
    piece_rows = going.shape[2]
    groups, cap = going.shape[:2]
    rows, enc = dpart.shape[2:]
    weights = [
        pltpu.make_async_copy(wk_hbm, wk, load_sem.at[1]),
        pltpu.make_async_copy(wv_hbm, wv, load_sem.at[2]),
    ]
    for copy in weights:
        copy.start()
    greet(place)
    wide_sum = Reduce(place, gpart, ghalf, gquarter, g_send, g_recv)
    near_sum = Reduce(place, dpart, dhalf, dquarter, d_send, d_recv)
    out_ring = Ring(out_w, out_near, out_whole, out_half, out_send, out_recv)
    in_ring = Ring(in_w, in_near, in_whole, in_half, in_send, in_recv)
    kv_ring = Ring(kv_w, kv_near, kv_whole, kv_half, kv_send, kv_recv)

    def dot(a, b, ca, cb):
        return lax.dot_general(
            a, b, (((ca,), (cb,)), ((), ())), precision=MID, preferred_element_type=jnp.float32
        )

    def g_load(i, slot):
        bx = wrap(x + shift_of(i // 2))
        start = pl.multiple_of((bx * SIDE + 2 * lax.rem(i, 2)) * width, width)
        return [pltpu.make_async_copy(wq_hbm.at[pl.ds(start, 2 * width)], tile.at[slot], tile_sem.at[slot])]

    def g_work(i, slot):
        bx, by = wrap(x + shift_of(i // 2)), 2 * lax.rem(i, 2)
        both = dot(dq_ref[...], tile[slot], 1, 1)
        gpart[bx, by] = both[:, :width]
        gpart[bx, by + 1] = both[:, width:]

        @pl.when(lax.rem(i, 2) == 1)
        def _():
            wide_sum.begin(0, shift_of(i // 2) + 1)

        @pl.when(i == 1)
        def _():
            for turn in TURNS:
                wide_sum.begin(1, turn)

    stream(2 * SIDE, g_load, g_work)

    def weight_grad(source, right_ref, ring):
        def at(i):
            j = i // 2
            core = ring.core + (1 - j // SIDE) * (1 - 2 * ring.core)
            return wrap(ring.z + shift_of(lax.rem(j, SIDE))) * 2 + core, lax.rem(i, 2)

        def load(i, slot):
            g, u = at(i)
            m = 2 * g + u
            return [
                pltpu.make_async_copy(
                    source.at[m // SIDE, lax.rem(m, SIDE)], tile.at[slot], tile_sem.at[slot]
                )
            ]

        def work(i, slot):
            g, u = at(i)
            part = pl.ds(pl.multiple_of(u * width, width), width)
            ring.w[g, part, :] = dot(tile[slot], right_ref[...], 0, 0)

            @pl.when((u == 1) & (i < 2 * SIDE))
            def _():
                ring.swap(i // 2, shift_of(i // 2)).start()

        stream(4 * SIDE, load, work)

    weight_grad(cot_hbm, att_ref, out_ring)
    for turn in TURNS:
        for half in (0, 1):
            wide_sum.middle(half, turn)
    out_ring.begin()
    for copy in weights:
        copy.wait()
    kv_w[...] = jnp.zeros_like(kv_w)

    def d_load(i, slot):
        at = (i // 2, pl.ds(2 * lax.rem(i, 2), 2))
        return [
            pltpu.make_async_copy(source.at[at], buf.at[slot], near_sem.at[which * 2 + slot])
            for which, (source, buf) in enumerate(
                ((nei_hbm, near_tile), (dk_hbm, dk_tile), (dv_hbm, dv_tile))
            )
        ]

    def d_work(i, slot):
        bx, by = i // 2, 2 * lax.rem(i, 2)
        dk = dk_tile[slot].reshape(2 * rows, width)
        dv = dv_tile[slot].reshape(2 * rows, width)
        near = near_tile[slot].reshape(2 * rows, enc)
        dpart[bx, pl.ds(by, 2)] = (dot(dk, wk[...], 1, 1) + dot(dv, wv[...], 1, 1)).reshape(
            2, rows, enc
        )
        pair = dot(near, jnp.concatenate([dk, dv], axis=1), 0, 0)
        kv_w[...] += pair.reshape(kv_w.shape)

    stream(2 * SIDE, d_load, d_work)
    for turn in TURNS:
        for half in (0, 1):
            near_sum.begin(half, turn)
    for turn, shift in enumerate((2, 1, 3, 0)):
        kv_ring.swap(turn, shift).start()
    out_ring.middle()
    for half in (0, 1):
        wide_sum.finish(half, 3)
        wide_sum.begin(half, 0)
    for half in (0, 1):
        for turn in (2, 4, 1):
            wide_sum.finish(half, turn)
    weight_grad(hid_hbm, dq_ref, in_ring)
    for half in (0, 1):
        wide_sum.middle(half, 0)
    for turn in TURNS:
        for half in (0, 1):
            near_sum.middle(half, turn)
    kv_ring.begin()
    in_ring.begin()
    for half in (0, 1):
        near_sum.finish(half, 3)
        near_sum.begin(half, 0)
    for half in (0, 1):
        for turn in (2, 4):
            near_sum.finish(half, turn)
        near_sum.middle(half, 0)
    kv_ring.middle()
    in_ring.middle()
    go_ref[...] = out_ring.finish()
    for half in (0, 1):
        wide_sum.finish(half, 0)
    gh_ref[...] = gpart[x, y]
    for half in (0, 1):
        near_sum.finish(half, 1)
        near_sum.finish(half, 0)
    for i in range(groups * cap):
        mine[i] = dpart[x, y, pl.ds(i * piece_rows, piece_rows), :]
    for slot in range(groups * cap):
        going[slot // cap, slot % cap] = mine[inst_ref[slot]]
    swaps = exchange(going, came_ref, swap_send, swap_recv, load_sem.at[3])
    pair = kv_ring.finish()
    gk_ref[...] = pair[:, :width]
    gv_ref[...] = pair[:, width:]
    gq_ref[...] = in_ring.finish()
    for copy in swaps:
        copy.wait()
    for target in (wide_sum, near_sum, out_ring, in_ring, kv_ring):
        target.drain()


def vmem(n):
    return [pl.BlockSpec(memory_space=pltpu.VMEM)] * n


def hbm(n):
    return [pl.BlockSpec(memory_space=pl.ANY)] * n


def smem(n):
    return [pl.BlockSpec(memory_space=pltpu.SMEM)] * n


def f32(*shape):
    return jax.ShapeDtypeStruct(shape, jnp.float32)


def gather_call(hidden, cotangent, outgoing, slots, wq, wo, wk, wv):
    tokens, width = hidden.shape
    groups, cap, piece_rows, enc = outgoing.shape
    rows = slots.shape[0] * piece_rows
    dma = pltpu.SemaphoreType.DMA
    out_shape = [
        f32(SIDE, SIDE, tokens, width),
        f32(SIDE, SIDE, tokens, width),
        f32(SIDE, SIDE, rows, enc),
        f32(tokens, width),
        f32(tokens, width),
        f32(SIDE, SIDE, rows, width),
        f32(SIDE, SIDE, rows, width),
    ]
    scratch = [
        pltpu.VMEM((tokens, width), jnp.float32),
        pltpu.VMEM((tokens, width), jnp.float32),
        pltpu.VMEM((SIDE, SIDE, rows, width), jnp.float32),
        pltpu.VMEM((SIDE, SIDE, rows, width), jnp.float32),
        pltpu.VMEM((SIDE, SIDE, tokens, width), jnp.float32),
        pltpu.VMEM((SIDE, SIDE, tokens, width), jnp.float32),
        pltpu.VMEM((SIDE, SIDE, rows, enc), jnp.float32),
        pltpu.VMEM(wq.shape, jnp.float32),
        pltpu.VMEM(wo.shape, jnp.float32),
        pltpu.VMEM((enc, 2 * width), jnp.float32),
        pltpu.VMEM(outgoing.shape, jnp.float32),
    ]
    scratch += [dma((40,))] * 6 + [dma((groups,))] * 2 + [dma((8,)), dma((30,))]
    return pl.pallas_call(
        gather_kernel,
        out_shape=out_shape,
        in_specs=hbm(2) + vmem(1) + smem(1) + hbm(4),
        out_specs=hbm(3) + vmem(4),
        scratch_shapes=scratch,
        compiler_params=pltpu.CompilerParams(
            collective_id=0, has_side_effects=True, vmem_limit_bytes=VMEM_LIMIT
        ),
        cost_estimate=pl.CostEstimate(flops=24_000_000_000, bytes_accessed=60_000_000, transcendentals=0),
    )(hidden, cotangent, outgoing, slots, wq, wo, wk, wv)


def reduce_call(dq, att, inst_of, dk, dv, hid, cot, nei, wq, wk, wv, groups):
    tokens, width = dq.shape
    rows = dk.shape[2]
    enc = wk.shape[0]
    slots = inst_of.shape[0]
    cap = slots // groups
    piece_rows = rows // slots
    dma = pltpu.SemaphoreType.DMA
    going = (groups, cap, piece_rows, enc)
    out_rows, enc_rows = wq.shape[0] // groups, enc // groups

    def ring(rows, cols):
        return [
            pltpu.VMEM((n, r, cols), jnp.float32)
            for n, r in ((groups, rows), (groups // 2, rows), (2, rows), (2, rows // 2))
        ]

    scratch = [
        pltpu.VMEM((SIDE, SIDE, tokens, width), jnp.float32),
        pltpu.VMEM((SIDE, SIDE, rows, enc), jnp.float32),
        pltpu.VMEM((20, tokens // 2, width), jnp.float32),
        pltpu.VMEM((20, tokens // 4, width), jnp.float32),
        pltpu.VMEM((20, rows // 2, enc), jnp.float32),
        pltpu.VMEM((20, rows // 4, enc), jnp.float32),
        pltpu.VMEM((2, 2 * width, width), jnp.float32),
        pltpu.VMEM((2, 2, rows, enc), jnp.float32),
        pltpu.VMEM((2, 2, rows, width), jnp.float32),
        pltpu.VMEM((2, 2, rows, width), jnp.float32),
        pltpu.VMEM(wk.shape, jnp.float32),
        pltpu.VMEM(wv.shape, jnp.float32),
        pltpu.VMEM(going, jnp.float32),
        pltpu.VMEM((slots, piece_rows, enc), jnp.float32),
    ]
    scratch += ring(out_rows, width) + ring(out_rows, width) + ring(enc_rows, 2 * width)
    scratch += [dma((40,))] * 4 + [dma((8,))] * 6 + [dma((groups,))] * 2
    scratch += [dma((4,)), dma((2,)), dma((6,))]
    return pl.pallas_call(
        reduce_kernel,
        out_shape=[
            f32(tokens, width),
            f32(*going),
            f32(out_rows, width),
            f32(out_rows, width),
            f32(enc_rows, width),
            f32(enc_rows, width),
        ],
        in_specs=vmem(2) + smem(1) + hbm(8),
        out_specs=vmem(6),
        scratch_shapes=scratch,
        compiler_params=pltpu.CompilerParams(
            collective_id=1, has_side_effects=True, vmem_limit_bytes=REDUCE_LIMIT
        ),
        cost_estimate=pl.CostEstimate(flops=50_000_000_000, bytes_accessed=60_000_000, transcendentals=0),
    )(dq, att, inst_of, dk, dv, hid, cot, nei, wq, wk, wv)


def body(
    hidden_states, out_cotangent, enc_table, nbr_ids, owner_map, w_query, w_key, w_value, w_out
):
    groups = lax.axis_size("wide")
    group = lax.axis_index("wide")
    stored = enc_table.shape[0]
    table_size = owner_map.shape[0]
    tokens, width = hidden_states.shape
    inst = NEIGH * (tokens // SPAN)
    capacity = inst // groups
    match = nbr_ids[:, :, None] == jnp.arange(table_size, dtype=jnp.int32)[None, None, :]
    slots = jnp.sum(jnp.where(match, owner_map[None, None, :], 0), axis=-1)
    slots = slots.reshape(groups, inst)
    owners = slots // stored
    local_slot = slots - owners * stored
    earlier = jnp.arange(inst)[None, :] < jnp.arange(inst)[:, None]
    same = owners[:, :, None] == owners[:, None, :]
    rank = jnp.sum((same & earlier[None, :, :]).astype(jnp.int32), axis=-1)
    slot_range = jnp.arange(capacity, dtype=jnp.int32)
    pick = ((owners[:, None, :] == group) & (rank[:, None, :] == slot_range[None, :, None])).astype(
        jnp.float32
    )
    one_local = (
        local_slot[:, :, None] == jnp.arange(stored, dtype=jnp.int32)[None, None, :]
    ).astype(jnp.float32)
    place = jnp.einsum("bri,bis->brs", pick, one_local, precision=HIGH)
    outgoing = jnp.einsum("brs,sxe->brxe", place, enc_table, precision=HIGH)
    mine = lax.dynamic_index_in_dim(owners * capacity + rank, group, 0, keepdims=False)
    numbers = jnp.arange(inst, dtype=jnp.int32)
    inst_of = jnp.sum(jnp.where(mine[None, :] == numbers[:, None], numbers[None, :], 0), axis=1)

    hid, cot, nei, attended, d_query, d_keys, d_values = gather_call(
        hidden_states, out_cotangent, outgoing, mine, w_query, w_out, w_key, w_value
    )
    grad_hidden, arrived, grad_query, grad_out, grad_key, grad_value = reduce_call(
        d_query, attended, inst_of, d_keys, d_values, hid, cot, nei, w_query, w_key, w_value, groups
    )
    grad_table = jnp.einsum("brs,brxe->sxe", place, arrived, precision=HIGH)
    return (grad_hidden, grad_query, grad_key, grad_value, grad_out, grad_table)


def solution(mesh):
    placed = (
        P("wide", "narrow"),
        P("wide", "narrow"),
        P("wide", "narrow", None),
        P(),
        P(),
        P(None, "narrow"),
        P(None, "narrow"),
        P(None, "narrow"),
        P(None, "narrow"),
    )
    return jax.shard_map(
        body,
        mesh=mesh,
        in_specs=placed,
        out_specs=(
            P("wide", "narrow"),
            P("wide", "narrow"),
            P("wide", "narrow"),
            P("wide", "narrow"),
            P("wide", "narrow"),
            P("wide", "narrow", None),
        ),
        check_vma=False,
    )
```

```python
import functools

import jax
import jax.numpy as jnp
from jax import lax
from jax.experimental import pallas as pl
from jax.experimental.pallas import tpu as pltpu
from jax.sharding import PartitionSpec as P

HEAD_DIM = 128
SPAN = 64
NEIGH = 2
SIDE = 4
VMEM_LIMIT = 60 * 1024 * 1024
REDUCE_LIMIT = 63 * 1024 * 1024

HIGH = lax.Precision.HIGHEST
MID = lax.Precision.HIGH
MESH = pl.DeviceIdType.MESH


def wrap(value):
    return lax.rem(value + 2 * SIDE, SIDE)


class Place:
    def __init__(self):
        me = lax.axis_index("narrow")
        self.x = me // SIDE
        self.y = lax.rem(me, SIDE)

    def own(self, half):
        return (self.x, self.y) if half == 0 else (self.y, self.x)

    @staticmethod
    def block(half, first, second):
        return (first, second) if half == 0 else (second, first)

    def device(self, half, first, second):
        bx, by = self.block(half, first, second)
        return {"narrow": bx * SIDE + by}

    def line(self, half, turn, shift):
        first, second = self.own(half)
        if isinstance(turn, int) and turn == 0:
            return wrap(first + shift), second
        return first, wrap(second + shift)


def greet(place):
    groups = lax.axis_size("wide")
    group = lax.axis_index("wide")
    barrier = pltpu.get_barrier_semaphore()
    for half in (0, 1):
        for shift in (1, -1):
            pl.semaphore_signal(
                barrier,
                inc=1,
                device_id=place.device(half, *place.line(half, 0, shift)),
                device_id_type=MESH,
            )
    for step in range(1, groups):
        pl.semaphore_signal(
            barrier,
            inc=1,
            device_id={"wide": lax.rem(group + step, groups)},
            device_id_type=MESH,
        )
    pl.semaphore_wait(barrier, 4 + groups - 1)


def exchange(out_ref, in_ref, send, recv, local):
    groups = lax.axis_size("wide")
    group = lax.axis_index("wide")
    copies = []
    for step in range(1, groups):
        peer = lax.rem(group + step, groups)
        copy = pltpu.make_async_remote_copy(
            src_ref=out_ref.at[peer],
            dst_ref=in_ref.at[group],
            send_sem=send.at[step],
            recv_sem=recv.at[step],
            device_id={"wide": peer},
            device_id_type=MESH,
        )
        copy.start()
        copies.append(copy)
    mine = pltpu.make_async_copy(out_ref.at[group], in_ref.at[group], local)
    mine.start()
    copies.append(mine)
    return copies


class Gather:
    def __init__(self, place, buf, send, recv):
        self.place, self.buf, self.send, self.recv = place, buf, send, recv
        self.rows = buf.shape[2]

    def copy(self, half, turn, kind, block, dest):
        rows = self.rows // 2 if kind < 2 else self.rows // 4
        start = half * (self.rows // 2) + (self.rows // 4 if kind == 3 else 0)
        bx, by = self.place.block(half, *block)
        piece = self.buf.at[bx, by, pl.ds(start, rows)]
        slot = (half * 5 + turn) * 4 + kind
        return pltpu.make_async_remote_copy(
            src_ref=piece,
            dst_ref=piece,
            send_sem=self.send.at[slot],
            recv_sem=self.recv.at[slot],
            device_id=self.place.device(half, *dest),
            device_id_type=MESH,
        )

    def at(self, half, turn, shift):
        first, second = self.place.own(half)
        if isinstance(turn, int) and turn == 0:
            return wrap(first + shift), second
        return wrap(first + turn - 1), wrap(second + shift)

    def describe(self, half, turn, kind):
        shift = (0, 0, -1, 1)[kind]
        ahead = (1, -1, 1, -1)[kind]
        return self.copy(
            half, turn, kind, self.at(half, turn, shift), self.place.line(half, turn, ahead)
        )

    def arrival(self, half, turn, kind):
        shift = (-1, 1, 2, 2)[kind]
        ahead = (1, -1, 1, -1)[kind]
        return self.copy(
            half, turn, kind, self.at(half, turn, shift), self.place.line(half, turn, ahead)
        )

    def begin(self, half, turn):
        self.describe(half, turn, 0).start()
        self.describe(half, turn, 1).start()

    def forward(self, half, turn):
        for kind in (0, 1):
            self.arrival(half, turn, kind).wait_recv()
            self.describe(half, turn, kind + 2).start()

    def finish(self, half, turn):
        for kind in (2, 3):
            self.arrival(half, turn, kind).wait_recv()

    def drain(self):
        for half in (0, 1):
            for turn in range(5):
                for kind in range(4):
                    self.describe(half, turn, kind).wait_send()


def attend(q_ref, da_ref, keys_ref, values_ref, att_ref, dq_ref, dk_ref, dv_ref):
    scale = HEAD_DIM ** (-0.5)
    heads = q_ref.shape[1] // HEAD_DIM
    spans = q_ref.shape[0] // SPAN
    few = keys_ref.shape[2] // spans
    near = SIDE * SIDE * few

    def dot(a, b, ca, cb, precision=MID):
        return lax.dot_general(
            a, b, (((ca,), (cb,)), ((), ())), precision=precision,
            preferred_element_type=jnp.float32,
        )

    def span(c, carry):
        rows = pl.ds(pl.multiple_of(c * SPAN, SPAN), SPAN)
        pieces = pl.ds(pl.multiple_of(c * few, few), few)
        for head in range(heads):
            cols = pl.ds(head * HEAD_DIM, HEAD_DIM)
            q = q_ref[rows, cols]
            da = da_ref[rows, cols]
            k = keys_ref[:, :, pieces, cols].reshape(near, HEAD_DIM)
            v = values_ref[:, :, pieces, cols].reshape(near, HEAD_DIM)
            scores = dot(q, k, 1, 1, HIGH) * scale
            dp = dot(da, v, 1, 1)
            top = jnp.max(scores, axis=-1, keepdims=True)
            e = jnp.exp(scores - top)
            probs = e / jnp.sum(e, axis=-1, keepdims=True)
            ds = probs * (dp - jnp.sum(dp * probs, axis=-1, keepdims=True)) * scale
            att_ref[rows, cols] = dot(probs, v, 1, 0)
            dq_ref[rows, cols] = dot(ds, k, 1, 0)
            shape = (SIDE, SIDE, few, HEAD_DIM)
            dk_ref[:, :, pieces, cols] = dot(ds, q, 0, 0).reshape(shape)
            dv_ref[:, :, pieces, cols] = dot(probs, da, 0, 0).reshape(shape)
        return carry

    lax.fori_loop(0, spans, span, 0)


def gather_kernel(
    hid_ref,
    cot_ref,
    table_ref,
    pick_ref,
    slot_ref,
    wq_ref,
    wo_ref,
    wk_ref,
    wv_ref,
    hid_out,
    cot_out,
    nei_out,
    att_ref,
    dq_ref,
    dk_ref,
    dv_ref,
    q_ref,
    da_ref,
    keys_ref,
    values_ref,
    hid,
    cot,
    nei,
    wq,
    wo,
    wkv,
    going,
    came,
    hid_send,
    hid_recv,
    cot_send,
    cot_recv,
    nei_send,
    nei_recv,
    swap_send,
    swap_recv,
    load_sem,
    store_sem,
):
    place = Place()
    x, y = place.x, place.y
    width = q_ref.shape[1]
    tokens = q_ref.shape[0]
    groups, cap, piece_rows, _ = came.shape
    inst = nei.shape[2] // piece_rows
    own = [
        pltpu.make_async_copy(hid_ref, hid.at[x, y], load_sem.at[0]),
        pltpu.make_async_copy(cot_ref, cot.at[x, y], load_sem.at[1]),
    ]
    weights = [
        pltpu.make_async_copy(wq_ref, wq, load_sem.at[2]),
        pltpu.make_async_copy(wo_ref, wo, load_sem.at[3]),
        pltpu.make_async_copy(wk_ref, wkv.at[:, pl.ds(0, width)], load_sem.at[4]),
        pltpu.make_async_copy(wv_ref, wkv.at[:, pl.ds(width, width)], load_sem.at[5]),
    ]
    for copy in own:
        copy.start()
    greet(place)
    for copy in own:
        copy.wait()
    gathers = [
        Gather(place, hid, hid_send, hid_recv),
        Gather(place, cot, cot_send, cot_recv),
        Gather(place, nei, nei_send, nei_recv),
    ]
    for turn in (0, 1):
        for gather in gathers[:2]:
            for half in (0, 1):
                gather.begin(half, turn)
    for i in range(groups * cap):
        going[i // cap, i % cap] = table_ref[pick_ref[i]]
    swaps = exchange(going, came, swap_send, swap_recv, load_sem.at[6])
    for copy in weights:
        copy.start()
    for copy in swaps:
        copy.wait()
    for i in range(inst):
        slot = slot_ref[i]
        nei[x, y, pl.ds(i * piece_rows, piece_rows), :] = came[slot // cap, lax.rem(slot, cap)]
    for turn in (0, 1):
        for half in (0, 1):
            gathers[2].begin(half, turn)
    for gather in gathers:
        for half in (0, 1):
            gather.forward(half, 0)
        for half in (0, 1):
            gather.begin(half, 2)
            gather.begin(half, 4)
    for gather in gathers:
        for half in (0, 1):
            gather.finish(half, 0)
            gather.begin(half, 3)
    for copy in weights:
        copy.wait()
    q_ref[...] = jnp.zeros_like(q_ref)
    da_ref[...] = jnp.zeros_like(da_ref)

    def turn_of(step):
        return step + (step // 2) * (1 - 2 * lax.rem(step, 2)) + 1

    def project(half, first):
        rows = pl.ds(half * (tokens // 2), tokens // 2)

        def column(second, carry):
            bx, by = place.block(half, first, second)
            part = pl.ds(pl.multiple_of((bx * SIDE + by) * width, width), width)
            q_ref[rows, :] += jnp.dot(
                hid[bx, by, rows, :], wq[part, :], precision=HIGH,
                preferred_element_type=jnp.float32,
            )
            da_ref[rows, :] += jnp.dot(
                cot[bx, by, rows, :], wo[part, :], precision=MID,
                preferred_element_type=jnp.float32,
            )
            return carry

        lax.fori_loop(0, SIDE, column, 0)
        few = nei.shape[2] // 2
        rows = pl.ds(half * few, few)
        if half == 0:
            blocks = nei[first, :, rows, :]
        else:
            blocks = nei[:, first, rows, :]
        both = jnp.dot(
            blocks.reshape(SIDE * few, nei.shape[3]), wkv[...], precision=HIGH,
            preferred_element_type=jnp.float32,
        ).reshape(SIDE, few, 2 * width)
        if half == 0:
            keys_ref[first, :, rows, :] = both[:, :, :width]
            values_ref[first, :, rows, :] = both[:, :, width:]
        else:
            keys_ref[:, first, rows, :] = both[:, :, :width]
            values_ref[:, first, rows, :] = both[:, :, width:]

    def keep(half, turn, first):
        copies = []
        for which, (buf, out) in enumerate(((hid, hid_out), (cot, cot_out), (nei, nei_out))):
            rows = pl.ds(half * (buf.shape[2] // 2), buf.shape[2] // 2)
            at = (first, slice(None), rows) if half == 0 else (slice(None), first, rows)
            copies.append(
                pltpu.make_async_copy(
                    buf.at[at], out.at[at], store_sem.at[(which * 2 + half) * 5 + turn]
                )
            )
        return copies

    def pass_on(turn):
        for gather in gathers:
            for half in (0, 1):
                gather.forward(half, turn)

    pass_on(turn_of(0))

    def main(step, carry):
        @pl.when(step < SIDE - 1)
        def _():
            pass_on(turn_of(step + 1))

        turn = turn_of(step)
        for half in (0, 1):
            for gather in gathers:
                gather.finish(half, turn)
            first = wrap(place.own(half)[0] + turn - 1)
            for copy in keep(half, turn, first):
                copy.start()
            project(half, first)
        return carry

    lax.fori_loop(0, SIDE, main, 0)
    attend(q_ref, da_ref, keys_ref, values_ref, att_ref, dq_ref, dk_ref, dv_ref)
    for gather in gathers:
        gather.drain()

    def stored(turn, carry):
        for half in (0, 1):
            first = wrap(place.own(half)[0] + turn - 1)
            for copy in keep(half, turn, first):
                copy.wait()
        return carry

    lax.fori_loop(1, SIDE + 1, stored, 0)


class Reduce:
    def __init__(self, place, part, whole_in, quarter_in, send, recv):
        self.place, self.part = place, part
        self.whole_in, self.quarter_in = whole_in, quarter_in
        self.send, self.recv = send, recv
        self.rows = part.shape[2]

    def at(self, half, turn, shift):
        first, second = self.place.own(half)
        if isinstance(turn, int) and turn == 0:
            return wrap(first + shift), second
        return wrap(first + turn - 1), wrap(second + shift)

    def piece(self, half, block, kind):
        rows = self.rows // 2 if kind < 2 else self.rows // 4
        start = half * (self.rows // 2) + (self.rows // 4 if kind == 3 else 0)
        bx, by = self.place.block(half, *block)
        return bx, by, pl.ds(start, rows)

    def copy(self, half, turn, kind):
        ahead = (1, -1, 1, -1)[kind]
        shift = (1, -1, 2, 2)[kind]
        slot = (half * 5 + turn) * 2 + kind % 2
        landing = (self.whole_in if kind < 2 else self.quarter_in).at[slot]
        bx, by, rows = self.piece(half, self.at(half, turn, shift), kind)
        sem = (half * 5 + turn) * 4 + kind
        return pltpu.make_async_remote_copy(
            src_ref=self.part.at[bx, by, rows],
            dst_ref=landing,
            send_sem=self.send.at[sem],
            recv_sem=self.recv.at[sem],
            device_id=self.place.device(half, *self.place.line(half, turn, ahead)),
            device_id_type=MESH,
        )

    def begin(self, half, turn):
        for kind in (2, 3):
            self.copy(half, turn, kind).start()

    def middle(self, half, turn):
        for kind in (2, 3):
            self.copy(half, turn, kind).wait_recv()
            slot = (half * 5 + turn) * 2 + kind % 2
            shift = 1 if kind == 2 else -1
            bx, by, rows = self.piece(half, self.at(half, turn, shift), kind)
            self.part[bx, by, rows, :] += self.quarter_in[slot]
            self.copy(half, turn, kind - 2).start()

    def finish(self, half, turn):
        for kind in (0, 1):
            self.copy(half, turn, kind).wait_recv()
        slot = (half * 5 + turn) * 2
        bx, by, rows = self.piece(half, self.at(half, turn, 0), 0)
        self.part[bx, by, rows, :] += self.whole_in[slot] + self.whole_in[slot + 1]

    def drain(self):
        for half in (0, 1):
            for turn in range(5):
                for kind in range(4):
                    self.copy(half, turn, kind).wait_send()


class Ring:
    def __init__(self, w, near_in, whole_in, half_in, send, recv):
        group = lax.axis_index("wide")
        self.z, self.core = group // 2, lax.rem(group, 2)
        self.w, self.near_in, self.whole_in, self.half_in = w, near_in, whole_in, half_in
        self.send, self.recv = send, recv
        self.half_rows = w.shape[1] // 2

    def index(self, shift):
        return wrap(self.z + shift) * 2 + self.core

    def swap(self, turn, shift):
        to = wrap(self.z + shift)
        return pltpu.make_async_remote_copy(
            src_ref=self.w.at[to * 2 + 1 - self.core],
            dst_ref=self.near_in.at[to],
            send_sem=self.send.at[4 + turn],
            recv_sem=self.recv.at[4 + turn],
            device_id={"wide": self.z * 2 + 1 - self.core},
            device_id_type=MESH,
        )

    def take(self, turn, shift):
        self.swap(turn, shift).wait_recv()
        self.w[self.index(shift)] += self.near_in[wrap(self.z + shift)]

    def copy(self, kind):
        ahead = (1, -1, 1, -1)[kind]
        shift = (1, -1, 2, 2)[kind]
        source = self.w.at[self.index(shift)]
        landing = self.whole_in
        if kind >= 2:
            source = self.w.at[self.index(shift), pl.ds((kind - 2) * self.half_rows, self.half_rows)]
            landing = self.half_in
        return pltpu.make_async_remote_copy(
            src_ref=source,
            dst_ref=landing.at[kind % 2],
            send_sem=self.send.at[kind],
            recv_sem=self.recv.at[kind],
            device_id={"wide": self.index(ahead)},
            device_id_type=MESH,
        )

    def begin(self):
        self.take(0, 2)
        for kind in (2, 3):
            self.copy(kind).start()

    def middle(self):
        for kind in (2, 3):
            shift = 1 if kind == 2 else -1
            self.take(kind - 1, shift)
            self.copy(kind).wait_recv()
            rows = pl.ds((kind - 2) * self.half_rows, self.half_rows)
            self.w[self.index(shift), rows, :] += self.half_in[kind - 2]
            self.copy(kind - 2).start()
        self.take(3, 0)

    def finish(self):
        for kind in (0, 1):
            self.copy(kind).wait_recv()
        return self.w[self.index(0)] + self.whole_in[0] + self.whole_in[1]

    def drain(self):
        for kind in range(4):
            self.copy(kind).wait_send()
        for turn, shift in enumerate((2, 1, 3, 0)):
            self.swap(turn, shift).wait_send()


TURNS = (3, 2, 4, 1)


def shift_of(step):
    return 2 - step + 3 * (step // 2) - 2 * (step // 3)


def stream(count, loads, work):
    for copy in loads(0, 0):
        copy.start()

    def one(i, carry):
        slot = lax.rem(i, 2)

        @pl.when(i + 1 < count)
        def _():
            for copy in loads(i + 1, 1 - slot):
                copy.start()

        for copy in loads(i, slot):
            copy.wait()
        work(i, slot)
        return carry

    lax.fori_loop(0, count, one, 0)


def reduce_kernel(
    dq_ref,
    att_ref,
    inst_ref,
    dk_hbm,
    dv_hbm,
    hid_hbm,
    cot_hbm,
    nei_hbm,
    wq_hbm,
    wk_hbm,
    wv_hbm,
    gh_ref,
    came_ref,
    gq_ref,
    go_ref,
    gk_ref,
    gv_ref,
    gpart,
    dpart,
    ghalf,
    gquarter,
    dhalf,
    dquarter,
    tile,
    near_tile,
    dk_tile,
    dv_tile,
    wk,
    wv,
    going,
    mine,
    out_w,
    out_near,
    out_whole,
    out_half,
    in_w,
    in_near,
    in_whole,
    in_half,
    kv_w,
    kv_near,
    kv_whole,
    kv_half,
    g_send,
    g_recv,
    d_send,
    d_recv,
    out_send,
    out_recv,
    in_send,
    in_recv,
    kv_send,
    kv_recv,
    swap_send,
    swap_recv,
    load_sem,
    tile_sem,
    near_sem,
):
    place = Place()
    x, y = place.x, place.y
    width = dq_ref.shape[1]
    piece_rows = going.shape[2]
    groups, cap = going.shape[:2]
    rows, enc = dpart.shape[2:]
    weights = [
        pltpu.make_async_copy(wk_hbm, wk, load_sem.at[1]),
        pltpu.make_async_copy(wv_hbm, wv, load_sem.at[2]),
    ]
    for copy in weights:
        copy.start()
    greet(place)
    wide_sum = Reduce(place, gpart, ghalf, gquarter, g_send, g_recv)
    near_sum = Reduce(place, dpart, dhalf, dquarter, d_send, d_recv)
    out_ring = Ring(out_w, out_near, out_whole, out_half, out_send, out_recv)
    in_ring = Ring(in_w, in_near, in_whole, in_half, in_send, in_recv)
    kv_ring = Ring(kv_w, kv_near, kv_whole, kv_half, kv_send, kv_recv)

    def dot(a, b, ca, cb):
        return lax.dot_general(
            a, b, (((ca,), (cb,)), ((), ())), precision=MID, preferred_element_type=jnp.float32
        )

    def g_load(i, slot):
        bx = wrap(x + shift_of(i // 2))
        start = pl.multiple_of((bx * SIDE + 2 * lax.rem(i, 2)) * width, width)
        return [pltpu.make_async_copy(wq_hbm.at[pl.ds(start, 2 * width)], tile.at[slot], tile_sem.at[slot])]

    def g_work(i, slot):
        bx, by = wrap(x + shift_of(i // 2)), 2 * lax.rem(i, 2)
        both = dot(dq_ref[...], tile[slot], 1, 1)
        gpart[bx, by] = both[:, :width]
        gpart[bx, by + 1] = both[:, width:]

        @pl.when(lax.rem(i, 2) == 1)
        def _():
            wide_sum.begin(0, shift_of(i // 2) + 1)

        @pl.when(i == 1)
        def _():
            for turn in TURNS:
                wide_sum.begin(1, turn)

    stream(2 * SIDE, g_load, g_work)

    def weight_grad(source, right_ref, ring, other):
        core = 1 - ring.core if other else ring.core

        def at(i):
            return wrap(ring.z + shift_of(i // 2)) * 2 + core, lax.rem(i, 2)

        def load(i, slot):
            g, u = at(i)
            m = 2 * g + u
            return [
                pltpu.make_async_copy(
                    source.at[m // SIDE, lax.rem(m, SIDE)], tile.at[slot], tile_sem.at[slot]
                )
            ]

        def work(i, slot):
            g, u = at(i)
            part = pl.ds(pl.multiple_of(u * width, width), width)
            ring.w[g, part, :] = dot(tile[slot], right_ref[...], 0, 0)
            if other:

                @pl.when(u == 1)
                def _():
                    ring.swap(i // 2, shift_of(i // 2)).start()

        stream(2 * SIDE, load, work)

    def near_load(sources):
        def load(i, slot):
            at = (i // 2, pl.ds(2 * lax.rem(i, 2), 2))
            return [
                pltpu.make_async_copy(source.at[at], buf.at[slot], near_sem.at[2 * which + slot])
                for which, (source, buf) in enumerate(sources)
            ]

        return load

    def d_work(i, slot):
        bx, by = i // 2, 2 * lax.rem(i, 2)
        dk = dk_tile[slot].reshape(2 * rows, width)
        dv = dv_tile[slot].reshape(2 * rows, width)
        dpart[bx, pl.ds(by, 2)] = (dot(dk, wk[...], 1, 1) + dot(dv, wv[...], 1, 1)).reshape(
            2, rows, enc
        )

    def neighbour_grad():
        for copy in weights:
            copy.wait()
        stream(2 * SIDE, near_load(((dk_hbm, dk_tile), (dv_hbm, dv_tile))), d_work)
        for turn in TURNS:
            for half in (0, 1):
                near_sum.begin(half, turn)

    def kv_work(i, slot):
        dk = dk_tile[slot].reshape(2 * rows, width)
        dv = dv_tile[slot].reshape(2 * rows, width)
        near = near_tile[slot].reshape(2 * rows, enc)
        pair = dot(near, jnp.concatenate([dk, dv], axis=1), 0, 0)
        kv_w[...] += pair.reshape(kv_w.shape)

    def kv_grad():
        kv_w[...] = jnp.zeros_like(kv_w)
        stream(
            2 * SIDE, near_load(((dk_hbm, dk_tile), (dv_hbm, dv_tile), (nei_hbm, near_tile))), kv_work
        )
        for turn, shift in enumerate((2, 1, 3, 0)):
            kv_ring.swap(turn, shift).start()

    def middle(target, turn):
        for half in (0, 1):
            target.middle(half, turn)

    def finish(target, turn):
        for half in (0, 1):
            target.finish(half, turn)
        if turn == 3:
            for half in (0, 1):
                target.begin(half, 0)

    middle(wide_sum, 3)
    weight_grad(hid_hbm, dq_ref, in_ring, True)
    middle(wide_sum, 2)
    neighbour_grad()
    weight_grad(hid_hbm, dq_ref, in_ring, False)
    middle(wide_sum, 4)
    in_ring.begin()
    weight_grad(cot_hbm, att_ref, out_ring, True)
    middle(near_sum, 2)
    weight_grad(cot_hbm, att_ref, out_ring, False)
    middle(near_sum, 1)
    middle(wide_sum, 1)
    in_ring.middle()
    out_ring.begin()
    middle(near_sum, 3)
    kv_grad()
    middle(near_sum, 4)
    finish(wide_sum, 4)
    kv_ring.begin()
    finish(near_sum, 2)
    out_ring.middle()
    finish(near_sum, 3)
    gq_ref[...] = in_ring.finish()
    finish(wide_sum, 3)
    finish(near_sum, 4)
    finish(wide_sum, 2)
    middle(near_sum, 0)
    kv_ring.middle()
    finish(wide_sum, 1)
    middle(wide_sum, 0)
    finish(near_sum, 1)
    go_ref[...] = out_ring.finish()
    finish(near_sum, 0)
    for i in range(groups * cap):
        mine[i] = dpart[x, y, pl.ds(i * piece_rows, piece_rows), :]
    for slot in range(groups * cap):
        going[slot // cap, slot % cap] = mine[inst_ref[slot]]
    swaps = exchange(going, came_ref, swap_send, swap_recv, load_sem.at[3])
    finish(wide_sum, 0)
    gh_ref[...] = gpart[x, y]
    pair = kv_ring.finish()
    gk_ref[...] = pair[:, :width]
    gv_ref[...] = pair[:, width:]
    for copy in swaps:
        copy.wait()
    for target in (wide_sum, near_sum, out_ring, in_ring, kv_ring):
        target.drain()


def result_kernel(slot_ref, came_ref, *refs):
    sources, table_ref, results = refs[:5], refs[5], refs[6:]
    for source, result in zip(sources, results):
        result[...] = source[...]
    table_ref[...] = jnp.zeros_like(table_ref)
    cap = came_ref.shape[1]
    for i in range(came_ref.shape[0] * cap):
        slot = slot_ref[i]
        table_ref[slot] += came_ref[i // cap, i % cap]


def vmem(n):
    return [pl.BlockSpec(memory_space=pltpu.VMEM)] * n


def hbm(n):
    return [pl.BlockSpec(memory_space=pl.ANY)] * n


def smem(n):
    return [pl.BlockSpec(memory_space=pltpu.SMEM)] * n


def f32(*shape):
    return jax.ShapeDtypeStruct(shape, jnp.float32)


def gather_call(hidden, cotangent, table, picks, slots, wq, wo, wk, wv, groups):
    tokens, width = hidden.shape
    _, piece_rows, enc = table.shape
    going = (groups, slots.shape[0] // groups, piece_rows, enc)
    rows = slots.shape[0] * piece_rows
    dma = pltpu.SemaphoreType.DMA
    out_shape = [
        f32(SIDE, SIDE, tokens, width),
        f32(SIDE, SIDE, tokens, width),
        f32(SIDE, SIDE, rows, enc),
        f32(tokens, width),
        f32(tokens, width),
        f32(SIDE, SIDE, rows, width),
        f32(SIDE, SIDE, rows, width),
    ]
    scratch = [
        pltpu.VMEM((tokens, width), jnp.float32),
        pltpu.VMEM((tokens, width), jnp.float32),
        pltpu.VMEM((SIDE, SIDE, rows, width), jnp.float32),
        pltpu.VMEM((SIDE, SIDE, rows, width), jnp.float32),
        pltpu.VMEM((SIDE, SIDE, tokens, width), jnp.float32),
        pltpu.VMEM((SIDE, SIDE, tokens, width), jnp.float32),
        pltpu.VMEM((SIDE, SIDE, rows, enc), jnp.float32),
        pltpu.VMEM(wq.shape, jnp.float32),
        pltpu.VMEM(wo.shape, jnp.float32),
        pltpu.VMEM((enc, 2 * width), jnp.float32),
        pltpu.VMEM(going, jnp.float32),
        pltpu.VMEM(going, jnp.float32),
    ]
    scratch += [dma((40,))] * 6 + [dma((groups,))] * 2 + [dma((8,)), dma((30,))]
    return pl.pallas_call(
        gather_kernel,
        out_shape=out_shape,
        in_specs=hbm(2) + vmem(1) + smem(2) + hbm(4),
        out_specs=hbm(3) + vmem(4),
        scratch_shapes=scratch,
        compiler_params=pltpu.CompilerParams(
            collective_id=0, has_side_effects=True, vmem_limit_bytes=VMEM_LIMIT
        ),
        cost_estimate=pl.CostEstimate(flops=24_000_000_000, bytes_accessed=60_000_000, transcendentals=0),
    )(hidden, cotangent, table, picks, slots, wq, wo, wk, wv)


def reduce_call(dq, att, inst_of, dk, dv, hid, cot, nei, wq, wk, wv, groups):
    tokens, width = dq.shape
    rows = dk.shape[2]
    enc = wk.shape[0]
    slots = inst_of.shape[0]
    cap = slots // groups
    piece_rows = rows // slots
    dma = pltpu.SemaphoreType.DMA
    going = (groups, cap, piece_rows, enc)
    out_rows, enc_rows = wq.shape[0] // groups, enc // groups

    def ring(rows, cols):
        return [
            pltpu.VMEM((n, r, cols), jnp.float32)
            for n, r in ((groups, rows), (groups // 2, rows), (2, rows), (2, rows // 2))
        ]

    scratch = [
        pltpu.VMEM((SIDE, SIDE, tokens, width), jnp.float32),
        pltpu.VMEM((SIDE, SIDE, rows, enc), jnp.float32),
        pltpu.VMEM((20, tokens // 2, width), jnp.float32),
        pltpu.VMEM((20, tokens // 4, width), jnp.float32),
        pltpu.VMEM((20, rows // 2, enc), jnp.float32),
        pltpu.VMEM((20, rows // 4, enc), jnp.float32),
        pltpu.VMEM((2, 2 * width, width), jnp.float32),
        pltpu.VMEM((2, 2, rows, enc), jnp.float32),
        pltpu.VMEM((2, 2, rows, width), jnp.float32),
        pltpu.VMEM((2, 2, rows, width), jnp.float32),
        pltpu.VMEM(wk.shape, jnp.float32),
        pltpu.VMEM(wv.shape, jnp.float32),
        pltpu.VMEM(going, jnp.float32),
        pltpu.VMEM((slots, piece_rows, enc), jnp.float32),
    ]
    scratch += ring(out_rows, width) + ring(out_rows, width) + ring(enc_rows, 2 * width)
    scratch += [dma((40,))] * 4 + [dma((8,))] * 6 + [dma((groups,))] * 2
    scratch += [dma((4,)), dma((2,)), dma((6,))]
    return pl.pallas_call(
        reduce_kernel,
        out_shape=[
            f32(tokens, width),
            f32(*going),
            f32(out_rows, width),
            f32(out_rows, width),
            f32(enc_rows, width),
            f32(enc_rows, width),
        ],
        in_specs=vmem(2) + smem(1) + hbm(8),
        out_specs=vmem(6),
        scratch_shapes=scratch,
        compiler_params=pltpu.CompilerParams(
            collective_id=1, has_side_effects=True, vmem_limit_bytes=REDUCE_LIMIT
        ),
        cost_estimate=pl.CostEstimate(flops=50_000_000_000, bytes_accessed=60_000_000, transcendentals=0),
    )(dq, att, inst_of, dk, dv, hid, cot, nei, wq, wk, wv)


def body(
    hidden_states, out_cotangent, enc_table, nbr_ids, owner_map, w_query, w_key, w_value, w_out
):
    groups = lax.axis_size("wide")
    group = lax.axis_index("wide")
    stored = enc_table.shape[0]
    table_size = owner_map.shape[0]
    tokens, width = hidden_states.shape
    inst = NEIGH * (tokens // SPAN)
    capacity = inst // groups
    match = nbr_ids[:, :, None] == jnp.arange(table_size, dtype=jnp.int32)[None, None, :]
    slots = jnp.sum(jnp.where(match, owner_map[None, None, :], 0), axis=-1)
    slots = slots.reshape(groups, inst)
    owners = slots // stored
    local_slot = slots - owners * stored
    earlier = jnp.arange(inst)[None, :] < jnp.arange(inst)[:, None]
    same = owners[:, :, None] == owners[:, None, :]
    rank = jnp.sum((same & earlier[None, :, :]).astype(jnp.int32), axis=-1)
    slot_range = jnp.arange(capacity, dtype=jnp.int32)
    pick = (owners[:, None, :] == group) & (rank[:, None, :] == slot_range[None, :, None])
    picks = jnp.sum(jnp.where(pick, local_slot[:, None, :], 0), axis=-1).reshape(-1)
    mine = lax.dynamic_index_in_dim(owners * capacity + rank, group, 0, keepdims=False)
    numbers = jnp.arange(inst, dtype=jnp.int32)
    inst_of = jnp.sum(jnp.where(mine[None, :] == numbers[:, None], numbers[None, :], 0), axis=1)

    hid, cot, nei, attended, d_query, d_keys, d_values = gather_call(
        hidden_states, out_cotangent, enc_table, picks, mine, w_query, w_out, w_key, w_value, groups
    )
    grad_hidden, arrived, grad_query, grad_out, grad_key, grad_value = reduce_call(
        d_query, attended, inst_of, d_keys, d_values, hid, cot, nei, w_query, w_key, w_value, groups
    )
    sums = (grad_hidden, grad_query, grad_key, grad_value, grad_out)
    grad_table, *sums = pl.pallas_call(
        result_kernel,
        out_shape=[f32(*enc_table.shape)] + [f32(*t.shape) for t in sums],
        in_specs=smem(1) + vmem(6),
        out_specs=vmem(6),
    )(picks, arrived, *sums)
    return (*sums, grad_table)


def solution(mesh):
    placed = (
        P("wide", "narrow"),
        P("wide", "narrow"),
        P("wide", "narrow", None),
        P(),
        P(),
        P(None, "narrow"),
        P(None, "narrow"),
        P(None, "narrow"),
        P(None, "narrow"),
    )
    return jax.shard_map(
        body,
        mesh=mesh,
        in_specs=placed,
        out_specs=(
            P("wide", "narrow"),
            P("wide", "narrow"),
            P("wide", "narrow"),
            P("wide", "narrow"),
            P("wide", "narrow"),
            P("wide", "narrow", None),
        ),
        check_vma=False,
    )
```

```python
import functools

import jax
import jax.numpy as jnp
from jax import lax
from jax.experimental import pallas as pl
from jax.experimental.pallas import tpu as pltpu
from jax.sharding import PartitionSpec as P

HEAD_DIM = 128
SPAN = 64
NEIGH = 2
SIDE = 4
VMEM_LIMIT = 60 * 1024 * 1024
REDUCE_LIMIT = 63 * 1024 * 1024

HIGH = lax.Precision.HIGHEST
MID = lax.Precision.HIGH
MESH = pl.DeviceIdType.MESH


def wrap(value):
    return lax.rem(value + 2 * SIDE, SIDE)


class Place:
    def __init__(self):
        me = lax.axis_index("narrow")
        self.x = me // SIDE
        self.y = lax.rem(me, SIDE)
        self.set = self.y // 2
        self.member = lax.rem(self.y, 2)

    def at(self, dx, dy):
        return {"narrow": wrap(self.x + dx) * SIDE + wrap(self.y + dy)}

    def mate(self):
        return {"narrow": self.x * SIDE + self.y + 1 - 2 * self.member}

    def partner(self):
        return {"narrow": self.x * SIDE + SIDE - 1 - self.y}

    def own(self, half):
        return (self.x, self.y) if half == 0 else (self.y, self.x)

    @staticmethod
    def block(half, first, second):
        return (first, second) if half == 0 else (second, first)

    def device(self, half, first, second):
        bx, by = self.block(half, first, second)
        return {"narrow": bx * SIDE + by}

    def line(self, half, turn, shift):
        first, second = self.own(half)
        if isinstance(turn, int) and turn == 0:
            return wrap(first + shift), second
        return first, wrap(second + shift)


class SetGather:
    def __init__(self, place, buf, send, recv):
        self.place, self.buf, self.send, self.recv = place, buf, send, recv
        self.rows = buf.shape[2] // 2

    def copy(self, slot, bx, member, start, rows, device):
        piece = self.buf.at[bx, member, pl.ds(start, rows)]
        return pltpu.make_async_remote_copy(
            src_ref=piece,
            dst_ref=piece,
            send_sem=self.send.at[slot],
            recv_sem=self.recv.at[slot],
            device_id=device,
            device_id_type=MESH,
        )

    def ring(self, which, kind, arriving=False):
        place = self.place
        member = place.member if which < 2 else 1 - place.member
        ahead = (1, -1, 1, -1)[kind]
        shift = (0, 0, -1, 1)[kind] - (ahead if arriving else 0)
        start = self.rows * (which > 0) + (self.rows // 2 if kind == 3 else 0)
        rows = self.rows if kind < 2 else self.rows // 2
        return self.copy(
            which * 4 + kind, wrap(place.x + shift), member, start, rows, place.at(ahead, 0)
        )

    def across(self, turn, arriving=False):
        place = self.place
        member = 1 - place.member if arriving else place.member
        bx = wrap(place.x + turn)
        start = self.rows if turn == 4 else 0
        return self.copy(12 + turn, bx, member, start, self.rows, place.mate())

    def begin(self, which):
        for kind in (0, 1):
            self.ring(which, kind).start()

    def forward(self, which):
        for kind in (0, 1):
            self.ring(which, kind, True).wait_recv()
            self.ring(which, kind + 2).start()

    def finish(self, which):
        for kind in (2, 3):
            self.ring(which, kind, True).wait_recv()

    def drain(self):
        for which in range(3):
            for kind in range(4):
                self.ring(which, kind).wait_send()
        for turn in range(5):
            self.across(turn).wait_send()


class SetReduce:
    def __init__(self, place, part, whole_in, quarter_in, across_in, send, recv):
        self.place, self.part = place, part
        self.whole_in, self.quarter_in, self.across_in = whole_in, quarter_in, across_in
        self.send, self.recv = send, recv
        self.rows = part.shape[2] // 2

    def ring(self, which, kind):
        place = self.place
        member = place.member if which < 2 else 1 - place.member
        ahead = (1, -1, 1, -1)[kind]
        shift = (1, -1, 2, 2)[kind]
        start = self.rows * (which > 0) + (self.rows // 2 if kind == 3 else 0)
        rows = self.rows if kind < 2 else self.rows // 2
        landing = self.whole_in if kind < 2 else self.quarter_in
        slot = which * 4 + kind
        return pltpu.make_async_remote_copy(
            src_ref=self.part.at[wrap(place.x + shift), member, pl.ds(start, rows)],
            dst_ref=landing.at[which * 2 + kind % 2],
            send_sem=self.send.at[slot],
            recv_sem=self.recv.at[slot],
            device_id=place.at(ahead, 0),
            device_id_type=MESH,
        )

    def across(self, turn):
        place = self.place
        start = self.rows if isinstance(turn, int) and turn == 4 else 0
        return pltpu.make_async_remote_copy(
            src_ref=self.part.at[
                wrap(place.x + turn), 1 - place.member, pl.ds(start, self.rows)
            ],
            dst_ref=self.across_in.at[turn],
            send_sem=self.send.at[12 + turn],
            recv_sem=self.recv.at[12 + turn],
            device_id=place.mate(),
            device_id_type=MESH,
        )

    def take(self, turn):
        self.across(turn).wait_recv()
        rows = pl.ds(self.rows if turn == 4 else 0, self.rows)
        self.part[wrap(self.place.x + turn), self.place.member, rows, :] += self.across_in[turn]

    def begin(self, which):
        for kind in (2, 3):
            self.ring(which, kind).start()

    def middle(self, which):
        member = self.place.member if which < 2 else 1 - self.place.member
        for kind in (2, 3):
            self.ring(which, kind).wait_recv()
            start = self.rows * (which > 0) + (self.rows // 2 if kind == 3 else 0)
            bx = wrap(self.place.x + (1 if kind == 2 else -1))
            self.part[bx, member, pl.ds(start, self.rows // 2), :] += self.quarter_in[
                which * 2 + kind % 2
            ]
            self.ring(which, kind - 2).start()

    def finish(self, which):
        member = self.place.member if which < 2 else 1 - self.place.member
        for kind in (0, 1):
            self.ring(which, kind).wait_recv()
        rows = pl.ds(self.rows * (which > 0), self.rows)
        self.part[self.place.x, member, rows, :] += (
            self.whole_in[which * 2] + self.whole_in[which * 2 + 1]
        )

    def drain(self):
        for which in range(3):
            for kind in range(4):
                self.ring(which, kind).wait_send()
        for turn in range(5):
            self.across(turn).wait_send()


def partner_copy(place, src, dst, send, recv, other_core=False):
    device = place.partner()
    if other_core:
        group = lax.axis_index("wide")
        device = {"wide": group + 1 - 2 * lax.rem(group, 2), **device}
    return pltpu.make_async_remote_copy(
        src_ref=src,
        dst_ref=dst,
        send_sem=send,
        recv_sem=recv,
        device_id=device,
        device_id_type=MESH,
    )


def greet(place, diagonal=False):
    groups = lax.axis_size("wide")
    group = lax.axis_index("wide")
    barrier = pltpu.get_barrier_semaphore()
    for half in (0, 1):
        for shift in (1, -1):
            pl.semaphore_signal(
                barrier,
                inc=1,
                device_id=place.device(half, *place.line(half, 0, shift)),
                device_id_type=MESH,
            )
    for step in range(1, groups):
        pl.semaphore_signal(
            barrier,
            inc=1,
            device_id={"wide": lax.rem(group + step, groups)},
            device_id_type=MESH,
        )
    if diagonal:
        pl.semaphore_signal(
            barrier,
            inc=1,
            device_id={"wide": group + 1 - 2 * lax.rem(group, 2), **place.partner()},
            device_id_type=MESH,
        )
    pl.semaphore_wait(barrier, 4 + groups - 1 + int(diagonal))


def exchange(out_ref, in_ref, send, recv, local):
    groups = lax.axis_size("wide")
    group = lax.axis_index("wide")
    copies = []
    for step in range(1, groups):
        peer = lax.rem(group + step, groups)
        copy = pltpu.make_async_remote_copy(
            src_ref=out_ref.at[peer],
            dst_ref=in_ref.at[group],
            send_sem=send.at[step],
            recv_sem=recv.at[step],
            device_id={"wide": peer},
            device_id_type=MESH,
        )
        copy.start()
        copies.append(copy)
    mine = pltpu.make_async_copy(out_ref.at[group], in_ref.at[group], local)
    mine.start()
    copies.append(mine)
    return copies


class Gather:
    def __init__(self, place, buf, send, recv):
        self.place, self.buf, self.send, self.recv = place, buf, send, recv
        self.rows = buf.shape[2]

    def copy(self, half, turn, kind, block, dest):
        rows = self.rows // 2 if kind < 2 else self.rows // 4
        start = half * (self.rows // 2) + (self.rows // 4 if kind == 3 else 0)
        bx, by = self.place.block(half, *block)
        piece = self.buf.at[bx, by, pl.ds(start, rows)]
        slot = (half * 5 + turn) * 4 + kind
        return pltpu.make_async_remote_copy(
            src_ref=piece,
            dst_ref=piece,
            send_sem=self.send.at[slot],
            recv_sem=self.recv.at[slot],
            device_id=self.place.device(half, *dest),
            device_id_type=MESH,
        )

    def at(self, half, turn, shift):
        first, second = self.place.own(half)
        if isinstance(turn, int) and turn == 0:
            return wrap(first + shift), second
        return wrap(first + turn - 1), wrap(second + shift)

    def describe(self, half, turn, kind):
        shift = (0, 0, -1, 1)[kind]
        ahead = (1, -1, 1, -1)[kind]
        return self.copy(
            half, turn, kind, self.at(half, turn, shift), self.place.line(half, turn, ahead)
        )

    def arrival(self, half, turn, kind):
        shift = (-1, 1, 2, 2)[kind]
        ahead = (1, -1, 1, -1)[kind]
        return self.copy(
            half, turn, kind, self.at(half, turn, shift), self.place.line(half, turn, ahead)
        )

    def begin(self, half, turn):
        self.describe(half, turn, 0).start()
        self.describe(half, turn, 1).start()

    def forward(self, half, turn):
        for kind in (0, 1):
            self.arrival(half, turn, kind).wait_recv()
            self.describe(half, turn, kind + 2).start()

    def finish(self, half, turn):
        for kind in (2, 3):
            self.arrival(half, turn, kind).wait_recv()

    def drain(self):
        for half in (0, 1):
            for turn in range(5):
                for kind in range(4):
                    self.describe(half, turn, kind).wait_send()


def attend(q_ref, da_ref, keys_ref, values_ref, att_ref, dq_ref, dk_ref, dv_ref):
    scale = HEAD_DIM ** (-0.5)
    heads = q_ref.shape[1] // HEAD_DIM
    spans = q_ref.shape[0] // SPAN
    few = keys_ref.shape[2] // spans
    near = SIDE * SIDE * few

    def dot(a, b, ca, cb, precision=MID):
        return lax.dot_general(
            a, b, (((ca,), (cb,)), ((), ())), precision=precision,
            preferred_element_type=jnp.float32,
        )

    def span(c, carry):
        rows = pl.ds(pl.multiple_of(c * SPAN, SPAN), SPAN)
        pieces = pl.ds(pl.multiple_of(c * few, few), few)
        for head in range(heads):
            cols = pl.ds(head * HEAD_DIM, HEAD_DIM)
            q = q_ref[rows, cols]
            da = da_ref[rows, cols]
            k = keys_ref[:, :, pieces, cols].reshape(near, HEAD_DIM)
            v = values_ref[:, :, pieces, cols].reshape(near, HEAD_DIM)
            scores = dot(q, k, 1, 1, HIGH) * scale
            dp = dot(da, v, 1, 1)
            top = jnp.max(scores, axis=-1, keepdims=True)
            e = jnp.exp(scores - top)
            probs = e / jnp.sum(e, axis=-1, keepdims=True)
            ds = probs * (dp - jnp.sum(dp * probs, axis=-1, keepdims=True)) * scale
            att_ref[rows, cols] = dot(probs, v, 1, 0)
            dq_ref[rows, cols] = dot(ds, k, 1, 0)
            shape = (SIDE, SIDE, few, HEAD_DIM)
            dk_ref[:, :, pieces, cols] = dot(ds, q, 0, 0).reshape(shape)
            dv_ref[:, :, pieces, cols] = dot(probs, da, 0, 0).reshape(shape)
        return carry

    lax.fori_loop(0, spans, span, 0)


class Spread:
    def __init__(self, place, source, wide_w, send, recv):
        self.place, self.source, self.w = place, source, wide_w
        self.send, self.recv = send, recv
        self.group = lax.axis_index("wide")
        self.z, self.core = self.group // 2, lax.rem(self.group, 2)
        self.width = source.shape[3]

    def slot(self, group):
        return self.w.at[group // 2, lax.rem(group, 2), :, pl.ds(self.width, self.width)]

    def first(self):
        block = self.source.at[self.z, 2 * (1 - self.place.set) + self.core]
        return partner_copy(
            self.place, block, self.slot(self.group), self.send.at[0], self.recv.at[0]
        )

    def to(self, index, group, target):
        return pltpu.make_async_remote_copy(
            src_ref=self.slot(group),
            dst_ref=self.slot(group),
            send_sem=self.send.at[index],
            recv_sem=self.recv.at[index],
            device_id={"wide": target},
            device_id_type=MESH,
        )

    def along(self, step, arriving=False):
        there = wrap(self.z + step) * 2 + self.core
        back = wrap(self.z - step) * 2 + self.core
        return self.to(step, back if arriving else self.group, there)

    def beside(self, step, arriving=False):
        core = 1 - self.core if arriving else self.core
        other = self.z * 2 + 1 - self.core
        return self.to(4 + step, wrap(self.z - step) * 2 + core, other)

    def spread(self):
        self.first().wait_recv()
        for step in (1, 3, 2):
            self.along(step).start()
        self.beside(0).start()

    def pass_on(self):
        for step in (1, 3, 2):
            self.along(step, True).wait_recv()
            self.beside(step).start()

    def finish(self):
        for step in range(SIDE):
            self.beside(step, True).wait_recv()

    def drain(self):
        self.first().wait_send()
        for step in (1, 2, 3):
            self.along(step).wait_send()
        for step in range(SIDE):
            self.beside(step).wait_send()


def gather_kernel(
    hid_ref,
    cot_ref,
    table_ref,
    pick_ref,
    slot_ref,
    wq_ref,
    wo_ref,
    wk_ref,
    wv_ref,
    hid_out,
    cot_out,
    nei_out,
    wq_out,
    att_ref,
    dq_ref,
    dk_ref,
    dv_ref,
    q_two,
    da_two,
    q_came,
    da_came,
    keys_ref,
    values_ref,
    hid,
    cot,
    nei,
    wq,
    wo,
    wkv,
    going,
    came,
    hid_send,
    hid_recv,
    cot_send,
    cot_recv,
    nei_send,
    nei_recv,
    wq_send,
    wq_recv,
    wo_send,
    wo_recv,
    pair_send,
    pair_recv,
    swap_send,
    swap_recv,
    load_sem,
    store_sem,
):
    place = Place()
    x, y = place.x, place.y
    tokens, width = dq_ref.shape
    groups, cap, piece_rows, _ = came.shape
    inst = nei.shape[2] // piece_rows
    own = [
        pltpu.make_async_copy(hid_ref, hid.at[x, place.member], load_sem.at[0]),
        pltpu.make_async_copy(cot_ref, cot.at[x, place.member], load_sem.at[1]),
    ]
    mine = pl.ds(2 * place.set, 2)
    left = pl.ds(0, width)
    weights = [
        pltpu.make_async_copy(wq_ref.at[:, mine], wq.at[:, :, :, left], load_sem.at[2]),
        pltpu.make_async_copy(wo_ref.at[:, mine], wo.at[:, :, :, left], load_sem.at[3]),
        pltpu.make_async_copy(wk_ref, wkv.at[:, pl.ds(0, width)], load_sem.at[4]),
        pltpu.make_async_copy(wv_ref, wkv.at[:, pl.ds(width, width)], load_sem.at[5]),
    ]
    for copy in own:
        copy.start()
    greet(place)
    for copy in own:
        copy.wait()
    pair = [
        SetGather(place, hid, hid_send, hid_recv),
        SetGather(place, cot, cot_send, cot_recv),
    ]
    near = Gather(place, nei, nei_send, nei_recv)
    spreads = [
        Spread(place, wq_ref, wq, wq_send, wq_recv),
        Spread(place, wo_ref, wo, wo_send, wo_recv),
    ]
    for gather in pair:
        gather.begin(0)
        gather.across(4).start()
    for spread in spreads:
        spread.first().start()
    for gather in pair:
        gather.across(0).start()
        gather.begin(1)
    for i in range(groups * cap):
        going[i // cap, i % cap] = table_ref[pick_ref[i]]
    swaps = exchange(going, came, swap_send, swap_recv, load_sem.at[6])
    for copy in weights:
        copy.start()
    for gather in pair:
        gather.forward(0)
        gather.across(1).start()
        gather.across(3).start()
        gather.across(4, True).wait_recv()
        gather.begin(2)
    for spread in spreads:
        spread.spread()
    for copy in swaps:
        copy.wait()
    for i in range(inst):
        slot = slot_ref[i]
        nei[x, y, pl.ds(i * piece_rows, piece_rows), :] = came[slot // cap, lax.rem(slot, cap)]
    for half in (0, 1):
        near.begin(half, 0)
    for gather in pair:
        gather.finish(0)
        gather.across(2).start()
    for gather in pair:
        gather.forward(1)
    for half in (0, 1):
        near.begin(half, 1)
    for gather in pair:
        gather.forward(2)
    for spread in spreads:
        spread.pass_on()
    for half in (0, 1):
        near.forward(half, 0)
        near.begin(half, 2)
        near.begin(half, 4)
    for copy in weights:
        copy.wait()
    for spread in spreads:
        spread.finish()
    keep_weights = pltpu.make_async_copy(wq, wq_out, load_sem.at[7])
    keep_weights.start()
    q_two[...] = jnp.zeros_like(q_two)
    da_two[...] = jnp.zeros_like(da_two)

    def project(half, bx):
        rows = pl.ds(half * (tokens // 2), tokens // 2)

        def column(member, carry):
            q_two[rows, :] += jnp.dot(
                hid[bx, member, rows, :], wq[bx, member], precision=HIGH,
                preferred_element_type=jnp.float32,
            )
            da_two[rows, :] += jnp.dot(
                cot[bx, member, rows, :], wo[bx, member], precision=MID,
                preferred_element_type=jnp.float32,
            )
            return carry

        lax.fori_loop(0, 2, column, 0)

    for turn in (0, 1, 3, 2):
        for gather in pair:
            gather.across(turn, True).wait_recv()
        project(0, wrap(x + turn))
    for half in (0, 1):
        near.finish(half, 0)
        near.begin(half, 3)
    for gather in pair:
        gather.finish(1)
        gather.finish(2)

    def second_half(bx, carry):
        project(1, bx)
        return carry

    lax.fori_loop(0, SIDE, second_half, 0)
    right = pl.ds(width, width)
    halves = [
        partner_copy(place, q_two.at[:, right], q_came, pair_send.at[0], pair_recv.at[0]),
        partner_copy(place, da_two.at[:, right], da_came, pair_send.at[1], pair_recv.at[1]),
    ]
    for copy in halves:
        copy.start()
    keeps = [
        pltpu.make_async_copy(hid, hid_out, store_sem.at[0]),
        pltpu.make_async_copy(cot, cot_out, store_sem.at[1]),
    ]
    for copy in keeps:
        copy.start()

    def turn_of(step):
        return step + (step // 2) * (1 - 2 * lax.rem(step, 2)) + 1

    def near_project(half, first):
        few = nei.shape[2] // 2
        rows = pl.ds(half * few, few)
        if half == 0:
            blocks = nei[first, :, rows, :]
        else:
            blocks = nei[:, first, rows, :]
        both = jnp.dot(
            blocks.reshape(SIDE * few, nei.shape[3]), wkv[...], precision=HIGH,
            preferred_element_type=jnp.float32,
        ).reshape(SIDE, few, 2 * width)
        if half == 0:
            keys_ref[first, :, rows, :] = both[:, :, :width]
            values_ref[first, :, rows, :] = both[:, :, width:]
        else:
            keys_ref[:, first, rows, :] = both[:, :, :width]
            values_ref[:, first, rows, :] = both[:, :, width:]

    def keep(half, turn, first):
        rows = pl.ds(half * (nei.shape[2] // 2), nei.shape[2] // 2)
        at = (first, slice(None), rows) if half == 0 else (slice(None), first, rows)
        return pltpu.make_async_copy(nei.at[at], nei_out.at[at], store_sem.at[2 + half * 5 + turn])

    def pass_on(turn):
        for half in (0, 1):
            near.forward(half, turn)

    pass_on(turn_of(0))

    def main(step, carry):
        @pl.when(step < SIDE - 1)
        def _():
            pass_on(turn_of(step + 1))

        turn = turn_of(step)
        for half in (0, 1):
            near.finish(half, turn)
            first = wrap(place.own(half)[0] + turn - 1)
            keep(half, turn, first).start()
            near_project(half, first)
        return carry

    lax.fori_loop(0, SIDE, main, 0)
    for copy in halves:
        copy.wait()
    q_came[...] += q_two[:, :width]
    da_came[...] += da_two[:, :width]
    attend(q_came, da_came, keys_ref, values_ref, att_ref, dq_ref, dk_ref, dv_ref)
    for target in (*pair, near, *spreads):
        target.drain()
    keep_weights.wait()
    for copy in keeps:
        copy.wait()

    def stored(turn, carry):
        for half in (0, 1):
            keep(half, turn, wrap(place.own(half)[0] + turn - 1)).wait()
        return carry

    lax.fori_loop(1, SIDE + 1, stored, 0)


class Reduce:
    def __init__(self, place, part, whole_in, quarter_in, send, recv):
        self.place, self.part = place, part
        self.whole_in, self.quarter_in = whole_in, quarter_in
        self.send, self.recv = send, recv
        self.rows = part.shape[2]

    def at(self, half, turn, shift):
        first, second = self.place.own(half)
        if isinstance(turn, int) and turn == 0:
            return wrap(first + shift), second
        return wrap(first + turn - 1), wrap(second + shift)

    def piece(self, half, block, kind):
        rows = self.rows // 2 if kind < 2 else self.rows // 4
        start = half * (self.rows // 2) + (self.rows // 4 if kind == 3 else 0)
        bx, by = self.place.block(half, *block)
        return bx, by, pl.ds(start, rows)

    def copy(self, half, turn, kind):
        ahead = (1, -1, 1, -1)[kind]
        shift = (1, -1, 2, 2)[kind]
        slot = (half * 5 + turn) * 2 + kind % 2
        landing = (self.whole_in if kind < 2 else self.quarter_in).at[slot]
        bx, by, rows = self.piece(half, self.at(half, turn, shift), kind)
        sem = (half * 5 + turn) * 4 + kind
        return pltpu.make_async_remote_copy(
            src_ref=self.part.at[bx, by, rows],
            dst_ref=landing,
            send_sem=self.send.at[sem],
            recv_sem=self.recv.at[sem],
            device_id=self.place.device(half, *self.place.line(half, turn, ahead)),
            device_id_type=MESH,
        )

    def begin(self, half, turn):
        for kind in (2, 3):
            self.copy(half, turn, kind).start()

    def middle(self, half, turn):
        for kind in (2, 3):
            self.copy(half, turn, kind).wait_recv()
            slot = (half * 5 + turn) * 2 + kind % 2
            shift = 1 if kind == 2 else -1
            bx, by, rows = self.piece(half, self.at(half, turn, shift), kind)
            self.part[bx, by, rows, :] += self.quarter_in[slot]
            self.copy(half, turn, kind - 2).start()

    def finish(self, half, turn):
        for kind in (0, 1):
            self.copy(half, turn, kind).wait_recv()
        slot = (half * 5 + turn) * 2
        bx, by, rows = self.piece(half, self.at(half, turn, 0), 0)
        self.part[bx, by, rows, :] += self.whole_in[slot] + self.whole_in[slot + 1]

    def drain(self):
        for half in (0, 1):
            for turn in range(5):
                for kind in range(4):
                    self.copy(half, turn, kind).wait_send()


class Ring:
    def __init__(self, w, near_in, whole_in, half_in, send, recv, keep):
        group = lax.axis_index("wide")
        self.z, self.core, self.keep = group // 2, lax.rem(group, 2), keep
        self.w, self.near_in, self.whole_in, self.half_in = w, near_in, whole_in, half_in
        self.send, self.recv = send, recv
        self.half_rows = w.shape[2] // 2

    def swap(self, turn, shift):
        to = wrap(self.z + shift)
        return pltpu.make_async_remote_copy(
            src_ref=self.w.at[1 - self.keep, to],
            dst_ref=self.near_in.at[to],
            send_sem=self.send.at[4 + turn],
            recv_sem=self.recv.at[4 + turn],
            device_id={"wide": self.z * 2 + 1 - self.core},
            device_id_type=MESH,
        )

    def take(self, turn, shift):
        self.swap(turn, shift).wait_recv()
        to = wrap(self.z + shift)
        self.w[self.keep, to] += self.near_in[to]

    def copy(self, kind):
        ahead = (1, -1, 1, -1)[kind]
        shift = (1, -1, 2, 2)[kind]
        source = self.w.at[self.keep, wrap(self.z + shift)]
        landing = self.whole_in
        if kind >= 2:
            source = source.at[pl.ds((kind - 2) * self.half_rows, self.half_rows)]
            landing = self.half_in
        return pltpu.make_async_remote_copy(
            src_ref=source,
            dst_ref=landing.at[kind % 2],
            send_sem=self.send.at[kind],
            recv_sem=self.recv.at[kind],
            device_id={"wide": wrap(self.z + ahead) * 2 + self.core},
            device_id_type=MESH,
        )

    def begin(self):
        self.take(0, 2)
        for kind in (2, 3):
            self.copy(kind).start()

    def middle(self):
        for kind in (2, 3):
            shift = 1 if kind == 2 else -1
            self.take(kind - 1, shift)
            self.copy(kind).wait_recv()
            rows = pl.ds((kind - 2) * self.half_rows, self.half_rows)
            self.w[self.keep, wrap(self.z + shift), rows, :] += self.half_in[kind - 2]
            self.copy(kind - 2).start()
        self.take(3, 0)

    def finish(self):
        for kind in (0, 1):
            self.copy(kind).wait_recv()
        return self.w[self.keep, self.z] + self.whole_in[0] + self.whole_in[1]

    def drain(self):
        for kind in range(4):
            self.copy(kind).wait_send()
        for turn, shift in enumerate((2, 1, 3, 0)):
            self.swap(turn, shift).wait_send()


TURNS = (3, 2, 4, 1)


def shift_of(step):
    return 2 - step + 3 * (step // 2) - 2 * (step // 3)


def stream(count, loads, work):
    for copy in loads(0, 0):
        copy.start()

    def one(i, carry):
        slot = lax.rem(i, 2)

        @pl.when(i + 1 < count)
        def _():
            for copy in loads(i + 1, 1 - slot):
                copy.start()

        for copy in loads(i, slot):
            copy.wait()
        work(i, slot)
        return carry

    lax.fori_loop(0, count, one, 0)


def reduce_kernel(
    dq_ref,
    att_ref,
    inst_ref,
    dk_hbm,
    dv_hbm,
    hid_hbm,
    cot_hbm,
    nei_hbm,
    wq_hbm,
    wk_hbm,
    wv_hbm,
    gh_ref,
    came_ref,
    gq_ref,
    go_ref,
    gk_ref,
    gv_ref,
    dq_two,
    att_two,
    gpart,
    dpart,
    ghalf,
    gquarter,
    gacross,
    dhalf,
    dquarter,
    w_tile,
    tile,
    near_tile,
    dk_tile,
    dv_tile,
    wk,
    wv,
    going,
    mine,
    out_w,
    out_near,
    out_whole,
    out_half,
    in_w,
    in_near,
    in_whole,
    in_half,
    kv_w,
    kv_near,
    kv_whole,
    kv_half,
    gq_done,
    go_done,
    g_send,
    g_recv,
    d_send,
    d_recv,
    out_send,
    out_recv,
    in_send,
    in_recv,
    kv_send,
    kv_recv,
    pair_send,
    pair_recv,
    swap_send,
    swap_recv,
    load_sem,
    tile_sem,
    near_sem,
):
    place = Place()
    x, y = place.x, place.y
    width = dq_ref.shape[1]
    piece_rows = going.shape[2]
    groups, cap = going.shape[:2]
    rows, enc = dpart.shape[2:]
    weights = [
        pltpu.make_async_copy(wk_hbm, wk, load_sem.at[1]),
        pltpu.make_async_copy(wv_hbm, wv, load_sem.at[2]),
    ]
    for copy in weights:
        copy.start()
    right = pl.ds(width, width)
    halves = [
        partner_copy(place, dq_ref, dq_two.at[:, right], pair_send.at[0], pair_recv.at[0]),
        partner_copy(place, att_ref, att_two.at[:, right], pair_send.at[1], pair_recv.at[1]),
    ]
    greet(place, True)
    for copy in halves:
        copy.start()
    dq_two[:, :width] = dq_ref[...]
    att_two[:, :width] = att_ref[...]
    core = lax.rem(lax.axis_index("wide"), 2)
    keep = lax.rem(core + place.set, 2)
    wide_sum = SetReduce(place, gpart, ghalf, gquarter, gacross, g_send, g_recv)
    near_sum = Reduce(place, dpart, dhalf, dquarter, d_send, d_recv)
    out_ring = Ring(out_w, out_near, out_whole, out_half, out_send, out_recv, keep)
    in_ring = Ring(in_w, in_near, in_whole, in_half, in_send, in_recv, keep)
    kv_ring = Ring(kv_w, kv_near, kv_whole, kv_half, kv_send, kv_recv, core)

    def dot(a, b, ca, cb):
        return lax.dot_general(
            a, b, (((ca,), (cb,)), ((), ())), precision=MID, preferred_element_type=jnp.float32
        )

    def g_load(i, slot):
        block = wq_hbm.at[wrap(x + shift_of(i // 2)), lax.rem(i, 2)]
        return [pltpu.make_async_copy(block, w_tile.at[slot], tile_sem.at[slot])]

    def g_work(i, slot):
        shift = shift_of(i // 2)
        gpart[wrap(x + shift), lax.rem(i, 2)] = dot(dq_two[...], w_tile[slot], 1, 1)

        @pl.when(i == 1)
        def _():
            wide_sum.begin(1)
            wide_sum.begin(2)

        @pl.when(lax.rem(i, 2) == 1)
        def _():
            wide_sum.across(shift).start()

    def weight_grad(source, two_ref, ring):
        def load(i, slot):
            block = source.at[wrap(ring.z + shift_of(i // 2)), lax.rem(i, 2)]
            return [pltpu.make_async_copy(block, tile.at[slot], tile_sem.at[slot])]

        def work(i, slot):
            shift, u = shift_of(i // 2), lax.rem(i, 2)
            part = pl.ds(pl.multiple_of(u * width, width), width)
            both = dot(tile[slot], two_ref[...], 0, 0)
            ring.w[0, wrap(ring.z + shift), part, :] = both[:, :width]
            ring.w[1, wrap(ring.z + shift), part, :] = both[:, width:]

            @pl.when(u == 1)
            def _():
                ring.swap(i // 2, shift).start()

        stream(2 * SIDE, load, work)

    def handed(which, done, out_ref):
        return partner_copy(
            place, done, out_ref, pair_send.at[2 + which], pair_recv.at[2 + which], True
        )

    def deliver(which, ring, done, out_ref):
        done[...] = ring.finish()

        @pl.when(keep == 0)
        def _():
            out_ref[...] = done[...]

        @pl.when(keep == 1)
        def _():
            handed(which, done, out_ref).start()

    def delivered(which, done, out_ref):
        @pl.when(keep == 1)
        def _():
            handed(which, done, out_ref).wait()

    def near_load(sources):
        def load(i, slot):
            at = (i // 2, pl.ds(2 * lax.rem(i, 2), 2))
            return [
                pltpu.make_async_copy(source.at[at], buf.at[slot], near_sem.at[2 * which + slot])
                for which, (source, buf) in enumerate(sources)
            ]

        return load

    def d_work(i, slot):
        bx, by = i // 2, 2 * lax.rem(i, 2)
        dk = dk_tile[slot].reshape(2 * rows, width)
        dv = dv_tile[slot].reshape(2 * rows, width)
        dpart[bx, pl.ds(by, 2)] = (dot(dk, wk[...], 1, 1) + dot(dv, wv[...], 1, 1)).reshape(
            2, rows, enc
        )

    def neighbour_grad():
        for copy in weights:
            copy.wait()
        stream(2 * SIDE, near_load(((dk_hbm, dk_tile), (dv_hbm, dv_tile))), d_work)
        for turn in TURNS:
            for half in (0, 1):
                near_sum.begin(half, turn)

    def kv_work(i, slot):
        dk = dk_tile[slot].reshape(2 * rows, width)
        dv = dv_tile[slot].reshape(2 * rows, width)
        near = near_tile[slot].reshape(2 * rows, enc)
        pair = dot(near, jnp.concatenate([dk, dv], axis=1), 0, 0)
        for group in range(groups):
            share = pair[group * kv_w.shape[2] : (group + 1) * kv_w.shape[2]]
            kv_w[group % 2, group // 2] += share

    def kv_grad():
        kv_w[...] = jnp.zeros_like(kv_w)
        stream(
            2 * SIDE, near_load(((dk_hbm, dk_tile), (dv_hbm, dv_tile), (nei_hbm, near_tile))), kv_work
        )
        for turn, shift in enumerate((2, 1, 3, 0)):
            kv_ring.swap(turn, shift).start()

    def near_middle(turn):
        for half in (0, 1):
            near_sum.middle(half, turn)

    def near_finish(turn):
        for half in (0, 1):
            near_sum.finish(half, turn)
        if turn == 3:
            for half in (0, 1):
                near_sum.begin(half, 0)

    neighbour_grad()
    halves[0].wait()
    stream(2 * SIDE, g_load, g_work)
    weight_grad(hid_hbm, dq_two, in_ring)
    wide_sum.middle(1)
    wide_sum.take(2)
    wide_sum.begin(0)
    in_ring.begin()
    halves[1].wait()
    weight_grad(cot_hbm, att_two, out_ring)
    near_middle(3)
    near_middle(4)
    near_middle(2)
    out_ring.begin()
    in_ring.middle()
    kv_grad()
    near_finish(3)
    kv_ring.begin()
    wide_sum.middle(2)
    near_middle(1)
    out_ring.middle()
    near_finish(4)
    deliver(0, in_ring, gq_done, gq_ref)
    near_finish(2)
    near_middle(0)
    wide_sum.take(1)
    wide_sum.take(3)
    kv_ring.middle()
    wide_sum.finish(2)
    wide_sum.across(4).start()
    wide_sum.finish(1)
    near_finish(1)
    deliver(1, out_ring, go_done, go_ref)
    wide_sum.middle(0)
    near_finish(0)
    for i in range(groups * cap):
        mine[i] = dpart[x, y, pl.ds(i * piece_rows, piece_rows), :]
    for slot in range(groups * cap):
        going[slot // cap, slot % cap] = mine[inst_ref[slot]]
    swaps = exchange(going, came_ref, swap_send, swap_recv, load_sem.at[3])
    wide_sum.take(0)
    pair = kv_ring.finish()
    gk_ref[...] = pair[:, :width]
    gv_ref[...] = pair[:, width:]
    wide_sum.take(4)
    wide_sum.finish(0)
    gh_ref[...] = gpart[x, place.member]
    delivered(0, gq_done, gq_ref)
    delivered(1, go_done, go_ref)
    for copy in swaps:
        copy.wait()
    for target in (wide_sum, near_sum, out_ring, in_ring, kv_ring):
        target.drain()


def result_kernel(slot_ref, came_ref, *refs):
    sources, table_ref, results = refs[:5], refs[5], refs[6:]
    for source, result in zip(sources, results):
        result[...] = source[...]
    table_ref[...] = jnp.zeros_like(table_ref)
    cap = came_ref.shape[1]
    for i in range(came_ref.shape[0] * cap):
        slot = slot_ref[i]
        table_ref[slot] += came_ref[i // cap, i % cap]


def vmem(n):
    return [pl.BlockSpec(memory_space=pltpu.VMEM)] * n


def hbm(n):
    return [pl.BlockSpec(memory_space=pl.ANY)] * n


def smem(n):
    return [pl.BlockSpec(memory_space=pltpu.SMEM)] * n


def f32(*shape):
    return jax.ShapeDtypeStruct(shape, jnp.float32)


def gather_call(hidden, cotangent, table, picks, slots, wq, wo, wk, wv, groups):
    tokens, width = hidden.shape
    _, piece_rows, enc = table.shape
    going = (groups, slots.shape[0] // groups, piece_rows, enc)
    rows = slots.shape[0] * piece_rows
    dma = pltpu.SemaphoreType.DMA
    blocks = (SIDE, 2, tokens, width)
    pairs = (SIDE, 2, width, 2 * width)
    out_shape = [
        f32(*blocks),
        f32(*blocks),
        f32(SIDE, SIDE, rows, enc),
        f32(*pairs),
        f32(tokens, width),
        f32(tokens, width),
        f32(SIDE, SIDE, rows, width),
        f32(SIDE, SIDE, rows, width),
    ]
    scratch = [
        pltpu.VMEM((tokens, 2 * width), jnp.float32),
        pltpu.VMEM((tokens, 2 * width), jnp.float32),
        pltpu.VMEM((tokens, width), jnp.float32),
        pltpu.VMEM((tokens, width), jnp.float32),
        pltpu.VMEM((SIDE, SIDE, rows, width), jnp.float32),
        pltpu.VMEM((SIDE, SIDE, rows, width), jnp.float32),
        pltpu.VMEM(blocks, jnp.float32),
        pltpu.VMEM(blocks, jnp.float32),
        pltpu.VMEM((SIDE, SIDE, rows, enc), jnp.float32),
        pltpu.VMEM(pairs, jnp.float32),
        pltpu.VMEM(pairs, jnp.float32),
        pltpu.VMEM((enc, 2 * width), jnp.float32),
        pltpu.VMEM(going, jnp.float32),
        pltpu.VMEM(going, jnp.float32),
    ]
    scratch += [dma((17,))] * 4 + [dma((40,))] * 2 + [dma((8,))] * 4 + [dma((2,))] * 2
    scratch += [dma((groups,))] * 2 + [dma((8,)), dma((12,))]
    return pl.pallas_call(
        gather_kernel,
        out_shape=out_shape,
        in_specs=hbm(2) + vmem(1) + smem(2) + hbm(4),
        out_specs=hbm(4) + vmem(4),
        scratch_shapes=scratch,
        compiler_params=pltpu.CompilerParams(
            collective_id=0, has_side_effects=True, vmem_limit_bytes=VMEM_LIMIT
        ),
        cost_estimate=pl.CostEstimate(flops=24_000_000_000, bytes_accessed=60_000_000, transcendentals=0),
    )(hidden, cotangent, table, picks, slots, wq, wo, wk, wv)


def reduce_call(dq, att, inst_of, dk, dv, hid, cot, nei, wq, wk, wv, groups):
    tokens, width = dq.shape
    rows = dk.shape[2]
    enc = wk.shape[0]
    slots = inst_of.shape[0]
    cap = slots // groups
    piece_rows = rows // slots
    dma = pltpu.SemaphoreType.DMA
    going = (groups, cap, piece_rows, enc)
    out_rows, enc_rows = 2 * width, enc // groups

    def ring(rows, cols):
        return [
            pltpu.VMEM((*n, r, cols), jnp.float32)
            for n, r in (((2, SIDE), rows), ((SIDE,), rows), ((2,), rows), ((2,), rows // 2))
        ]

    scratch = [
        pltpu.VMEM((tokens, 2 * width), jnp.float32),
        pltpu.VMEM((tokens, 2 * width), jnp.float32),
        pltpu.VMEM((SIDE, 2, tokens, width), jnp.float32),
        pltpu.VMEM((SIDE, SIDE, rows, enc), jnp.float32),
        pltpu.VMEM((6, tokens // 2, width), jnp.float32),
        pltpu.VMEM((6, tokens // 4, width), jnp.float32),
        pltpu.VMEM((5, tokens // 2, width), jnp.float32),
        pltpu.VMEM((20, rows // 2, enc), jnp.float32),
        pltpu.VMEM((20, rows // 4, enc), jnp.float32),
        pltpu.VMEM((2, width, 2 * width), jnp.float32),
        pltpu.VMEM((2, tokens, width), jnp.float32),
        pltpu.VMEM((2, 2, rows, enc), jnp.float32),
        pltpu.VMEM((2, 2, rows, width), jnp.float32),
        pltpu.VMEM((2, 2, rows, width), jnp.float32),
        pltpu.VMEM(wk.shape, jnp.float32),
        pltpu.VMEM(wv.shape, jnp.float32),
        pltpu.VMEM(going, jnp.float32),
        pltpu.VMEM((slots, piece_rows, enc), jnp.float32),
    ]
    scratch += ring(out_rows, width) + ring(out_rows, width) + ring(enc_rows, 2 * width)
    scratch += [pltpu.VMEM((out_rows, width), jnp.float32)] * 2
    scratch += [dma((17,))] * 2 + [dma((40,))] * 2 + [dma((8,))] * 6 + [dma((4,))] * 2
    scratch += [dma((groups,))] * 2 + [dma((4,)), dma((2,)), dma((6,))]
    return pl.pallas_call(
        reduce_kernel,
        out_shape=[
            f32(tokens, width),
            f32(*going),
            f32(out_rows, width),
            f32(out_rows, width),
            f32(enc_rows, width),
            f32(enc_rows, width),
        ],
        in_specs=vmem(2) + smem(1) + hbm(8),
        out_specs=vmem(6),
        scratch_shapes=scratch,
        compiler_params=pltpu.CompilerParams(
            collective_id=1, has_side_effects=True, vmem_limit_bytes=REDUCE_LIMIT
        ),
        cost_estimate=pl.CostEstimate(flops=50_000_000_000, bytes_accessed=60_000_000, transcendentals=0),
    )(dq, att, inst_of, dk, dv, hid, cot, nei, wq, wk, wv)


def body(
    hidden_states, out_cotangent, enc_table, nbr_ids, owner_map, w_query, w_key, w_value, w_out
):
    groups = lax.axis_size("wide")
    group = lax.axis_index("wide")
    stored = enc_table.shape[0]
    table_size = owner_map.shape[0]
    tokens, width = hidden_states.shape
    inst = NEIGH * (tokens // SPAN)
    capacity = inst // groups
    match = nbr_ids[:, :, None] == jnp.arange(table_size, dtype=jnp.int32)[None, None, :]
    slots = jnp.sum(jnp.where(match, owner_map[None, None, :], 0), axis=-1)
    slots = slots.reshape(groups, inst)
    owners = slots // stored
    local_slot = slots - owners * stored
    earlier = jnp.arange(inst)[None, :] < jnp.arange(inst)[:, None]
    same = owners[:, :, None] == owners[:, None, :]
    rank = jnp.sum((same & earlier[None, :, :]).astype(jnp.int32), axis=-1)
    slot_range = jnp.arange(capacity, dtype=jnp.int32)
    pick = (owners[:, None, :] == group) & (rank[:, None, :] == slot_range[None, :, None])
    picks = jnp.sum(jnp.where(pick, local_slot[:, None, :], 0), axis=-1).reshape(-1)
    mine = lax.dynamic_index_in_dim(owners * capacity + rank, group, 0, keepdims=False)
    numbers = jnp.arange(inst, dtype=jnp.int32)
    inst_of = jnp.sum(jnp.where(mine[None, :] == numbers[:, None], numbers[None, :], 0), axis=1)

    query_blocks = w_query.reshape(SIDE, SIDE, width, width)
    out_blocks = w_out.reshape(SIDE, SIDE, width, width)
    hid, cot, nei, query_pair, attended, d_query, d_keys, d_values = gather_call(
        hidden_states, out_cotangent, enc_table, picks, mine, query_blocks, out_blocks, w_key,
        w_value, groups,
    )
    grad_hidden, arrived, grad_query, grad_out, grad_key, grad_value = reduce_call(
        d_query, attended, inst_of, d_keys, d_values, hid, cot, nei, query_pair, w_key, w_value,
        groups,
    )
    sums = (grad_hidden, grad_query, grad_key, grad_value, grad_out)
    grad_table, *sums = pl.pallas_call(
        result_kernel,
        out_shape=[f32(*enc_table.shape)] + [f32(*t.shape) for t in sums],
        in_specs=smem(1) + vmem(6),
        out_specs=vmem(6),
    )(picks, arrived, *sums)
    return (*sums, grad_table)


def solution(mesh):
    placed = (
        P("wide", "narrow"),
        P("wide", "narrow"),
        P("wide", "narrow", None),
        P(),
        P(),
        P(None, "narrow"),
        P(None, "narrow"),
        P(None, "narrow"),
        P(None, "narrow"),
    )
    return jax.shard_map(
        body,
        mesh=mesh,
        in_specs=placed,
        out_specs=(
            P("wide", "narrow"),
            P("wide", "narrow"),
            P("wide", "narrow"),
            P("wide", "narrow"),
            P("wide", "narrow"),
            P("wide", "narrow", None),
        ),
        check_vma=False,
    )
```

```python
import functools

import jax
import jax.numpy as jnp
from jax import lax
from jax.experimental import pallas as pl
from jax.experimental.pallas import tpu as pltpu
from jax.sharding import PartitionSpec as P

HEAD_DIM = 128
SPAN = 64
NEIGH = 2
SIDE = 4
VMEM_LIMIT = 60 * 1024 * 1024
REDUCE_LIMIT = 63 * 1024 * 1024

HIGH = lax.Precision.HIGHEST
MID = lax.Precision.HIGH
MESH = pl.DeviceIdType.MESH


def wrap(value):
    return lax.rem(value + 2 * SIDE, SIDE)


class Place:
    def __init__(self):
        me = lax.axis_index("narrow")
        self.x = me // SIDE
        self.y = lax.rem(me, SIDE)
        self.set = self.y // 2
        self.member = lax.rem(self.y, 2)

    def at(self, dx, dy):
        return {"narrow": wrap(self.x + dx) * SIDE + wrap(self.y + dy)}

    def mate(self):
        return {"narrow": self.x * SIDE + self.y + 1 - 2 * self.member}

    def partner(self):
        return {"narrow": self.x * SIDE + SIDE - 1 - self.y}

    def own(self, half):
        return (self.x, self.y) if half == 0 else (self.y, self.x)

    @staticmethod
    def block(half, first, second):
        return (first, second) if half == 0 else (second, first)

    def device(self, half, first, second):
        bx, by = self.block(half, first, second)
        return {"narrow": bx * SIDE + by}

    def line(self, half, turn, shift):
        first, second = self.own(half)
        if isinstance(turn, int) and turn == 0:
            return wrap(first + shift), second
        return first, wrap(second + shift)


class SetGather:
    def __init__(self, place, buf, send, recv):
        self.place, self.buf, self.send, self.recv = place, buf, send, recv
        self.rows = buf.shape[2] // 2

    def copy(self, slot, bx, member, start, rows, device):
        piece = self.buf.at[bx, member, pl.ds(start, rows)]
        return pltpu.make_async_remote_copy(
            src_ref=piece,
            dst_ref=piece,
            send_sem=self.send.at[slot],
            recv_sem=self.recv.at[slot],
            device_id=device,
            device_id_type=MESH,
        )

    def ring(self, which, kind, arriving=False):
        place = self.place
        member = place.member if which < 2 else 1 - place.member
        ahead = (1, -1, 1, -1)[kind]
        shift = (0, 0, -1, 1)[kind] - (ahead if arriving else 0)
        start = self.rows * (which > 0) + (self.rows // 2 if kind == 3 else 0)
        rows = self.rows if kind < 2 else self.rows // 2
        return self.copy(
            which * 4 + kind, wrap(place.x + shift), member, start, rows, place.at(ahead, 0)
        )

    def across(self, turn, arriving=False):
        place = self.place
        member = 1 - place.member if arriving else place.member
        bx = wrap(place.x + turn)
        start = self.rows if turn == 4 else 0
        return self.copy(12 + turn, bx, member, start, self.rows, place.mate())

    def begin(self, which):
        for kind in (0, 1):
            self.ring(which, kind).start()

    def forward(self, which):
        for kind in (0, 1):
            self.ring(which, kind, True).wait_recv()
            self.ring(which, kind + 2).start()

    def finish(self, which):
        for kind in (2, 3):
            self.ring(which, kind, True).wait_recv()

    def drain(self):
        for which in range(3):
            for kind in range(4):
                self.ring(which, kind).wait_send()
        for turn in range(5):
            self.across(turn).wait_send()


class SetReduce:
    def __init__(self, place, part, whole_in, quarter_in, across_in, send, recv):
        self.place, self.part = place, part
        self.whole_in, self.quarter_in, self.across_in = whole_in, quarter_in, across_in
        self.send, self.recv = send, recv
        self.rows = part.shape[2] // 2

    def ring(self, which, kind):
        place = self.place
        member = place.member if which < 2 else 1 - place.member
        ahead = (1, -1, 1, -1)[kind]
        shift = (1, -1, 2, 2)[kind]
        start = self.rows * (which > 0) + (self.rows // 2 if kind == 3 else 0)
        rows = self.rows if kind < 2 else self.rows // 2
        landing = self.whole_in if kind < 2 else self.quarter_in
        slot = which * 4 + kind
        return pltpu.make_async_remote_copy(
            src_ref=self.part.at[wrap(place.x + shift), member, pl.ds(start, rows)],
            dst_ref=landing.at[which * 2 + kind % 2],
            send_sem=self.send.at[slot],
            recv_sem=self.recv.at[slot],
            device_id=place.at(ahead, 0),
            device_id_type=MESH,
        )

    def across(self, turn):
        place = self.place
        start = self.rows if isinstance(turn, int) and turn == 4 else 0
        return pltpu.make_async_remote_copy(
            src_ref=self.part.at[
                wrap(place.x + turn), 1 - place.member, pl.ds(start, self.rows)
            ],
            dst_ref=self.across_in.at[turn],
            send_sem=self.send.at[12 + turn],
            recv_sem=self.recv.at[12 + turn],
            device_id=place.mate(),
            device_id_type=MESH,
        )

    def take(self, turn):
        self.across(turn).wait_recv()
        rows = pl.ds(self.rows if turn == 4 else 0, self.rows)
        self.part[wrap(self.place.x + turn), self.place.member, rows, :] += self.across_in[turn]

    def begin(self, which):
        for kind in (2, 3):
            self.ring(which, kind).start()

    def middle(self, which):
        member = self.place.member if which < 2 else 1 - self.place.member
        for kind in (2, 3):
            self.ring(which, kind).wait_recv()
            start = self.rows * (which > 0) + (self.rows // 2 if kind == 3 else 0)
            bx = wrap(self.place.x + (1 if kind == 2 else -1))
            self.part[bx, member, pl.ds(start, self.rows // 2), :] += self.quarter_in[
                which * 2 + kind % 2
            ]
            self.ring(which, kind - 2).start()

    def finish(self, which):
        member = self.place.member if which < 2 else 1 - self.place.member
        for kind in (0, 1):
            self.ring(which, kind).wait_recv()
        rows = pl.ds(self.rows * (which > 0), self.rows)
        self.part[self.place.x, member, rows, :] += (
            self.whole_in[which * 2] + self.whole_in[which * 2 + 1]
        )

    def drain(self):
        for which in range(3):
            for kind in range(4):
                self.ring(which, kind).wait_send()
        for turn in range(5):
            self.across(turn).wait_send()


def partner_copy(place, src, dst, send, recv, other_core=False):
    device = place.partner()
    if other_core:
        group = lax.axis_index("wide")
        device = {"wide": group + 1 - 2 * lax.rem(group, 2), **device}
    return pltpu.make_async_remote_copy(
        src_ref=src,
        dst_ref=dst,
        send_sem=send,
        recv_sem=recv,
        device_id=device,
        device_id_type=MESH,
    )


def greet(place, diagonal=False):
    groups = lax.axis_size("wide")
    group = lax.axis_index("wide")
    barrier = pltpu.get_barrier_semaphore()
    for half in (0, 1):
        for shift in (1, -1):
            pl.semaphore_signal(
                barrier,
                inc=1,
                device_id=place.device(half, *place.line(half, 0, shift)),
                device_id_type=MESH,
            )
    for step in range(1, groups):
        pl.semaphore_signal(
            barrier,
            inc=1,
            device_id={"wide": lax.rem(group + step, groups)},
            device_id_type=MESH,
        )
    if diagonal:
        pl.semaphore_signal(
            barrier,
            inc=1,
            device_id={"wide": group + 1 - 2 * lax.rem(group, 2), **place.partner()},
            device_id_type=MESH,
        )
    pl.semaphore_wait(barrier, 4 + groups - 1 + int(diagonal))


def exchange(out_ref, in_ref, send, recv, local):
    groups = lax.axis_size("wide")
    group = lax.axis_index("wide")
    copies = []
    for step in range(1, groups):
        peer = lax.rem(group + step, groups)
        copy = pltpu.make_async_remote_copy(
            src_ref=out_ref.at[peer],
            dst_ref=in_ref.at[group],
            send_sem=send.at[step],
            recv_sem=recv.at[step],
            device_id={"wide": peer},
            device_id_type=MESH,
        )
        copy.start()
        copies.append(copy)
    mine = pltpu.make_async_copy(out_ref.at[group], in_ref.at[group], local)
    mine.start()
    copies.append(mine)
    return copies


class Gather:
    def __init__(self, place, buf, send, recv):
        self.place, self.buf, self.send, self.recv = place, buf, send, recv
        self.rows = buf.shape[2]

    def copy(self, half, turn, kind, block, dest):
        rows = self.rows // 2 if kind < 2 else self.rows // 4
        start = half * (self.rows // 2) + (self.rows // 4 if kind == 3 else 0)
        bx, by = self.place.block(half, *block)
        piece = self.buf.at[bx, by, pl.ds(start, rows)]
        slot = (half * 5 + turn) * 4 + kind
        return pltpu.make_async_remote_copy(
            src_ref=piece,
            dst_ref=piece,
            send_sem=self.send.at[slot],
            recv_sem=self.recv.at[slot],
            device_id=self.place.device(half, *dest),
            device_id_type=MESH,
        )

    def at(self, half, turn, shift):
        first, second = self.place.own(half)
        if isinstance(turn, int) and turn == 0:
            return wrap(first + shift), second
        return wrap(first + turn - 1), wrap(second + shift)

    def describe(self, half, turn, kind):
        shift = (0, 0, -1, 1)[kind]
        ahead = (1, -1, 1, -1)[kind]
        return self.copy(
            half, turn, kind, self.at(half, turn, shift), self.place.line(half, turn, ahead)
        )

    def arrival(self, half, turn, kind):
        shift = (-1, 1, 2, 2)[kind]
        ahead = (1, -1, 1, -1)[kind]
        return self.copy(
            half, turn, kind, self.at(half, turn, shift), self.place.line(half, turn, ahead)
        )

    def begin(self, half, turn):
        self.describe(half, turn, 0).start()
        self.describe(half, turn, 1).start()

    def forward(self, half, turn):
        for kind in (0, 1):
            self.arrival(half, turn, kind).wait_recv()
            self.describe(half, turn, kind + 2).start()

    def finish(self, half, turn):
        for kind in (2, 3):
            self.arrival(half, turn, kind).wait_recv()

    def drain(self):
        for half in (0, 1):
            for turn in range(5):
                for kind in range(4):
                    self.describe(half, turn, kind).wait_send()


def attend(half, q_ref, da_ref, keys_ref, values_ref, att_ref, dq_ref, dk_ref, dv_ref):
    scale = HEAD_DIM ** (-0.5)
    heads = q_ref.shape[1] // HEAD_DIM
    spans = q_ref.shape[0] // SPAN
    few = keys_ref.shape[2] // spans
    near = SIDE * SIDE * few

    def dot(a, b, ca, cb, precision=MID):
        return lax.dot_general(
            a, b, (((ca,), (cb,)), ((), ())), precision=precision,
            preferred_element_type=jnp.float32,
        )

    def span(c, carry):
        rows = pl.ds(pl.multiple_of(c * SPAN, SPAN), SPAN)
        pieces = pl.ds(pl.multiple_of(c * few, few), few)
        for head in range(heads):
            cols = pl.ds(head * HEAD_DIM, HEAD_DIM)
            q = q_ref[rows, cols]
            da = da_ref[rows, cols]
            k = keys_ref[:, :, pieces, cols].reshape(near, HEAD_DIM)
            v = values_ref[:, :, pieces, cols].reshape(near, HEAD_DIM)
            scores = dot(q, k, 1, 1, HIGH) * scale
            dp = dot(da, v, 1, 1)
            top = jnp.max(scores, axis=-1, keepdims=True)
            e = jnp.exp(scores - top)
            probs = e / jnp.sum(e, axis=-1, keepdims=True)
            ds = probs * (dp - jnp.sum(dp * probs, axis=-1, keepdims=True)) * scale
            att_ref[rows, cols] = dot(probs, v, 1, 0)
            dq_ref[rows, cols] = dot(ds, k, 1, 0)
            shape = (SIDE, SIDE, few, HEAD_DIM)
            dk_ref[:, :, pieces, cols] = dot(ds, q, 0, 0).reshape(shape)
            dv_ref[:, :, pieces, cols] = dot(probs, da, 0, 0).reshape(shape)
        return carry

    lax.fori_loop(half * spans // 2, (half + 1) * spans // 2, span, 0)


class Spread:
    def __init__(self, place, source, wide_w, send, recv):
        self.place, self.source, self.w = place, source, wide_w
        self.send, self.recv = send, recv
        self.group = lax.axis_index("wide")
        self.z, self.core = self.group // 2, lax.rem(self.group, 2)
        self.width = source.shape[3]

    def slot(self, group):
        return self.w.at[group // 2, lax.rem(group, 2), :, pl.ds(self.width, self.width)]

    def first(self):
        block = self.source.at[self.z, 2 * (1 - self.place.set) + self.core]
        return partner_copy(
            self.place, block, self.slot(self.group), self.send.at[0], self.recv.at[0]
        )

    def to(self, index, group, target):
        return pltpu.make_async_remote_copy(
            src_ref=self.slot(group),
            dst_ref=self.slot(group),
            send_sem=self.send.at[index],
            recv_sem=self.recv.at[index],
            device_id={"wide": target},
            device_id_type=MESH,
        )

    def along(self, step, arriving=False):
        there = wrap(self.z + step) * 2 + self.core
        back = wrap(self.z - step) * 2 + self.core
        return self.to(step, back if arriving else self.group, there)

    def beside(self, step, arriving=False):
        core = 1 - self.core if arriving else self.core
        other = self.z * 2 + 1 - self.core
        return self.to(4 + step, wrap(self.z - step) * 2 + core, other)

    def spread(self):
        self.first().wait_recv()
        for step in (1, 3, 2):
            self.along(step).start()
        self.beside(0).start()

    def pass_on(self):
        for step in (1, 3, 2):
            self.along(step, True).wait_recv()
            self.beside(step).start()

    def finish(self):
        for step in range(SIDE):
            self.beside(step, True).wait_recv()

    def drain(self):
        self.first().wait_send()
        for step in (1, 2, 3):
            self.along(step).wait_send()
        for step in range(SIDE):
            self.beside(step).wait_send()


def gather_kernel(
    hid_ref,
    cot_ref,
    table_ref,
    pick_ref,
    slot_ref,
    wq_ref,
    wo_ref,
    wk_ref,
    wv_ref,
    hid_out,
    cot_out,
    nei_out,
    wq_out,
    att_ref,
    dq_ref,
    dk_ref,
    dv_ref,
    q_two,
    da_two,
    q_came,
    da_came,
    keys_ref,
    values_ref,
    hid,
    cot,
    nei,
    wq,
    wo,
    wkv,
    going,
    came,
    hid_send,
    hid_recv,
    cot_send,
    cot_recv,
    nei_send,
    nei_recv,
    wq_send,
    wq_recv,
    wo_send,
    wo_recv,
    pair_send,
    pair_recv,
    swap_send,
    swap_recv,
    load_sem,
    store_sem,
):
    place = Place()
    x, y = place.x, place.y
    tokens, width = dq_ref.shape
    groups, cap, piece_rows, _ = came.shape
    inst = nei.shape[2] // piece_rows
    own = [
        pltpu.make_async_copy(hid_ref, hid.at[x, place.member], load_sem.at[0]),
        pltpu.make_async_copy(cot_ref, cot.at[x, place.member], load_sem.at[1]),
    ]
    mine = pl.ds(2 * place.set, 2)
    left = pl.ds(0, width)
    weights = [
        pltpu.make_async_copy(wq_ref.at[:, mine], wq.at[:, :, :, left], load_sem.at[2]),
        pltpu.make_async_copy(wo_ref.at[:, mine], wo.at[:, :, :, left], load_sem.at[3]),
        pltpu.make_async_copy(wk_ref, wkv.at[:, pl.ds(0, width)], load_sem.at[4]),
        pltpu.make_async_copy(wv_ref, wkv.at[:, pl.ds(width, width)], load_sem.at[5]),
    ]
    for copy in own:
        copy.start()
    greet(place)
    for copy in own:
        copy.wait()
    pair = [
        SetGather(place, hid, hid_send, hid_recv),
        SetGather(place, cot, cot_send, cot_recv),
    ]
    near = Gather(place, nei, nei_send, nei_recv)
    spreads = [
        Spread(place, wq_ref, wq, wq_send, wq_recv),
        Spread(place, wo_ref, wo, wo_send, wo_recv),
    ]
    hid_set, cot_set = pair

    def offer():
        for i in range(groups * cap):
            going[i // cap, i % cap] = table_ref[pick_ref[i]]
        return exchange(going, came, swap_send, swap_recv, load_sem.at[6])

    def accept(swaps):
        for copy in swaps:
            copy.wait()
        for i in range(inst):
            slot = slot_ref[i]
            nei[x, y, pl.ds(i * piece_rows, piece_rows), :] = came[
                slot // cap, lax.rem(slot, cap)
            ]

    def set_forward(gather):
        gather.forward(0)
        gather.across(1).start()
        gather.across(3).start()

    def set_other(gather):
        gather.across(4, True).wait_recv()
        gather.begin(2)

    def set_finish(gather):
        gather.finish(0)
        gather.across(2).start()

    def add_products(gather, half, bx):
        rows = pl.ds(half * (tokens // 2), tokens // 2)
        total, weight, precision = (
            (q_two, wq, HIGH) if gather is hid_set else (da_two, wo, MID)
        )

        def column(member, carry):
            total[rows, :] += jnp.dot(
                gather.buf[bx, member, rows, :], weight[bx, member], precision=precision,
                preferred_element_type=jnp.float32,
            )
            return carry

        lax.fori_loop(0, 2, column, 0)

    def project(gather, half):
        if half == 0:
            for turn in (0, 1, 3, 2):
                gather.across(turn, True).wait_recv()
                add_products(gather, 0, wrap(x + turn))
            return
        gather.finish(1)
        gather.finish(2)

        def block(bx, carry):
            add_products(gather, 1, bx)
            return carry

        lax.fori_loop(0, SIDE, block, 0)

    def half_copy(gather, half):
        rows = pl.ds(half * (tokens // 2), tokens // 2)
        total, came_ref = (q_two, q_came) if gather is hid_set else (da_two, da_came)
        sem = half + 2 * int(gather is cot_set)
        return partner_copy(
            place,
            total.at[rows, pl.ds(width, width)],
            came_ref.at[rows],
            pair_send.at[sem],
            pair_recv.at[sem],
        )

    def add_half(gather, half):
        half_copy(gather, half).wait_recv()
        rows = pl.ds(half * (tokens // 2), tokens // 2)
        total, came_ref = (q_two, q_came) if gather is hid_set else (da_two, da_came)
        came_ref[rows, :] += total[rows, :width]

    def near_keep(half, turn):
        first = wrap(place.own(half)[0] + turn - 1)
        rows = pl.ds(half * (nei.shape[2] // 2), nei.shape[2] // 2)
        at = (first, slice(None), rows) if half == 0 else (slice(None), first, rows)
        return pltpu.make_async_copy(nei.at[at], nei_out.at[at], store_sem.at[2 + half * 5 + turn])

    def near_project(half, turn):
        near.finish(half, turn)
        near_keep(half, turn).start()
        first = wrap(place.own(half)[0] + turn - 1)
        few = nei.shape[2] // 2
        rows = pl.ds(half * few, few)
        if half == 0:
            blocks = nei[first, :, rows, :]
        else:
            blocks = nei[:, first, rows, :]
        both = jnp.dot(
            blocks.reshape(SIDE * few, nei.shape[3]), wkv[...], precision=HIGH,
            preferred_element_type=jnp.float32,
        ).reshape(SIDE, few, 2 * width)
        if half == 0:
            keys_ref[first, :, rows, :] = both[:, :, :width]
            values_ref[first, :, rows, :] = both[:, :, width:]
        else:
            keys_ref[:, first, rows, :] = both[:, :, :width]
            values_ref[:, first, rows, :] = both[:, :, width:]

    def near_begin(turn):
        for half in (0, 1):
            near.begin(half, turn)

    attended = (q_came, da_came, keys_ref, values_ref, att_ref, dq_ref, dk_ref, dv_ref)

    hid_set.begin(1)
    hid_set.across(4).start()
    cot_set.begin(1)
    for spread in spreads:
        spread.first().start()
    cot_set.begin(0)
    swaps = offer()
    cot_set.across(0).start()
    cot_set.across(4).start()
    for copy in weights:
        copy.start()
    q_two[...] = jnp.zeros_like(q_two)
    da_two[...] = jnp.zeros_like(da_two)
    for spread in spreads:
        spread.spread()
    set_other(hid_set)
    accept(swaps)
    near_begin(1)
    set_forward(cot_set)
    near_begin(0)
    for spread in spreads:
        spread.pass_on()
    set_other(cot_set)
    near.forward(0, 1)
    hid_set.begin(0)
    set_finish(cot_set)
    cot_set.forward(1)
    cot_set.forward(2)
    for half in (0, 1):
        near.forward(half, 0)
    near_begin(2)
    near_begin(4)
    for copy in weights:
        copy.wait()
    for spread in spreads:
        spread.finish()
    keep_weights = pltpu.make_async_copy(wq, wq_out, load_sem.at[7])
    keep_weights.start()
    near.forward(0, 2)
    hid_set.across(0).start()
    project(cot_set, 1)
    half_copy(cot_set, 1).start()
    set_forward(hid_set)
    near_project(0, 2)
    hid_set.forward(2)
    project(cot_set, 0)
    near_project(0, 1)
    set_finish(hid_set)
    hid_set.forward(1)
    near.forward(1, 2)
    for half in (0, 1):
        near.finish(half, 0)
    near_begin(3)
    half_copy(cot_set, 0).start()
    keep_cot = pltpu.make_async_copy(cot, cot_out, store_sem.at[1])
    keep_cot.start()
    project(hid_set, 1)
    near.forward(1, 1)
    add_half(cot_set, 1)
    half_copy(hid_set, 1).start()
    near_project(1, 2)
    near.forward(1, 4)
    near.forward(0, 4)
    near.forward(1, 3)
    project(hid_set, 0)
    half_copy(hid_set, 0).start()
    keep_hid = pltpu.make_async_copy(hid, hid_out, store_sem.at[0])
    keep_hid.start()
    near_project(1, 1)
    near_project(1, 4)
    near_project(1, 3)
    near.forward(0, 3)
    add_half(hid_set, 1)
    attend(1, *attended)
    add_half(cot_set, 0)
    near_project(0, 4)
    near_project(0, 3)
    add_half(hid_set, 0)
    attend(0, *attended)
    for target in (*pair, near, *spreads):
        target.drain()
    for gather in pair:
        for half in (0, 1):
            half_copy(gather, half).wait_send()
    for copy in (keep_weights, keep_hid, keep_cot):
        copy.wait()
    for half in (0, 1):
        for turn in range(1, SIDE + 1):
            near_keep(half, turn).wait()


class Reduce:
    def __init__(self, place, part, whole_in, quarter_in, send, recv):
        self.place, self.part = place, part
        self.whole_in, self.quarter_in = whole_in, quarter_in
        self.send, self.recv = send, recv
        self.rows = part.shape[2]

    def at(self, half, turn, shift):
        first, second = self.place.own(half)
        if isinstance(turn, int) and turn == 0:
            return wrap(first + shift), second
        return wrap(first + turn - 1), wrap(second + shift)

    def piece(self, half, block, kind):
        rows = self.rows // 2 if kind < 2 else self.rows // 4
        start = half * (self.rows // 2) + (self.rows // 4 if kind == 3 else 0)
        bx, by = self.place.block(half, *block)
        return bx, by, pl.ds(start, rows)

    def copy(self, half, turn, kind):
        ahead = (1, -1, 1, -1)[kind]
        shift = (1, -1, 2, 2)[kind]
        slot = (half * 5 + turn) * 2 + kind % 2
        landing = (self.whole_in if kind < 2 else self.quarter_in).at[slot]
        bx, by, rows = self.piece(half, self.at(half, turn, shift), kind)
        sem = (half * 5 + turn) * 4 + kind
        return pltpu.make_async_remote_copy(
            src_ref=self.part.at[bx, by, rows],
            dst_ref=landing,
            send_sem=self.send.at[sem],
            recv_sem=self.recv.at[sem],
            device_id=self.place.device(half, *self.place.line(half, turn, ahead)),
            device_id_type=MESH,
        )

    def begin(self, half, turn):
        for kind in (2, 3):
            self.copy(half, turn, kind).start()

    def middle(self, half, turn):
        for kind in (2, 3):
            self.copy(half, turn, kind).wait_recv()
            slot = (half * 5 + turn) * 2 + kind % 2
            shift = 1 if kind == 2 else -1
            bx, by, rows = self.piece(half, self.at(half, turn, shift), kind)
            self.part[bx, by, rows, :] += self.quarter_in[slot]
            self.copy(half, turn, kind - 2).start()

    def finish(self, half, turn):
        for kind in (0, 1):
            self.copy(half, turn, kind).wait_recv()
        slot = (half * 5 + turn) * 2
        bx, by, rows = self.piece(half, self.at(half, turn, 0), 0)
        self.part[bx, by, rows, :] += self.whole_in[slot] + self.whole_in[slot + 1]

    def drain(self):
        for half in (0, 1):
            for turn in range(5):
                for kind in range(4):
                    self.copy(half, turn, kind).wait_send()


class Ring:
    def __init__(self, w, near_in, whole_in, half_in, send, recv, keep):
        group = lax.axis_index("wide")
        self.z, self.core, self.keep = group // 2, lax.rem(group, 2), keep
        self.w, self.near_in, self.whole_in, self.half_in = w, near_in, whole_in, half_in
        self.send, self.recv = send, recv
        self.half_rows = w.shape[2] // 2

    def swap(self, turn, shift):
        to = wrap(self.z + shift)
        return pltpu.make_async_remote_copy(
            src_ref=self.w.at[1 - self.keep, to],
            dst_ref=self.near_in.at[to],
            send_sem=self.send.at[4 + turn],
            recv_sem=self.recv.at[4 + turn],
            device_id={"wide": self.z * 2 + 1 - self.core},
            device_id_type=MESH,
        )

    def take(self, turn, shift):
        self.swap(turn, shift).wait_recv()
        to = wrap(self.z + shift)
        self.w[self.keep, to] += self.near_in[to]

    def copy(self, kind):
        ahead = (1, -1, 1, -1)[kind]
        shift = (1, -1, 2, 2)[kind]
        source = self.w.at[self.keep, wrap(self.z + shift)]
        landing = self.whole_in
        if kind >= 2:
            source = source.at[pl.ds((kind - 2) * self.half_rows, self.half_rows)]
            landing = self.half_in
        return pltpu.make_async_remote_copy(
            src_ref=source,
            dst_ref=landing.at[kind % 2],
            send_sem=self.send.at[kind],
            recv_sem=self.recv.at[kind],
            device_id={"wide": wrap(self.z + ahead) * 2 + self.core},
            device_id_type=MESH,
        )

    def begin(self):
        self.take(0, 2)
        for kind in (2, 3):
            self.copy(kind).start()

    def middle(self):
        for kind in (2, 3):
            shift = 1 if kind == 2 else -1
            self.take(kind - 1, shift)
            self.copy(kind).wait_recv()
            rows = pl.ds((kind - 2) * self.half_rows, self.half_rows)
            self.w[self.keep, wrap(self.z + shift), rows, :] += self.half_in[kind - 2]
            self.copy(kind - 2).start()
        self.take(3, 0)

    def finish(self):
        for kind in (0, 1):
            self.copy(kind).wait_recv()
        return self.w[self.keep, self.z] + self.whole_in[0] + self.whole_in[1]

    def drain(self):
        for kind in range(4):
            self.copy(kind).wait_send()
        for turn, shift in enumerate((2, 1, 3, 0)):
            self.swap(turn, shift).wait_send()


TURNS = (3, 2, 4, 1)


def shift_of(step):
    return 2 - step + 3 * (step // 2) - 2 * (step // 3)


def stream(count, loads, work):
    for copy in loads(0, 0):
        copy.start()

    def one(i, carry):
        slot = lax.rem(i, 2)

        @pl.when(i + 1 < count)
        def _():
            for copy in loads(i + 1, 1 - slot):
                copy.start()

        for copy in loads(i, slot):
            copy.wait()
        work(i, slot)
        return carry

    lax.fori_loop(0, count, one, 0)


def reduce_kernel(
    dq_ref,
    att_ref,
    inst_ref,
    dk_hbm,
    dv_hbm,
    hid_hbm,
    cot_hbm,
    nei_hbm,
    wq_hbm,
    wk_hbm,
    wv_hbm,
    gh_ref,
    came_ref,
    gq_ref,
    go_ref,
    gk_ref,
    gv_ref,
    dq_two,
    att_two,
    gpart,
    dpart,
    ghalf,
    gquarter,
    gacross,
    dhalf,
    dquarter,
    w_tile,
    tile,
    near_tile,
    dk_tile,
    dv_tile,
    wk,
    wv,
    going,
    mine,
    out_w,
    out_near,
    out_whole,
    out_half,
    in_w,
    in_near,
    in_whole,
    in_half,
    kv_w,
    kv_near,
    kv_whole,
    kv_half,
    gq_done,
    go_done,
    g_send,
    g_recv,
    d_send,
    d_recv,
    out_send,
    out_recv,
    in_send,
    in_recv,
    kv_send,
    kv_recv,
    pair_send,
    pair_recv,
    swap_send,
    swap_recv,
    load_sem,
    tile_sem,
    near_sem,
):
    place = Place()
    x, y = place.x, place.y
    width = dq_ref.shape[1]
    piece_rows = going.shape[2]
    groups, cap = going.shape[:2]
    rows, enc = dpart.shape[2:]
    weights = [
        pltpu.make_async_copy(wk_hbm, wk, load_sem.at[1]),
        pltpu.make_async_copy(wv_hbm, wv, load_sem.at[2]),
    ]
    for copy in weights:
        copy.start()
    right = pl.ds(width, width)
    halves = [
        partner_copy(place, dq_ref, dq_two.at[:, right], pair_send.at[0], pair_recv.at[0]),
        partner_copy(place, att_ref, att_two.at[:, right], pair_send.at[1], pair_recv.at[1]),
    ]
    greet(place, True)
    for copy in halves:
        copy.start()
    dq_two[:, :width] = dq_ref[...]
    att_two[:, :width] = att_ref[...]
    core = lax.rem(lax.axis_index("wide"), 2)
    keep = lax.rem(core + place.set, 2)
    wide_sum = SetReduce(place, gpart, ghalf, gquarter, gacross, g_send, g_recv)
    near_sum = Reduce(place, dpart, dhalf, dquarter, d_send, d_recv)
    out_ring = Ring(out_w, out_near, out_whole, out_half, out_send, out_recv, keep)
    in_ring = Ring(in_w, in_near, in_whole, in_half, in_send, in_recv, keep)
    kv_ring = Ring(kv_w, kv_near, kv_whole, kv_half, kv_send, kv_recv, core)

    def dot(a, b, ca, cb):
        return lax.dot_general(
            a, b, (((ca,), (cb,)), ((), ())), precision=MID, preferred_element_type=jnp.float32
        )

    def g_load(i, slot):
        block = wq_hbm.at[wrap(x + shift_of(i // 2)), lax.rem(i, 2)]
        return [pltpu.make_async_copy(block, w_tile.at[slot], tile_sem.at[slot])]

    def g_work(i, slot):
        shift = shift_of(i // 2)
        gpart[wrap(x + shift), lax.rem(i, 2)] = dot(dq_two[...], w_tile[slot], 1, 1)

        @pl.when(i == 1)
        def _():
            wide_sum.begin(1)
            wide_sum.begin(2)

        @pl.when(lax.rem(i, 2) == 1)
        def _():
            wide_sum.across(shift).start()

    def weight_grad(source, two_ref, ring):
        def load(i, slot):
            block = source.at[wrap(ring.z + shift_of(i // 2)), lax.rem(i, 2)]
            return [pltpu.make_async_copy(block, tile.at[slot], tile_sem.at[slot])]

        def work(i, slot):
            shift, u = shift_of(i // 2), lax.rem(i, 2)
            part = pl.ds(pl.multiple_of(u * width, width), width)
            both = dot(tile[slot], two_ref[...], 0, 0)
            ring.w[0, wrap(ring.z + shift), part, :] = both[:, :width]
            ring.w[1, wrap(ring.z + shift), part, :] = both[:, width:]

            @pl.when(u == 1)
            def _():
                ring.swap(i // 2, shift).start()

        stream(2 * SIDE, load, work)

    def handed(which, done, out_ref):
        return partner_copy(
            place, done, out_ref, pair_send.at[2 + which], pair_recv.at[2 + which], True
        )

    def deliver(which, ring, done, out_ref):
        done[...] = ring.finish()

        @pl.when(keep == 0)
        def _():
            out_ref[...] = done[...]

        @pl.when(keep == 1)
        def _():
            handed(which, done, out_ref).start()

    def delivered(which, done, out_ref):
        @pl.when(keep == 1)
        def _():
            handed(which, done, out_ref).wait()

    def near_load(sources):
        def load(i, slot):
            at = (i // 2, pl.ds(2 * lax.rem(i, 2), 2))
            return [
                pltpu.make_async_copy(source.at[at], buf.at[slot], near_sem.at[2 * which + slot])
                for which, (source, buf) in enumerate(sources)
            ]

        return load

    def d_work(i, slot):
        bx, by = i // 2, 2 * lax.rem(i, 2)
        dk = dk_tile[slot].reshape(2 * rows, width)
        dv = dv_tile[slot].reshape(2 * rows, width)
        dpart[bx, pl.ds(by, 2)] = (dot(dk, wk[...], 1, 1) + dot(dv, wv[...], 1, 1)).reshape(
            2, rows, enc
        )

    def neighbour_grad():
        for copy in weights:
            copy.wait()
        stream(2 * SIDE, near_load(((dk_hbm, dk_tile), (dv_hbm, dv_tile))), d_work)
        for turn in TURNS:
            for half in (0, 1):
                near_sum.begin(half, turn)

    def kv_work(i, slot):
        dk = dk_tile[slot].reshape(2 * rows, width)
        dv = dv_tile[slot].reshape(2 * rows, width)
        near = near_tile[slot].reshape(2 * rows, enc)
        pair = dot(near, jnp.concatenate([dk, dv], axis=1), 0, 0)
        for group in range(groups):
            share = pair[group * kv_w.shape[2] : (group + 1) * kv_w.shape[2]]
            kv_w[group % 2, group // 2] += share

    def kv_grad():
        kv_w[...] = jnp.zeros_like(kv_w)
        stream(
            2 * SIDE, near_load(((dk_hbm, dk_tile), (dv_hbm, dv_tile), (nei_hbm, near_tile))), kv_work
        )
        for turn, shift in enumerate((2, 1, 3, 0)):
            kv_ring.swap(turn, shift).start()

    def near_middle(turn):
        for half in (0, 1):
            near_sum.middle(half, turn)

    def near_finish(turn):
        for half in (0, 1):
            near_sum.finish(half, turn)
        if turn == 3:
            for half in (0, 1):
                near_sum.begin(half, 0)

    neighbour_grad()
    halves[0].wait()
    stream(2 * SIDE, g_load, g_work)
    weight_grad(hid_hbm, dq_two, in_ring)
    wide_sum.middle(1)
    wide_sum.take(2)
    wide_sum.begin(0)
    in_ring.begin()
    halves[1].wait()
    weight_grad(cot_hbm, att_two, out_ring)
    near_middle(3)
    near_middle(4)
    near_middle(2)
    out_ring.begin()
    in_ring.middle()
    kv_grad()
    near_finish(3)
    kv_ring.begin()
    wide_sum.middle(2)
    near_middle(1)
    out_ring.middle()
    near_finish(4)
    deliver(0, in_ring, gq_done, gq_ref)
    near_finish(2)
    near_middle(0)
    wide_sum.take(1)
    wide_sum.take(3)
    kv_ring.middle()
    wide_sum.finish(2)
    wide_sum.across(4).start()
    wide_sum.finish(1)
    near_finish(1)
    deliver(1, out_ring, go_done, go_ref)
    wide_sum.middle(0)
    near_finish(0)
    for i in range(groups * cap):
        mine[i] = dpart[x, y, pl.ds(i * piece_rows, piece_rows), :]
    for slot in range(groups * cap):
        going[slot // cap, slot % cap] = mine[inst_ref[slot]]
    swaps = exchange(going, came_ref, swap_send, swap_recv, load_sem.at[3])
    wide_sum.take(0)
    pair = kv_ring.finish()
    gk_ref[...] = pair[:, :width]
    gv_ref[...] = pair[:, width:]
    wide_sum.take(4)
    wide_sum.finish(0)
    gh_ref[...] = gpart[x, place.member]
    delivered(0, gq_done, gq_ref)
    delivered(1, go_done, go_ref)
    for copy in swaps:
        copy.wait()
    for target in (wide_sum, near_sum, out_ring, in_ring, kv_ring):
        target.drain()


def result_kernel(slot_ref, came_ref, *refs):
    sources, table_ref, results = refs[:5], refs[5], refs[6:]
    for source, result in zip(sources, results):
        result[...] = source[...]
    table_ref[...] = jnp.zeros_like(table_ref)
    cap = came_ref.shape[1]
    for i in range(came_ref.shape[0] * cap):
        slot = slot_ref[i]
        table_ref[slot] += came_ref[i // cap, i % cap]


def vmem(n):
    return [pl.BlockSpec(memory_space=pltpu.VMEM)] * n


def hbm(n):
    return [pl.BlockSpec(memory_space=pl.ANY)] * n


def smem(n):
    return [pl.BlockSpec(memory_space=pltpu.SMEM)] * n


def f32(*shape):
    return jax.ShapeDtypeStruct(shape, jnp.float32)


def gather_call(hidden, cotangent, table, picks, slots, wq, wo, wk, wv, groups):
    tokens, width = hidden.shape
    _, piece_rows, enc = table.shape
    going = (groups, slots.shape[0] // groups, piece_rows, enc)
    rows = slots.shape[0] * piece_rows
    dma = pltpu.SemaphoreType.DMA
    blocks = (SIDE, 2, tokens, width)
    pairs = (SIDE, 2, width, 2 * width)
    out_shape = [
        f32(*blocks),
        f32(*blocks),
        f32(SIDE, SIDE, rows, enc),
        f32(*pairs),
        f32(tokens, width),
        f32(tokens, width),
        f32(SIDE, SIDE, rows, width),
        f32(SIDE, SIDE, rows, width),
    ]
    scratch = [
        pltpu.VMEM((tokens, 2 * width), jnp.float32),
        pltpu.VMEM((tokens, 2 * width), jnp.float32),
        pltpu.VMEM((tokens, width), jnp.float32),
        pltpu.VMEM((tokens, width), jnp.float32),
        pltpu.VMEM((SIDE, SIDE, rows, width), jnp.float32),
        pltpu.VMEM((SIDE, SIDE, rows, width), jnp.float32),
        pltpu.VMEM(blocks, jnp.float32),
        pltpu.VMEM(blocks, jnp.float32),
        pltpu.VMEM((SIDE, SIDE, rows, enc), jnp.float32),
        pltpu.VMEM(pairs, jnp.float32),
        pltpu.VMEM(pairs, jnp.float32),
        pltpu.VMEM((enc, 2 * width), jnp.float32),
        pltpu.VMEM(going, jnp.float32),
        pltpu.VMEM(going, jnp.float32),
    ]
    scratch += [dma((17,))] * 4 + [dma((40,))] * 2 + [dma((8,))] * 4 + [dma((4,))] * 2
    scratch += [dma((groups,))] * 2 + [dma((8,)), dma((12,))]
    return pl.pallas_call(
        gather_kernel,
        out_shape=out_shape,
        in_specs=hbm(2) + vmem(1) + smem(2) + hbm(4),
        out_specs=hbm(4) + vmem(4),
        scratch_shapes=scratch,
        compiler_params=pltpu.CompilerParams(
            collective_id=0, has_side_effects=True, vmem_limit_bytes=VMEM_LIMIT
        ),
        cost_estimate=pl.CostEstimate(flops=24_000_000_000, bytes_accessed=60_000_000, transcendentals=0),
    )(hidden, cotangent, table, picks, slots, wq, wo, wk, wv)


def reduce_call(dq, att, inst_of, dk, dv, hid, cot, nei, wq, wk, wv, groups):
    tokens, width = dq.shape
    rows = dk.shape[2]
    enc = wk.shape[0]
    slots = inst_of.shape[0]
    cap = slots // groups
    piece_rows = rows // slots
    dma = pltpu.SemaphoreType.DMA
    going = (groups, cap, piece_rows, enc)
    out_rows, enc_rows = 2 * width, enc // groups

    def ring(rows, cols):
        return [
            pltpu.VMEM((*n, r, cols), jnp.float32)
            for n, r in (((2, SIDE), rows), ((SIDE,), rows), ((2,), rows), ((2,), rows // 2))
        ]

    scratch = [
        pltpu.VMEM((tokens, 2 * width), jnp.float32),
        pltpu.VMEM((tokens, 2 * width), jnp.float32),
        pltpu.VMEM((SIDE, 2, tokens, width), jnp.float32),
        pltpu.VMEM((SIDE, SIDE, rows, enc), jnp.float32),
        pltpu.VMEM((6, tokens // 2, width), jnp.float32),
        pltpu.VMEM((6, tokens // 4, width), jnp.float32),
        pltpu.VMEM((5, tokens // 2, width), jnp.float32),
        pltpu.VMEM((20, rows // 2, enc), jnp.float32),
        pltpu.VMEM((20, rows // 4, enc), jnp.float32),
        pltpu.VMEM((2, width, 2 * width), jnp.float32),
        pltpu.VMEM((2, tokens, width), jnp.float32),
        pltpu.VMEM((2, 2, rows, enc), jnp.float32),
        pltpu.VMEM((2, 2, rows, width), jnp.float32),
        pltpu.VMEM((2, 2, rows, width), jnp.float32),
        pltpu.VMEM(wk.shape, jnp.float32),
        pltpu.VMEM(wv.shape, jnp.float32),
        pltpu.VMEM(going, jnp.float32),
        pltpu.VMEM((slots, piece_rows, enc), jnp.float32),
    ]
    scratch += ring(out_rows, width) + ring(out_rows, width) + ring(enc_rows, 2 * width)
    scratch += [pltpu.VMEM((out_rows, width), jnp.float32)] * 2
    scratch += [dma((17,))] * 2 + [dma((40,))] * 2 + [dma((8,))] * 6 + [dma((4,))] * 2
    scratch += [dma((groups,))] * 2 + [dma((4,)), dma((2,)), dma((6,))]
    return pl.pallas_call(
        reduce_kernel,
        out_shape=[
            f32(tokens, width),
            f32(*going),
            f32(out_rows, width),
            f32(out_rows, width),
            f32(enc_rows, width),
            f32(enc_rows, width),
        ],
        in_specs=vmem(2) + smem(1) + hbm(8),
        out_specs=vmem(6),
        scratch_shapes=scratch,
        compiler_params=pltpu.CompilerParams(
            collective_id=1, has_side_effects=True, vmem_limit_bytes=REDUCE_LIMIT
        ),
        cost_estimate=pl.CostEstimate(flops=50_000_000_000, bytes_accessed=60_000_000, transcendentals=0),
    )(dq, att, inst_of, dk, dv, hid, cot, nei, wq, wk, wv)


def body(
    hidden_states, out_cotangent, enc_table, nbr_ids, owner_map, w_query, w_key, w_value, w_out
):
    groups = lax.axis_size("wide")
    group = lax.axis_index("wide")
    stored = enc_table.shape[0]
    table_size = owner_map.shape[0]
    tokens, width = hidden_states.shape
    inst = NEIGH * (tokens // SPAN)
    capacity = inst // groups
    match = nbr_ids[:, :, None] == jnp.arange(table_size, dtype=jnp.int32)[None, None, :]
    slots = jnp.sum(jnp.where(match, owner_map[None, None, :], 0), axis=-1)
    slots = slots.reshape(groups, inst)
    owners = slots // stored
    local_slot = slots - owners * stored
    earlier = jnp.arange(inst)[None, :] < jnp.arange(inst)[:, None]
    same = owners[:, :, None] == owners[:, None, :]
    rank = jnp.sum((same & earlier[None, :, :]).astype(jnp.int32), axis=-1)
    slot_range = jnp.arange(capacity, dtype=jnp.int32)
    pick = (owners[:, None, :] == group) & (rank[:, None, :] == slot_range[None, :, None])
    picks = jnp.sum(jnp.where(pick, local_slot[:, None, :], 0), axis=-1).reshape(-1)
    mine = lax.dynamic_index_in_dim(owners * capacity + rank, group, 0, keepdims=False)
    numbers = jnp.arange(inst, dtype=jnp.int32)
    inst_of = jnp.sum(jnp.where(mine[None, :] == numbers[:, None], numbers[None, :], 0), axis=1)

    query_blocks = w_query.reshape(SIDE, SIDE, width, width)
    out_blocks = w_out.reshape(SIDE, SIDE, width, width)
    hid, cot, nei, query_pair, attended, d_query, d_keys, d_values = gather_call(
        hidden_states, out_cotangent, enc_table, picks, mine, query_blocks, out_blocks, w_key,
        w_value, groups,
    )
    grad_hidden, arrived, grad_query, grad_out, grad_key, grad_value = reduce_call(
        d_query, attended, inst_of, d_keys, d_values, hid, cot, nei, query_pair, w_key, w_value,
        groups,
    )
    sums = (grad_hidden, grad_query, grad_key, grad_value, grad_out)
    grad_table, *sums = pl.pallas_call(
        result_kernel,
        out_shape=[f32(*enc_table.shape)] + [f32(*t.shape) for t in sums],
        in_specs=smem(1) + vmem(6),
        out_specs=vmem(6),
    )(picks, arrived, *sums)
    return (*sums, grad_table)


def solution(mesh):
    placed = (
        P("wide", "narrow"),
        P("wide", "narrow"),
        P("wide", "narrow", None),
        P(),
        P(),
        P(None, "narrow"),
        P(None, "narrow"),
        P(None, "narrow"),
        P(None, "narrow"),
    )
    return jax.shard_map(
        body,
        mesh=mesh,
        in_specs=placed,
        out_specs=(
            P("wide", "narrow"),
            P("wide", "narrow"),
            P("wide", "narrow"),
            P("wide", "narrow"),
            P("wide", "narrow"),
            P("wide", "narrow", None),
        ),
        check_vma=False,
    )
```

```python
import functools

import jax
import jax.numpy as jnp
from jax import lax
from jax.experimental import pallas as pl
from jax.experimental.pallas import tpu as pltpu
from jax.sharding import PartitionSpec as P

HEAD_DIM = 128
SPAN = 64
NEIGH = 2
SIDE = 4
VMEM_LIMIT = 60 * 1024 * 1024
REDUCE_LIMIT = 63 * 1024 * 1024

HIGH = lax.Precision.HIGHEST
MID = lax.Precision.HIGH
MESH = pl.DeviceIdType.MESH


def wrap(value):
    return lax.rem(value + 2 * SIDE, SIDE)


class Place:
    def __init__(self):
        me = lax.axis_index("narrow")
        self.x = me // SIDE
        self.y = lax.rem(me, SIDE)
        self.set = self.y // 2
        self.member = lax.rem(self.y, 2)

    def at(self, dx, dy):
        return {"narrow": wrap(self.x + dx) * SIDE + wrap(self.y + dy)}

    def mate(self):
        return {"narrow": self.x * SIDE + self.y + 1 - 2 * self.member}

    def partner(self):
        return {"narrow": self.x * SIDE + SIDE - 1 - self.y}

    def own(self, half):
        return (self.x, self.y) if half == 0 else (self.y, self.x)

    @staticmethod
    def block(half, first, second):
        return (first, second) if half == 0 else (second, first)

    def device(self, half, first, second):
        bx, by = self.block(half, first, second)
        return {"narrow": bx * SIDE + by}

    def line(self, half, turn, shift):
        first, second = self.own(half)
        if isinstance(turn, int) and turn == 0:
            return wrap(first + shift), second
        return first, wrap(second + shift)


class SetGather:
    def __init__(self, place, buf, send, recv):
        self.place, self.buf, self.send, self.recv = place, buf, send, recv
        self.rows = buf.shape[2] // 2

    def copy(self, slot, bx, member, start, rows, device):
        piece = self.buf.at[bx, member, pl.ds(start, rows)]
        return pltpu.make_async_remote_copy(
            src_ref=piece,
            dst_ref=piece,
            send_sem=self.send.at[slot],
            recv_sem=self.recv.at[slot],
            device_id=device,
            device_id_type=MESH,
        )

    def ring(self, which, kind, arriving=False):
        place = self.place
        member = place.member if which < 2 else 1 - place.member
        ahead = (1, -1, 1, -1)[kind]
        shift = (0, 0, -1, 1)[kind] - (ahead if arriving else 0)
        start = self.rows * (which > 0) + (self.rows // 2 if kind == 3 else 0)
        rows = self.rows if kind < 2 else self.rows // 2
        return self.copy(
            which * 4 + kind, wrap(place.x + shift), member, start, rows, place.at(ahead, 0)
        )

    def across(self, turn, arriving=False):
        place = self.place
        member = 1 - place.member if arriving else place.member
        bx = wrap(place.x + turn)
        start = self.rows if turn == 4 else 0
        return self.copy(12 + turn, bx, member, start, self.rows, place.mate())

    def begin(self, which):
        for kind in (0, 1):
            self.ring(which, kind).start()

    def forward(self, which):
        for kind in (0, 1):
            self.ring(which, kind, True).wait_recv()
            self.ring(which, kind + 2).start()

    def finish(self, which):
        for kind in (2, 3):
            self.ring(which, kind, True).wait_recv()

    def drain(self):
        for which in range(3):
            for kind in range(4):
                self.ring(which, kind).wait_send()
        for turn in range(5):
            self.across(turn).wait_send()


class SetReduce:
    def __init__(self, place, part, whole_in, quarter_in, across_in, send, recv):
        self.place, self.part = place, part
        self.whole_in, self.quarter_in, self.across_in = whole_in, quarter_in, across_in
        self.send, self.recv = send, recv
        self.rows = part.shape[2] // 2

    def ring(self, which, kind):
        place = self.place
        member = place.member if which < 2 else 1 - place.member
        ahead = (1, -1, 1, -1)[kind]
        shift = (1, -1, 2, 2)[kind]
        start = self.rows * (which > 0) + (self.rows // 2 if kind == 3 else 0)
        rows = self.rows if kind < 2 else self.rows // 2
        landing = self.whole_in if kind < 2 else self.quarter_in
        slot = which * 4 + kind
        return pltpu.make_async_remote_copy(
            src_ref=self.part.at[wrap(place.x + shift), member, pl.ds(start, rows)],
            dst_ref=landing.at[which * 2 + kind % 2],
            send_sem=self.send.at[slot],
            recv_sem=self.recv.at[slot],
            device_id=place.at(ahead, 0),
            device_id_type=MESH,
        )

    def across(self, turn):
        place = self.place
        start = self.rows if isinstance(turn, int) and turn == 4 else 0
        return pltpu.make_async_remote_copy(
            src_ref=self.part.at[
                wrap(place.x + turn), 1 - place.member, pl.ds(start, self.rows)
            ],
            dst_ref=self.across_in.at[turn],
            send_sem=self.send.at[12 + turn],
            recv_sem=self.recv.at[12 + turn],
            device_id=place.mate(),
            device_id_type=MESH,
        )

    def take(self, turn):
        self.across(turn).wait_recv()
        rows = pl.ds(self.rows if turn == 4 else 0, self.rows)
        self.part[wrap(self.place.x + turn), self.place.member, rows, :] += self.across_in[turn]

    def begin(self, which):
        for kind in (2, 3):
            self.ring(which, kind).start()

    def middle(self, which):
        member = self.place.member if which < 2 else 1 - self.place.member
        for kind in (2, 3):
            self.ring(which, kind).wait_recv()
            start = self.rows * (which > 0) + (self.rows // 2 if kind == 3 else 0)
            bx = wrap(self.place.x + (1 if kind == 2 else -1))
            self.part[bx, member, pl.ds(start, self.rows // 2), :] += self.quarter_in[
                which * 2 + kind % 2
            ]
            self.ring(which, kind - 2).start()

    def finish(self, which):
        member = self.place.member if which < 2 else 1 - self.place.member
        for kind in (0, 1):
            self.ring(which, kind).wait_recv()
        rows = pl.ds(self.rows * (which > 0), self.rows)
        self.part[self.place.x, member, rows, :] += (
            self.whole_in[which * 2] + self.whole_in[which * 2 + 1]
        )

    def drain(self):
        for which in range(3):
            for kind in range(4):
                self.ring(which, kind).wait_send()
        for turn in range(5):
            self.across(turn).wait_send()


def partner_copy(place, src, dst, send, recv, other_core=False):
    device = place.partner()
    if other_core:
        group = lax.axis_index("wide")
        device = {"wide": group + 1 - 2 * lax.rem(group, 2), **device}
    return pltpu.make_async_remote_copy(
        src_ref=src,
        dst_ref=dst,
        send_sem=send,
        recv_sem=recv,
        device_id=device,
        device_id_type=MESH,
    )


def greet(place, diagonal=False):
    groups = lax.axis_size("wide")
    group = lax.axis_index("wide")
    barrier = pltpu.get_barrier_semaphore()
    for half in (0, 1):
        for shift in (1, -1):
            pl.semaphore_signal(
                barrier,
                inc=1,
                device_id=place.device(half, *place.line(half, 0, shift)),
                device_id_type=MESH,
            )
    for step in range(1, groups):
        pl.semaphore_signal(
            barrier,
            inc=1,
            device_id={"wide": lax.rem(group + step, groups)},
            device_id_type=MESH,
        )
    if diagonal:
        pl.semaphore_signal(
            barrier,
            inc=1,
            device_id={"wide": group + 1 - 2 * lax.rem(group, 2), **place.partner()},
            device_id_type=MESH,
        )
    pl.semaphore_wait(barrier, 4 + groups - 1 + int(diagonal))


def exchange(out_ref, in_ref, send, recv, local):
    groups = lax.axis_size("wide")
    group = lax.axis_index("wide")
    copies = []
    for step in range(1, groups):
        peer = lax.rem(group + step, groups)
        copy = pltpu.make_async_remote_copy(
            src_ref=out_ref.at[peer],
            dst_ref=in_ref.at[group],
            send_sem=send.at[step],
            recv_sem=recv.at[step],
            device_id={"wide": peer},
            device_id_type=MESH,
        )
        copy.start()
        copies.append(copy)
    mine = pltpu.make_async_copy(out_ref.at[group], in_ref.at[group], local)
    mine.start()
    copies.append(mine)
    return copies


class Gather:
    def __init__(self, place, buf, send, recv):
        self.place, self.buf, self.send, self.recv = place, buf, send, recv
        self.rows = buf.shape[2]

    def copy(self, half, turn, kind, block, dest):
        rows = self.rows // 2 if kind < 2 else self.rows // 4
        start = half * (self.rows // 2) + (self.rows // 4 if kind == 3 else 0)
        bx, by = self.place.block(half, *block)
        piece = self.buf.at[bx, by, pl.ds(start, rows)]
        slot = (half * 5 + turn) * 4 + kind
        return pltpu.make_async_remote_copy(
            src_ref=piece,
            dst_ref=piece,
            send_sem=self.send.at[slot],
            recv_sem=self.recv.at[slot],
            device_id=self.place.device(half, *dest),
            device_id_type=MESH,
        )

    def at(self, half, turn, shift):
        first, second = self.place.own(half)
        if isinstance(turn, int) and turn == 0:
            return wrap(first + shift), second
        return wrap(first + turn - 1), wrap(second + shift)

    def describe(self, half, turn, kind):
        shift = (0, 0, -1, 1)[kind]
        ahead = (1, -1, 1, -1)[kind]
        return self.copy(
            half, turn, kind, self.at(half, turn, shift), self.place.line(half, turn, ahead)
        )

    def arrival(self, half, turn, kind):
        shift = (-1, 1, 2, 2)[kind]
        ahead = (1, -1, 1, -1)[kind]
        return self.copy(
            half, turn, kind, self.at(half, turn, shift), self.place.line(half, turn, ahead)
        )

    def begin(self, half, turn):
        self.describe(half, turn, 0).start()
        self.describe(half, turn, 1).start()

    def forward(self, half, turn):
        for kind in (0, 1):
            self.arrival(half, turn, kind).wait_recv()
            self.describe(half, turn, kind + 2).start()

    def finish(self, half, turn):
        for kind in (2, 3):
            self.arrival(half, turn, kind).wait_recv()

    def drain(self):
        for half in (0, 1):
            for turn in range(5):
                for kind in range(4):
                    self.describe(half, turn, kind).wait_send()


def attend(half, q_ref, da_ref, keys_ref, values_ref, att_ref, dq_ref, dk_ref, dv_ref):
    scale = HEAD_DIM ** (-0.5)
    heads = q_ref.shape[1] // HEAD_DIM
    spans = q_ref.shape[0] // SPAN
    few = keys_ref.shape[2] // spans
    near = SIDE * SIDE * few

    def dot(a, b, ca, cb, precision=MID):
        return lax.dot_general(
            a, b, (((ca,), (cb,)), ((), ())), precision=precision,
            preferred_element_type=jnp.float32,
        )

    def span(c, carry):
        rows = pl.ds(pl.multiple_of(c * SPAN, SPAN), SPAN)
        pieces = pl.ds(pl.multiple_of(c * few, few), few)
        for head in range(heads):
            cols = pl.ds(head * HEAD_DIM, HEAD_DIM)
            q = q_ref[rows, cols]
            da = da_ref[rows, cols]
            k = keys_ref[:, :, pieces, cols].reshape(near, HEAD_DIM)
            v = values_ref[:, :, pieces, cols].reshape(near, HEAD_DIM)
            scores = dot(q, k, 1, 1, HIGH) * scale
            dp = dot(da, v, 1, 1)
            top = jnp.max(scores, axis=-1, keepdims=True)
            e = jnp.exp(scores - top)
            probs = e / jnp.sum(e, axis=-1, keepdims=True)
            ds = probs * (dp - jnp.sum(dp * probs, axis=-1, keepdims=True)) * scale
            att_ref[rows, cols] = dot(probs, v, 1, 0)
            dq_ref[rows, cols] = dot(ds, k, 1, 0)
            shape = (SIDE, SIDE, few, HEAD_DIM)
            dk_ref[:, :, pieces, cols] = dot(ds, q, 0, 0).reshape(shape)
            dv_ref[:, :, pieces, cols] = dot(probs, da, 0, 0).reshape(shape)
        return carry

    lax.fori_loop(half * spans // 2, (half + 1) * spans // 2, span, 0)


class Spread:
    def __init__(self, place, source, wide_w, send, recv):
        self.place, self.source, self.w = place, source, wide_w
        self.send, self.recv = send, recv
        self.group = lax.axis_index("wide")
        self.z, self.core = self.group // 2, lax.rem(self.group, 2)
        self.width = source.shape[3]

    def slot(self, group):
        return self.w.at[group // 2, lax.rem(group, 2), :, pl.ds(self.width, self.width)]

    def first(self):
        block = self.source.at[self.z, 2 * (1 - self.place.set) + self.core]
        return partner_copy(
            self.place, block, self.slot(self.group), self.send.at[0], self.recv.at[0]
        )

    def to(self, index, group, target):
        return pltpu.make_async_remote_copy(
            src_ref=self.slot(group),
            dst_ref=self.slot(group),
            send_sem=self.send.at[index],
            recv_sem=self.recv.at[index],
            device_id={"wide": target},
            device_id_type=MESH,
        )

    def along(self, step, arriving=False):
        there = wrap(self.z + step) * 2 + self.core
        back = wrap(self.z - step) * 2 + self.core
        return self.to(step, back if arriving else self.group, there)

    def beside(self, step, arriving=False):
        core = 1 - self.core if arriving else self.core
        other = self.z * 2 + 1 - self.core
        return self.to(4 + step, wrap(self.z - step) * 2 + core, other)

    def spread(self):
        self.first().wait_recv()
        for step in (1, 3, 2):
            self.along(step).start()
        self.beside(0).start()

    def pass_on(self):
        for step in (1, 3, 2):
            self.along(step, True).wait_recv()
            self.beside(step).start()

    def finish(self):
        for step in range(SIDE):
            self.beside(step, True).wait_recv()

    def drain(self):
        self.first().wait_send()
        for step in (1, 2, 3):
            self.along(step).wait_send()
        for step in range(SIDE):
            self.beside(step).wait_send()


def gather_kernel(
    hid_ref,
    cot_ref,
    table_ref,
    nbr_ref,
    map_ref,
    wq_ref,
    wo_ref,
    wk_ref,
    wv_ref,
    hid_out,
    cot_out,
    nei_out,
    wq_out,
    pick_ref,
    slot_ref,
    inst_ref,
    att_ref,
    dq_ref,
    dk_ref,
    dv_ref,
    q_two,
    da_two,
    q_came,
    da_came,
    keys_ref,
    values_ref,
    hid,
    cot,
    nei,
    wq,
    wo,
    wkv,
    going,
    came,
    hid_send,
    hid_recv,
    cot_send,
    cot_recv,
    nei_send,
    nei_recv,
    wq_send,
    wq_recv,
    wo_send,
    wo_recv,
    pair_send,
    pair_recv,
    swap_send,
    swap_recv,
    load_sem,
    store_sem,
):
    place = Place()
    x, y = place.x, place.y
    tokens, width = dq_ref.shape
    groups, cap, piece_rows, _ = came.shape
    inst = nei.shape[2] // piece_rows
    own = [
        pltpu.make_async_copy(hid_ref, hid.at[x, place.member], load_sem.at[0]),
        pltpu.make_async_copy(cot_ref, cot.at[x, place.member], load_sem.at[1]),
    ]
    mine = pl.ds(2 * place.set, 2)
    left = pl.ds(0, width)
    weights = [
        pltpu.make_async_copy(wq_ref.at[:, mine], wq.at[:, :, :, left], load_sem.at[2]),
        pltpu.make_async_copy(wo_ref.at[:, mine], wo.at[:, :, :, left], load_sem.at[3]),
        pltpu.make_async_copy(wk_ref, wkv.at[:, pl.ds(0, width)], load_sem.at[4]),
        pltpu.make_async_copy(wv_ref, wkv.at[:, pl.ds(width, width)], load_sem.at[5]),
    ]
    for copy in own:
        copy.start()
    greet(place)
    for copy in own:
        copy.wait()
    pair = [
        SetGather(place, hid, hid_send, hid_recv),
        SetGather(place, cot, cot_send, cot_recv),
    ]
    near = Gather(place, nei, nei_send, nei_recv)
    spreads = [
        Spread(place, wq_ref, wq, wq_send, wq_recv),
        Spread(place, wo_ref, wo, wo_send, wo_recv),
    ]
    hid_set, cot_set = pair

    group = lax.axis_index("wide")
    stored = table_ref.shape[0]

    def stored_at(g, i):
        return map_ref[nbr_ref[g * (inst // NEIGH) + i // NEIGH, i % NEIGH]]

    def offer():
        def one(g, carry):
            count = jnp.int32(0)
            chosen = [jnp.int32(0)] * cap
            for i in range(inst):
                at = stored_at(g, i) - group * stored
                hit = (at >= 0) & (at < stored)
                chosen = [
                    jnp.where(hit & (count == r), at, old) for r, old in enumerate(chosen)
                ]
                count = count + hit.astype(jnp.int32)
            for r in range(cap):
                pick_ref[g * cap + r] = chosen[r]
                going[g, r] = table_ref[chosen[r]]
            return carry

        lax.fori_loop(0, groups, one, 0)
        return exchange(going, came, swap_send, swap_recv, load_sem.at[6])

    def places():
        owners = [lax.div(stored_at(group, i), stored) for i in range(inst)]
        slots = [
            owner * cap + sum((owners[j] == owner).astype(jnp.int32) for j in range(i))
            for i, owner in enumerate(owners)
        ]
        for i in range(inst):
            slot_ref[i] = slots[i]

        def one(slot, carry):
            inst_ref[slot] = sum(jnp.where(slot_ref[i] == slot, i, 0) for i in range(inst))
            return carry

        lax.fori_loop(0, inst, one, 0)

    def accept(swaps):
        for copy in swaps:
            copy.wait()
        for i in range(inst):
            slot = slot_ref[i]
            nei[x, y, pl.ds(i * piece_rows, piece_rows), :] = came[
                slot // cap, lax.rem(slot, cap)
            ]

    def set_forward(gather):
        gather.forward(0)
        gather.across(1).start()
        gather.across(3).start()

    def set_other(gather):
        gather.across(4, True).wait_recv()
        gather.begin(2)

    def set_finish(gather):
        gather.finish(0)
        gather.across(2).start()

    def add_products(gather, half, bx):
        rows = pl.ds(half * (tokens // 2), tokens // 2)
        total, weight, precision = (
            (q_two, wq, HIGH) if gather is hid_set else (da_two, wo, MID)
        )

        def column(member, carry):
            total[rows, :] += jnp.dot(
                gather.buf[bx, member, rows, :], weight[bx, member], precision=precision,
                preferred_element_type=jnp.float32,
            )
            return carry

        lax.fori_loop(0, 2, column, 0)

    def project(gather, half):
        if half == 0:
            for turn in (0, 1, 3, 2):
                gather.across(turn, True).wait_recv()
                add_products(gather, 0, wrap(x + turn))
            return
        gather.finish(1)
        gather.finish(2)

        def block(bx, carry):
            add_products(gather, 1, bx)
            return carry

        lax.fori_loop(0, SIDE, block, 0)

    def half_copy(gather, half):
        rows = pl.ds(half * (tokens // 2), tokens // 2)
        total, came_ref = (q_two, q_came) if gather is hid_set else (da_two, da_came)
        sem = half + 2 * int(gather is cot_set)
        return partner_copy(
            place,
            total.at[rows, pl.ds(width, width)],
            came_ref.at[rows],
            pair_send.at[sem],
            pair_recv.at[sem],
        )

    def add_half(gather, half):
        half_copy(gather, half).wait_recv()
        rows = pl.ds(half * (tokens // 2), tokens // 2)
        total, came_ref = (q_two, q_came) if gather is hid_set else (da_two, da_came)
        came_ref[rows, :] += total[rows, :width]

    def near_keep(half, turn):
        first = wrap(place.own(half)[0] + turn - 1)
        rows = pl.ds(half * (nei.shape[2] // 2), nei.shape[2] // 2)
        at = (first, slice(None), rows) if half == 0 else (slice(None), first, rows)
        return pltpu.make_async_copy(nei.at[at], nei_out.at[at], store_sem.at[2 + half * 5 + turn])

    def near_project(half, turn):
        near.finish(half, turn)
        near_keep(half, turn).start()
        first = wrap(place.own(half)[0] + turn - 1)
        few = nei.shape[2] // 2
        rows = pl.ds(half * few, few)
        if half == 0:
            blocks = nei[first, :, rows, :]
        else:
            blocks = nei[:, first, rows, :]
        both = jnp.dot(
            blocks.reshape(SIDE * few, nei.shape[3]), wkv[...], precision=HIGH,
            preferred_element_type=jnp.float32,
        ).reshape(SIDE, few, 2 * width)
        if half == 0:
            keys_ref[first, :, rows, :] = both[:, :, :width]
            values_ref[first, :, rows, :] = both[:, :, width:]
        else:
            keys_ref[:, first, rows, :] = both[:, :, :width]
            values_ref[:, first, rows, :] = both[:, :, width:]

    def near_begin(turn):
        for half in (0, 1):
            near.begin(half, turn)

    attended = (q_came, da_came, keys_ref, values_ref, att_ref, dq_ref, dk_ref, dv_ref)

    hid_set.begin(1)
    hid_set.across(4).start()
    cot_set.begin(1)
    for spread in spreads:
        spread.first().start()
    cot_set.begin(0)
    swaps = offer()
    places()
    cot_set.across(0).start()
    cot_set.across(4).start()
    for copy in weights:
        copy.start()
    q_two[...] = jnp.zeros_like(q_two)
    da_two[...] = jnp.zeros_like(da_two)
    for spread in spreads:
        spread.spread()
    set_other(hid_set)
    accept(swaps)
    near_begin(1)
    set_forward(cot_set)
    near_begin(0)
    for spread in spreads:
        spread.pass_on()
    set_other(cot_set)
    near.forward(0, 1)
    hid_set.begin(0)
    set_finish(cot_set)
    cot_set.forward(1)
    cot_set.forward(2)
    for half in (0, 1):
        near.forward(half, 0)
    near_begin(2)
    near_begin(4)
    for copy in weights:
        copy.wait()
    for spread in spreads:
        spread.finish()
    keep_weights = pltpu.make_async_copy(wq, wq_out, load_sem.at[7])
    keep_weights.start()
    near.forward(0, 2)
    hid_set.across(0).start()
    project(cot_set, 1)
    half_copy(cot_set, 1).start()
    set_forward(hid_set)
    near_project(0, 2)
    hid_set.forward(2)
    project(cot_set, 0)
    near_project(0, 1)
    set_finish(hid_set)
    hid_set.forward(1)
    near.forward(1, 2)
    for half in (0, 1):
        near.finish(half, 0)
    near_begin(3)
    half_copy(cot_set, 0).start()
    keep_cot = pltpu.make_async_copy(cot, cot_out, store_sem.at[1])
    keep_cot.start()
    project(hid_set, 1)
    near.forward(1, 1)
    add_half(cot_set, 1)
    half_copy(hid_set, 1).start()
    near_project(1, 2)
    near.forward(1, 4)
    near.forward(0, 4)
    near.forward(1, 3)
    project(hid_set, 0)
    half_copy(hid_set, 0).start()
    keep_hid = pltpu.make_async_copy(hid, hid_out, store_sem.at[0])
    keep_hid.start()
    near_project(1, 1)
    near_project(1, 4)
    near_project(1, 3)
    near.forward(0, 3)
    add_half(hid_set, 1)
    attend(1, *attended)
    add_half(cot_set, 0)
    near_project(0, 4)
    near_project(0, 3)
    add_half(hid_set, 0)
    attend(0, *attended)
    for target in (*pair, near, *spreads):
        target.drain()
    for gather in pair:
        for half in (0, 1):
            half_copy(gather, half).wait_send()
    for copy in (keep_weights, keep_hid, keep_cot):
        copy.wait()
    for half in (0, 1):
        for turn in range(1, SIDE + 1):
            near_keep(half, turn).wait()


class Reduce:
    def __init__(self, place, part, whole_in, quarter_in, send, recv):
        self.place, self.part = place, part
        self.whole_in, self.quarter_in = whole_in, quarter_in
        self.send, self.recv = send, recv
        self.rows = part.shape[2]

    def at(self, half, turn, shift):
        first, second = self.place.own(half)
        if isinstance(turn, int) and turn == 0:
            return wrap(first + shift), second
        return wrap(first + turn - 1), wrap(second + shift)

    def piece(self, half, block, kind):
        rows = self.rows // 2 if kind < 2 else self.rows // 4
        start = half * (self.rows // 2) + (self.rows // 4 if kind == 3 else 0)
        bx, by = self.place.block(half, *block)
        return bx, by, pl.ds(start, rows)

    def copy(self, half, turn, kind):
        ahead = (1, -1, 1, -1)[kind]
        shift = (1, -1, 2, 2)[kind]
        slot = (half * 5 + turn) * 2 + kind % 2
        landing = (self.whole_in if kind < 2 else self.quarter_in).at[slot]
        bx, by, rows = self.piece(half, self.at(half, turn, shift), kind)
        sem = (half * 5 + turn) * 4 + kind
        return pltpu.make_async_remote_copy(
            src_ref=self.part.at[bx, by, rows],
            dst_ref=landing,
            send_sem=self.send.at[sem],
            recv_sem=self.recv.at[sem],
            device_id=self.place.device(half, *self.place.line(half, turn, ahead)),
            device_id_type=MESH,
        )

    def begin(self, half, turn):
        for kind in (2, 3):
            self.copy(half, turn, kind).start()

    def middle(self, half, turn):
        for kind in (2, 3):
            self.copy(half, turn, kind).wait_recv()
            slot = (half * 5 + turn) * 2 + kind % 2
            shift = 1 if kind == 2 else -1
            bx, by, rows = self.piece(half, self.at(half, turn, shift), kind)
            self.part[bx, by, rows, :] += self.quarter_in[slot]
            self.copy(half, turn, kind - 2).start()

    def finish(self, half, turn):
        for kind in (0, 1):
            self.copy(half, turn, kind).wait_recv()
        slot = (half * 5 + turn) * 2
        bx, by, rows = self.piece(half, self.at(half, turn, 0), 0)
        self.part[bx, by, rows, :] += self.whole_in[slot] + self.whole_in[slot + 1]

    def drain(self):
        for half in (0, 1):
            for turn in range(5):
                for kind in range(4):
                    self.copy(half, turn, kind).wait_send()


class Ring:
    def __init__(self, w, near_in, whole_in, half_in, send, recv, keep):
        group = lax.axis_index("wide")
        self.z, self.core, self.keep = group // 2, lax.rem(group, 2), keep
        self.w, self.near_in, self.whole_in, self.half_in = w, near_in, whole_in, half_in
        self.send, self.recv = send, recv
        self.half_rows = w.shape[2] // 2

    def swap(self, turn, shift):
        to = wrap(self.z + shift)
        return pltpu.make_async_remote_copy(
            src_ref=self.w.at[1 - self.keep, to],
            dst_ref=self.near_in.at[to],
            send_sem=self.send.at[4 + turn],
            recv_sem=self.recv.at[4 + turn],
            device_id={"wide": self.z * 2 + 1 - self.core},
            device_id_type=MESH,
        )

    def take(self, turn, shift):
        self.swap(turn, shift).wait_recv()
        to = wrap(self.z + shift)
        self.w[self.keep, to] += self.near_in[to]

    def copy(self, kind):
        ahead = (1, -1, 1, -1)[kind]
        shift = (1, -1, 2, 2)[kind]
        source = self.w.at[self.keep, wrap(self.z + shift)]
        landing = self.whole_in
        if kind >= 2:
            source = source.at[pl.ds((kind - 2) * self.half_rows, self.half_rows)]
            landing = self.half_in
        return pltpu.make_async_remote_copy(
            src_ref=source,
            dst_ref=landing.at[kind % 2],
            send_sem=self.send.at[kind],
            recv_sem=self.recv.at[kind],
            device_id={"wide": wrap(self.z + ahead) * 2 + self.core},
            device_id_type=MESH,
        )

    def begin(self):
        self.take(0, 2)
        for kind in (2, 3):
            self.copy(kind).start()

    def middle(self):
        for kind in (2, 3):
            shift = 1 if kind == 2 else -1
            self.take(kind - 1, shift)
            self.copy(kind).wait_recv()
            rows = pl.ds((kind - 2) * self.half_rows, self.half_rows)
            self.w[self.keep, wrap(self.z + shift), rows, :] += self.half_in[kind - 2]
            self.copy(kind - 2).start()
        self.take(3, 0)

    def finish(self):
        for kind in (0, 1):
            self.copy(kind).wait_recv()
        return self.w[self.keep, self.z] + self.whole_in[0] + self.whole_in[1]

    def drain(self):
        for kind in range(4):
            self.copy(kind).wait_send()
        for turn, shift in enumerate((2, 1, 3, 0)):
            self.swap(turn, shift).wait_send()


TURNS = (3, 2, 4, 1)


def shift_of(step):
    return 2 - step + 3 * (step // 2) - 2 * (step // 3)


def stream(count, loads, work):
    for copy in loads(0, 0):
        copy.start()

    def one(i, carry):
        slot = lax.rem(i, 2)

        @pl.when(i + 1 < count)
        def _():
            for copy in loads(i + 1, 1 - slot):
                copy.start()

        for copy in loads(i, slot):
            copy.wait()
        work(i, slot)
        return carry

    lax.fori_loop(0, count, one, 0)


def reduce_kernel(
    dq_ref,
    att_ref,
    inst_ref,
    dk_hbm,
    dv_hbm,
    hid_hbm,
    cot_hbm,
    nei_hbm,
    wq_hbm,
    wk_hbm,
    wv_hbm,
    gh_ref,
    came_ref,
    gq_ref,
    go_ref,
    gk_ref,
    gv_ref,
    dq_two,
    att_two,
    gpart,
    dpart,
    ghalf,
    gquarter,
    gacross,
    dhalf,
    dquarter,
    w_tile,
    tile,
    near_tile,
    dk_tile,
    dv_tile,
    wk,
    wv,
    going,
    mine,
    out_w,
    out_near,
    out_whole,
    out_half,
    in_w,
    in_near,
    in_whole,
    in_half,
    kv_w,
    kv_near,
    kv_whole,
    kv_half,
    gq_done,
    go_done,
    g_send,
    g_recv,
    d_send,
    d_recv,
    out_send,
    out_recv,
    in_send,
    in_recv,
    kv_send,
    kv_recv,
    pair_send,
    pair_recv,
    swap_send,
    swap_recv,
    load_sem,
    tile_sem,
    near_sem,
):
    place = Place()
    x, y = place.x, place.y
    width = dq_ref.shape[1]
    piece_rows = going.shape[2]
    groups, cap = going.shape[:2]
    rows, enc = dpart.shape[2:]
    weights = [
        pltpu.make_async_copy(wk_hbm, wk, load_sem.at[1]),
        pltpu.make_async_copy(wv_hbm, wv, load_sem.at[2]),
    ]
    for copy in weights:
        copy.start()
    right = pl.ds(width, width)
    halves = [
        partner_copy(place, dq_ref, dq_two.at[:, right], pair_send.at[0], pair_recv.at[0]),
        partner_copy(place, att_ref, att_two.at[:, right], pair_send.at[1], pair_recv.at[1]),
    ]
    greet(place, True)
    for copy in halves:
        copy.start()
    dq_two[:, :width] = dq_ref[...]
    att_two[:, :width] = att_ref[...]
    core = lax.rem(lax.axis_index("wide"), 2)
    keep = lax.rem(core + place.set, 2)
    wide_sum = SetReduce(place, gpart, ghalf, gquarter, gacross, g_send, g_recv)
    near_sum = Reduce(place, dpart, dhalf, dquarter, d_send, d_recv)
    out_ring = Ring(out_w, out_near, out_whole, out_half, out_send, out_recv, keep)
    in_ring = Ring(in_w, in_near, in_whole, in_half, in_send, in_recv, keep)
    kv_ring = Ring(kv_w, kv_near, kv_whole, kv_half, kv_send, kv_recv, core)

    def dot(a, b, ca, cb):
        return lax.dot_general(
            a, b, (((ca,), (cb,)), ((), ())), precision=MID, preferred_element_type=jnp.float32
        )

    def g_load(i, slot):
        block = wq_hbm.at[wrap(x + shift_of(i // 2)), lax.rem(i, 2)]
        return [pltpu.make_async_copy(block, w_tile.at[slot], tile_sem.at[slot])]

    def g_work(i, slot):
        shift = shift_of(i // 2)
        gpart[wrap(x + shift), lax.rem(i, 2)] = dot(dq_two[...], w_tile[slot], 1, 1)

        @pl.when(i == 1)
        def _():
            wide_sum.begin(1)
            wide_sum.begin(2)

        @pl.when(lax.rem(i, 2) == 1)
        def _():
            wide_sum.across(shift).start()

    def weight_grad(source, two_ref, ring):
        def load(i, slot):
            block = source.at[wrap(ring.z + shift_of(i // 2)), lax.rem(i, 2)]
            return [pltpu.make_async_copy(block, tile.at[slot], tile_sem.at[slot])]

        def work(i, slot):
            shift, u = shift_of(i // 2), lax.rem(i, 2)
            part = pl.ds(pl.multiple_of(u * width, width), width)
            both = dot(tile[slot], two_ref[...], 0, 0)
            ring.w[0, wrap(ring.z + shift), part, :] = both[:, :width]
            ring.w[1, wrap(ring.z + shift), part, :] = both[:, width:]

            @pl.when(u == 1)
            def _():
                ring.swap(i // 2, shift).start()

        stream(2 * SIDE, load, work)

    def handed(which, done, out_ref):
        return partner_copy(
            place, done, out_ref, pair_send.at[2 + which], pair_recv.at[2 + which], True
        )

    def deliver(which, ring, done, out_ref):
        done[...] = ring.finish()

        @pl.when(keep == 0)
        def _():
            out_ref[...] = done[...]

        @pl.when(keep == 1)
        def _():
            handed(which, done, out_ref).start()

    def delivered(which, done, out_ref):
        @pl.when(keep == 1)
        def _():
            handed(which, done, out_ref).wait()

    def near_load(sources):
        def load(i, slot):
            at = (wrap(x + shift_of(i // 2)), pl.ds(2 * lax.rem(i, 2), 2))
            return [
                pltpu.make_async_copy(source.at[at], buf.at[slot], near_sem.at[2 * which + slot])
                for which, (source, buf) in enumerate(sources)
            ]

        return load

    def d_work(i, slot):
        shift = shift_of(i // 2)
        bx, by = wrap(x + shift), 2 * lax.rem(i, 2)
        dk = dk_tile[slot].reshape(2 * rows, width)
        dv = dv_tile[slot].reshape(2 * rows, width)
        dpart[bx, pl.ds(by, 2)] = (dot(dk, wk[...], 1, 1) + dot(dv, wv[...], 1, 1)).reshape(
            2, rows, enc
        )

        @pl.when(i == 1)
        def _():
            for turn in TURNS:
                near_sum.begin(1, turn)

        @pl.when(lax.rem(i, 2) == 1)
        def _():
            near_sum.begin(0, shift + 1)

    def neighbour_grad():
        for copy in weights:
            copy.wait()
        stream(2 * SIDE, near_load(((dk_hbm, dk_tile), (dv_hbm, dv_tile))), d_work)

    def kv_work(i, slot):
        dk = dk_tile[slot].reshape(2 * rows, width)
        dv = dv_tile[slot].reshape(2 * rows, width)
        near = near_tile[slot].reshape(2 * rows, enc)
        pair = dot(near, jnp.concatenate([dk, dv], axis=1), 0, 0)
        for group in range(groups):
            share = pair[group * kv_w.shape[2] : (group + 1) * kv_w.shape[2]]
            kv_w[group % 2, group // 2] += share

    def kv_grad():
        kv_w[...] = jnp.zeros_like(kv_w)
        stream(
            2 * SIDE, near_load(((dk_hbm, dk_tile), (dv_hbm, dv_tile), (nei_hbm, near_tile))), kv_work
        )
        for turn, shift in enumerate((2, 1, 3, 0)):
            kv_ring.swap(turn, shift).start()

    def near_middle(turn):
        for half in (0, 1):
            near_sum.middle(half, turn)

    def near_finish(turn):
        for half in (0, 1):
            near_sum.finish(half, turn)
        if turn == 3:
            for half in (0, 1):
                near_sum.begin(half, 0)

    neighbour_grad()
    halves[0].wait()
    stream(2 * SIDE, g_load, g_work)
    weight_grad(hid_hbm, dq_two, in_ring)
    wide_sum.middle(1)
    wide_sum.take(2)
    wide_sum.begin(0)
    in_ring.begin()
    halves[1].wait()
    weight_grad(cot_hbm, att_two, out_ring)
    near_middle(3)
    near_middle(4)
    near_middle(2)
    out_ring.begin()
    in_ring.middle()
    kv_grad()
    near_finish(3)
    kv_ring.begin()
    wide_sum.middle(2)
    near_middle(1)
    out_ring.middle()
    near_finish(4)
    deliver(0, in_ring, gq_done, gq_ref)
    near_finish(2)
    near_middle(0)
    wide_sum.take(1)
    wide_sum.take(3)
    kv_ring.middle()
    wide_sum.finish(2)
    wide_sum.across(4).start()
    wide_sum.finish(1)
    near_finish(1)
    deliver(1, out_ring, go_done, go_ref)
    wide_sum.middle(0)
    near_finish(0)
    for i in range(groups * cap):
        mine[i] = dpart[x, y, pl.ds(i * piece_rows, piece_rows), :]
    for slot in range(groups * cap):
        going[slot // cap, slot % cap] = mine[inst_ref[slot]]
    swaps = exchange(going, came_ref, swap_send, swap_recv, load_sem.at[3])
    wide_sum.take(0)
    pair = kv_ring.finish()
    gk_ref[...] = pair[:, :width]
    gv_ref[...] = pair[:, width:]
    wide_sum.take(4)
    wide_sum.finish(0)
    gh_ref[...] = gpart[x, place.member]
    delivered(0, gq_done, gq_ref)
    delivered(1, go_done, go_ref)
    for copy in swaps:
        copy.wait()
    for target in (wide_sum, near_sum, out_ring, in_ring, kv_ring):
        target.drain()


def result_kernel(slot_ref, came_ref, *refs):
    sources, table_ref, results = refs[:5], refs[5], refs[6:]
    for source, result in zip(sources, results):
        result[...] = source[...]
    table_ref[...] = jnp.zeros_like(table_ref)
    cap = came_ref.shape[1]
    for i in range(came_ref.shape[0] * cap):
        slot = slot_ref[i]
        table_ref[slot] += came_ref[i // cap, i % cap]


def vmem(n):
    return [pl.BlockSpec(memory_space=pltpu.VMEM)] * n


def hbm(n):
    return [pl.BlockSpec(memory_space=pl.ANY)] * n


def smem(n):
    return [pl.BlockSpec(memory_space=pltpu.SMEM)] * n


def f32(*shape):
    return jax.ShapeDtypeStruct(shape, jnp.float32)


def gather_call(hidden, cotangent, table, nbr_ids, owner_map, wq, wo, wk, wv, groups):
    tokens, width = hidden.shape
    _, piece_rows, enc = table.shape
    inst = nbr_ids.size // groups
    going = (groups, inst // groups, piece_rows, enc)
    rows = inst * piece_rows
    places = jax.ShapeDtypeStruct((inst,), jnp.int32)
    dma = pltpu.SemaphoreType.DMA
    blocks = (SIDE, 2, tokens, width)
    pairs = (SIDE, 2, width, 2 * width)
    out_shape = [
        f32(*blocks),
        f32(*blocks),
        f32(SIDE, SIDE, rows, enc),
        f32(*pairs),
        places,
        places,
        places,
        f32(tokens, width),
        f32(tokens, width),
        f32(SIDE, SIDE, rows, width),
        f32(SIDE, SIDE, rows, width),
    ]
    scratch = [
        pltpu.VMEM((tokens, 2 * width), jnp.float32),
        pltpu.VMEM((tokens, 2 * width), jnp.float32),
        pltpu.VMEM((tokens, width), jnp.float32),
        pltpu.VMEM((tokens, width), jnp.float32),
        pltpu.VMEM((SIDE, SIDE, rows, width), jnp.float32),
        pltpu.VMEM((SIDE, SIDE, rows, width), jnp.float32),
        pltpu.VMEM(blocks, jnp.float32),
        pltpu.VMEM(blocks, jnp.float32),
        pltpu.VMEM((SIDE, SIDE, rows, enc), jnp.float32),
        pltpu.VMEM(pairs, jnp.float32),
        pltpu.VMEM(pairs, jnp.float32),
        pltpu.VMEM((enc, 2 * width), jnp.float32),
        pltpu.VMEM(going, jnp.float32),
        pltpu.VMEM(going, jnp.float32),
    ]
    scratch += [dma((17,))] * 4 + [dma((40,))] * 2 + [dma((8,))] * 4 + [dma((4,))] * 2
    scratch += [dma((groups,))] * 2 + [dma((8,)), dma((12,))]
    return pl.pallas_call(
        gather_kernel,
        out_shape=out_shape,
        in_specs=hbm(2) + vmem(1) + smem(2) + hbm(4),
        out_specs=hbm(4) + smem(3) + vmem(4),
        scratch_shapes=scratch,
        compiler_params=pltpu.CompilerParams(
            collective_id=0, has_side_effects=True, vmem_limit_bytes=VMEM_LIMIT
        ),
        cost_estimate=pl.CostEstimate(flops=24_000_000_000, bytes_accessed=60_000_000, transcendentals=0),
    )(hidden, cotangent, table, nbr_ids, owner_map, wq, wo, wk, wv)


def reduce_call(dq, att, inst_of, dk, dv, hid, cot, nei, wq, wk, wv, groups):
    tokens, width = dq.shape
    rows = dk.shape[2]
    enc = wk.shape[0]
    slots = inst_of.shape[0]
    cap = slots // groups
    piece_rows = rows // slots
    dma = pltpu.SemaphoreType.DMA
    going = (groups, cap, piece_rows, enc)
    out_rows, enc_rows = 2 * width, enc // groups

    def ring(rows, cols):
        return [
            pltpu.VMEM((*n, r, cols), jnp.float32)
            for n, r in (((2, SIDE), rows), ((SIDE,), rows), ((2,), rows), ((2,), rows // 2))
        ]

    scratch = [
        pltpu.VMEM((tokens, 2 * width), jnp.float32),
        pltpu.VMEM((tokens, 2 * width), jnp.float32),
        pltpu.VMEM((SIDE, 2, tokens, width), jnp.float32),
        pltpu.VMEM((SIDE, SIDE, rows, enc), jnp.float32),
        pltpu.VMEM((6, tokens // 2, width), jnp.float32),
        pltpu.VMEM((6, tokens // 4, width), jnp.float32),
        pltpu.VMEM((5, tokens // 2, width), jnp.float32),
        pltpu.VMEM((20, rows // 2, enc), jnp.float32),
        pltpu.VMEM((20, rows // 4, enc), jnp.float32),
        pltpu.VMEM((2, width, 2 * width), jnp.float32),
        pltpu.VMEM((2, tokens, width), jnp.float32),
        pltpu.VMEM((2, 2, rows, enc), jnp.float32),
        pltpu.VMEM((2, 2, rows, width), jnp.float32),
        pltpu.VMEM((2, 2, rows, width), jnp.float32),
        pltpu.VMEM(wk.shape, jnp.float32),
        pltpu.VMEM(wv.shape, jnp.float32),
        pltpu.VMEM(going, jnp.float32),
        pltpu.VMEM((slots, piece_rows, enc), jnp.float32),
    ]
    scratch += ring(out_rows, width) + ring(out_rows, width) + ring(enc_rows, 2 * width)
    scratch += [pltpu.VMEM((out_rows, width), jnp.float32)] * 2
    scratch += [dma((17,))] * 2 + [dma((40,))] * 2 + [dma((8,))] * 6 + [dma((4,))] * 2
    scratch += [dma((groups,))] * 2 + [dma((4,)), dma((2,)), dma((6,))]
    return pl.pallas_call(
        reduce_kernel,
        out_shape=[
            f32(tokens, width),
            f32(*going),
            f32(out_rows, width),
            f32(out_rows, width),
            f32(enc_rows, width),
            f32(enc_rows, width),
        ],
        in_specs=vmem(2) + smem(1) + hbm(8),
        out_specs=vmem(6),
        scratch_shapes=scratch,
        compiler_params=pltpu.CompilerParams(
            collective_id=1, has_side_effects=True, vmem_limit_bytes=REDUCE_LIMIT
        ),
        cost_estimate=pl.CostEstimate(flops=50_000_000_000, bytes_accessed=60_000_000, transcendentals=0),
    )(dq, att, inst_of, dk, dv, hid, cot, nei, wq, wk, wv)


def body(
    hidden_states, out_cotangent, enc_table, nbr_ids, owner_map, w_query, w_key, w_value, w_out
):
    groups = lax.axis_size("wide")
    width = hidden_states.shape[1]
    query_blocks = w_query.reshape(SIDE, SIDE, width, width)
    out_blocks = w_out.reshape(SIDE, SIDE, width, width)
    hid, cot, nei, query_pair, picks, _, inst_of, attended, d_query, d_keys, d_values = gather_call(
        hidden_states, out_cotangent, enc_table, nbr_ids, owner_map, query_blocks, out_blocks,
        w_key, w_value, groups,
    )
    grad_hidden, arrived, grad_query, grad_out, grad_key, grad_value = reduce_call(
        d_query, attended, inst_of, d_keys, d_values, hid, cot, nei, query_pair, w_key, w_value,
        groups,
    )
    sums = (grad_hidden, grad_query, grad_key, grad_value, grad_out)
    grad_table, *sums = pl.pallas_call(
        result_kernel,
        out_shape=[f32(*enc_table.shape)] + [f32(*t.shape) for t in sums],
        in_specs=smem(1) + vmem(6),
        out_specs=vmem(6),
    )(picks, arrived, *sums)
    return (*sums, grad_table)


def solution(mesh):
    placed = (
        P("wide", "narrow"),
        P("wide", "narrow"),
        P("wide", "narrow", None),
        P(),
        P(),
        P(None, "narrow"),
        P(None, "narrow"),
        P(None, "narrow"),
        P(None, "narrow"),
    )
    return jax.shard_map(
        body,
        mesh=mesh,
        in_specs=placed,
        out_specs=(
            P("wide", "narrow"),
            P("wide", "narrow"),
            P("wide", "narrow"),
            P("wide", "narrow"),
            P("wide", "narrow"),
            P("wide", "narrow", None),
        ),
        check_vma=False,
    )
```

```python
import functools

import jax
import jax.numpy as jnp
from jax import lax
from jax.experimental import pallas as pl
from jax.experimental.pallas import tpu as pltpu
from jax.sharding import PartitionSpec as P

HEAD_DIM = 128
SPAN = 64
NEIGH = 2
SIDE = 4
VMEM_LIMIT = 60 * 1024 * 1024
REDUCE_LIMIT = 63 * 1024 * 1024

HIGH = lax.Precision.HIGHEST
MID = lax.Precision.HIGH
MESH = pl.DeviceIdType.MESH


def wrap(value):
    return lax.rem(value + 2 * SIDE, SIDE)


class Place:
    def __init__(self):
        me = lax.axis_index("narrow")
        self.x = me // SIDE
        self.y = lax.rem(me, SIDE)
        self.set = self.y // 2
        self.member = lax.rem(self.y, 2)

    def at(self, dx, dy):
        return {"narrow": wrap(self.x + dx) * SIDE + wrap(self.y + dy)}

    def mate(self):
        return {"narrow": self.x * SIDE + self.y + 1 - 2 * self.member}

    def partner(self):
        return {"narrow": self.x * SIDE + SIDE - 1 - self.y}

    def own(self, half):
        return (self.x, self.y) if half == 0 else (self.y, self.x)

    @staticmethod
    def block(half, first, second):
        return (first, second) if half == 0 else (second, first)

    def device(self, half, first, second):
        bx, by = self.block(half, first, second)
        return {"narrow": bx * SIDE + by}

    def line(self, half, turn, shift):
        first, second = self.own(half)
        if isinstance(turn, int) and turn == 0:
            return wrap(first + shift), second
        return first, wrap(second + shift)


class SetGather:
    def __init__(self, place, buf, send, recv):
        self.place, self.buf, self.send, self.recv = place, buf, send, recv
        self.rows = buf.shape[2] // 2

    def copy(self, slot, bx, member, start, rows, device):
        piece = self.buf.at[bx, member, pl.ds(start, rows)]
        return pltpu.make_async_remote_copy(
            src_ref=piece,
            dst_ref=piece,
            send_sem=self.send.at[slot],
            recv_sem=self.recv.at[slot],
            device_id=device,
            device_id_type=MESH,
        )

    def ring(self, which, kind, arriving=False):
        place = self.place
        member = place.member if which < 2 else 1 - place.member
        ahead = (1, -1, 1, -1)[kind]
        shift = (0, 0, -1, 1)[kind] - (ahead if arriving else 0)
        start = self.rows * (which > 0) + (self.rows // 2 if kind == 3 else 0)
        rows = self.rows if kind < 2 else self.rows // 2
        return self.copy(
            which * 4 + kind, wrap(place.x + shift), member, start, rows, place.at(ahead, 0)
        )

    def across(self, turn, arriving=False):
        place = self.place
        member = 1 - place.member if arriving else place.member
        bx = wrap(place.x + turn)
        start = self.rows if turn == 4 else 0
        return self.copy(12 + turn, bx, member, start, self.rows, place.mate())

    def begin(self, which):
        for kind in (0, 1):
            self.ring(which, kind).start()

    def forward(self, which):
        for kind in (0, 1):
            self.ring(which, kind, True).wait_recv()
            self.ring(which, kind + 2).start()

    def finish(self, which):
        for kind in (2, 3):
            self.ring(which, kind, True).wait_recv()

    def drain(self):
        for which in range(3):
            for kind in range(4):
                self.ring(which, kind).wait_send()
        for turn in range(5):
            self.across(turn).wait_send()


class SetReduce:
    def __init__(self, place, part, whole_in, quarter_in, across_in, send, recv):
        self.place, self.part = place, part
        self.whole_in, self.quarter_in, self.across_in = whole_in, quarter_in, across_in
        self.send, self.recv = send, recv
        self.rows = part.shape[2] // 2

    def ring(self, which, kind):
        place = self.place
        member = place.member if which < 2 else 1 - place.member
        ahead = (1, -1, 1, -1)[kind]
        shift = (1, -1, 2, 2)[kind]
        start = self.rows * (which > 0) + (self.rows // 2 if kind == 3 else 0)
        rows = self.rows if kind < 2 else self.rows // 2
        landing = self.whole_in if kind < 2 else self.quarter_in
        slot = which * 4 + kind
        return pltpu.make_async_remote_copy(
            src_ref=self.part.at[wrap(place.x + shift), member, pl.ds(start, rows)],
            dst_ref=landing.at[which * 2 + kind % 2],
            send_sem=self.send.at[slot],
            recv_sem=self.recv.at[slot],
            device_id=place.at(ahead, 0),
            device_id_type=MESH,
        )

    def across(self, turn):
        place = self.place
        start = self.rows if isinstance(turn, int) and turn == 4 else 0
        return pltpu.make_async_remote_copy(
            src_ref=self.part.at[
                wrap(place.x + turn), 1 - place.member, pl.ds(start, self.rows)
            ],
            dst_ref=self.across_in.at[turn],
            send_sem=self.send.at[12 + turn],
            recv_sem=self.recv.at[12 + turn],
            device_id=place.mate(),
            device_id_type=MESH,
        )

    def take(self, turn):
        self.across(turn).wait_recv()
        rows = pl.ds(self.rows if turn == 4 else 0, self.rows)
        self.part[wrap(self.place.x + turn), self.place.member, rows, :] += self.across_in[turn]

    def begin(self, which):
        for kind in (2, 3):
            self.ring(which, kind).start()

    def middle(self, which):
        member = self.place.member if which < 2 else 1 - self.place.member
        for kind in (2, 3):
            self.ring(which, kind).wait_recv()
            start = self.rows * (which > 0) + (self.rows // 2 if kind == 3 else 0)
            bx = wrap(self.place.x + (1 if kind == 2 else -1))
            self.part[bx, member, pl.ds(start, self.rows // 2), :] += self.quarter_in[
                which * 2 + kind % 2
            ]
            self.ring(which, kind - 2).start()

    def finish(self, which):
        member = self.place.member if which < 2 else 1 - self.place.member
        for kind in (0, 1):
            self.ring(which, kind).wait_recv()
        rows = pl.ds(self.rows * (which > 0), self.rows)
        self.part[self.place.x, member, rows, :] += (
            self.whole_in[which * 2] + self.whole_in[which * 2 + 1]
        )

    def drain(self):
        for which in range(3):
            for kind in range(4):
                self.ring(which, kind).wait_send()
        for turn in range(5):
            self.across(turn).wait_send()


def partner_copy(place, src, dst, send, recv, other_core=False):
    device = place.partner()
    if other_core:
        group = lax.axis_index("wide")
        device = {"wide": group + 1 - 2 * lax.rem(group, 2), **device}
    return pltpu.make_async_remote_copy(
        src_ref=src,
        dst_ref=dst,
        send_sem=send,
        recv_sem=recv,
        device_id=device,
        device_id_type=MESH,
    )


def greet(place, diagonal=False):
    groups = lax.axis_size("wide")
    group = lax.axis_index("wide")
    barrier = pltpu.get_barrier_semaphore()
    for half in (0, 1):
        for shift in (1, -1):
            pl.semaphore_signal(
                barrier,
                inc=1,
                device_id=place.device(half, *place.line(half, 0, shift)),
                device_id_type=MESH,
            )
    for step in range(1, groups):
        pl.semaphore_signal(
            barrier,
            inc=1,
            device_id={"wide": lax.rem(group + step, groups)},
            device_id_type=MESH,
        )
    if diagonal:
        pl.semaphore_signal(
            barrier,
            inc=1,
            device_id={"wide": group + 1 - 2 * lax.rem(group, 2), **place.partner()},
            device_id_type=MESH,
        )
    pl.semaphore_wait(barrier, 4 + groups - 1 + int(diagonal))


def exchange(out_ref, in_ref, send, recv, local):
    groups = lax.axis_size("wide")
    group = lax.axis_index("wide")
    copies = []
    for step in range(1, groups):
        peer = lax.rem(group + step, groups)
        copy = pltpu.make_async_remote_copy(
            src_ref=out_ref.at[peer],
            dst_ref=in_ref.at[group],
            send_sem=send.at[step],
            recv_sem=recv.at[step],
            device_id={"wide": peer},
            device_id_type=MESH,
        )
        copy.start()
        copies.append(copy)
    mine = pltpu.make_async_copy(out_ref.at[group], in_ref.at[group], local)
    mine.start()
    copies.append(mine)
    return copies


class Gather:
    def __init__(self, place, buf, send, recv):
        self.place, self.buf, self.send, self.recv = place, buf, send, recv
        self.rows = buf.shape[2]

    def copy(self, half, turn, kind, block, dest):
        rows = self.rows // 2 if kind < 2 else self.rows // 4
        start = half * (self.rows // 2) + (self.rows // 4 if kind == 3 else 0)
        bx, by = self.place.block(half, *block)
        piece = self.buf.at[bx, by, pl.ds(start, rows)]
        slot = (half * 5 + turn) * 4 + kind
        return pltpu.make_async_remote_copy(
            src_ref=piece,
            dst_ref=piece,
            send_sem=self.send.at[slot],
            recv_sem=self.recv.at[slot],
            device_id=self.place.device(half, *dest),
            device_id_type=MESH,
        )

    def at(self, half, turn, shift):
        first, second = self.place.own(half)
        if isinstance(turn, int) and turn == 0:
            return wrap(first + shift), second
        return wrap(first + turn - 1), wrap(second + shift)

    def along_y(self, half, turn):
        return half == 1 if isinstance(turn, int) and turn == 0 else half == 0

    def describe(self, half, turn, kind):
        shift = (0, 0, -1, 1)[kind]
        ahead = (1, -1, 1, -1)[kind]
        if kind >= 2 and self.along_y(half, turn):
            ahead = 2 * self.place.member - 1
            shift = -ahead
        return self.copy(
            half, turn, kind, self.at(half, turn, shift), self.place.line(half, turn, ahead)
        )

    def arrival(self, half, turn, kind):
        shift = (-1, 1, 2, 2)[kind]
        ahead = (1, -1, 1, -1)[kind]
        return self.copy(
            half, turn, kind, self.at(half, turn, shift), self.place.line(half, turn, ahead)
        )

    def begin(self, half, turn):
        self.describe(half, turn, 0).start()
        self.describe(half, turn, 1).start()

    def forward(self, half, turn):
        if self.along_y(half, turn):
            for kind in (0, 1):
                self.arrival(half, turn, kind).wait_recv()
            for kind in (2, 3):
                self.describe(half, turn, kind).start()
            return
        for kind in (0, 1):
            self.arrival(half, turn, kind).wait_recv()
            self.describe(half, turn, kind + 2).start()

    def finish(self, half, turn):
        for kind in (2, 3):
            self.arrival(half, turn, kind).wait_recv()

    def drain(self):
        for half in (0, 1):
            for turn in range(5):
                for kind in range(4):
                    self.describe(half, turn, kind).wait_send()


def attend(half, q_ref, da_ref, keys_ref, values_ref, att_ref, dq_ref, dk_ref, dv_ref):
    scale = HEAD_DIM ** (-0.5)
    heads = q_ref.shape[1] // HEAD_DIM
    spans = q_ref.shape[0] // SPAN
    few = keys_ref.shape[2] // spans
    near = SIDE * SIDE * few

    def dot(a, b, ca, cb, precision=MID):
        return lax.dot_general(
            a, b, (((ca,), (cb,)), ((), ())), precision=precision,
            preferred_element_type=jnp.float32,
        )

    def span(c, carry):
        rows = pl.ds(pl.multiple_of(c * SPAN, SPAN), SPAN)
        pieces = pl.ds(pl.multiple_of(c * few, few), few)
        for head in range(heads):
            cols = pl.ds(head * HEAD_DIM, HEAD_DIM)
            q = q_ref[rows, cols]
            da = da_ref[rows, cols]
            k = keys_ref[:, :, pieces, cols].reshape(near, HEAD_DIM)
            v = values_ref[:, :, pieces, cols].reshape(near, HEAD_DIM)
            scores = dot(q, k, 1, 1, HIGH) * scale
            dp = dot(da, v, 1, 1)
            top = jnp.max(scores, axis=-1, keepdims=True)
            e = jnp.exp(scores - top)
            probs = e / jnp.sum(e, axis=-1, keepdims=True)
            ds = probs * (dp - jnp.sum(dp * probs, axis=-1, keepdims=True)) * scale
            att_ref[rows, cols] = dot(probs, v, 1, 0)
            dq_ref[rows, cols] = dot(ds, k, 1, 0)
            shape = (SIDE, SIDE, few, HEAD_DIM)
            dk_ref[:, :, pieces, cols] = dot(ds, q, 0, 0).reshape(shape)
            dv_ref[:, :, pieces, cols] = dot(probs, da, 0, 0).reshape(shape)
        return carry

    lax.fori_loop(half * spans // 2, (half + 1) * spans // 2, span, 0)


class Spread:
    def __init__(self, place, source, wide_w, send, recv):
        self.place, self.source, self.w = place, source, wide_w
        self.send, self.recv = send, recv
        self.group = lax.axis_index("wide")
        self.z, self.core = self.group // 2, lax.rem(self.group, 2)
        self.width = source.shape[3]

    def slot(self, group):
        return self.w.at[group // 2, lax.rem(group, 2), :, pl.ds(self.width, self.width)]

    def first(self):
        block = self.source.at[self.z, 2 * (1 - self.place.set) + self.core]
        return partner_copy(
            self.place, block, self.slot(self.group), self.send.at[0], self.recv.at[0]
        )

    def to(self, index, group, target):
        return pltpu.make_async_remote_copy(
            src_ref=self.slot(group),
            dst_ref=self.slot(group),
            send_sem=self.send.at[index],
            recv_sem=self.recv.at[index],
            device_id={"wide": target},
            device_id_type=MESH,
        )

    def along(self, step, arriving=False):
        there = wrap(self.z + step) * 2 + self.core
        back = wrap(self.z - step) * 2 + self.core
        return self.to(step, back if arriving else self.group, there)

    def beside(self, step, arriving=False):
        core = 1 - self.core if arriving else self.core
        other = self.z * 2 + 1 - self.core
        return self.to(4 + step, wrap(self.z - step) * 2 + core, other)

    def spread(self):
        self.first().wait_recv()
        for step in (1, 3, 2):
            self.along(step).start()
        self.beside(0).start()

    def pass_on(self):
        for step in (1, 3, 2):
            self.along(step, True).wait_recv()
            self.beside(step).start()

    def finish(self):
        for step in range(SIDE):
            self.beside(step, True).wait_recv()

    def drain(self):
        self.first().wait_send()
        for step in (1, 2, 3):
            self.along(step).wait_send()
        for step in range(SIDE):
            self.beside(step).wait_send()


def gather_kernel(
    hid_ref,
    cot_ref,
    table_ref,
    nbr_ref,
    map_ref,
    wq_ref,
    wo_ref,
    wk_ref,
    wv_ref,
    hid_out,
    cot_out,
    nei_out,
    wq_out,
    pick_ref,
    slot_ref,
    inst_ref,
    att_ref,
    dq_ref,
    dk_ref,
    dv_ref,
    q_two,
    da_two,
    q_came,
    da_came,
    keys_ref,
    values_ref,
    hid,
    cot,
    nei,
    wq,
    wo,
    wkv,
    going,
    came,
    hid_send,
    hid_recv,
    cot_send,
    cot_recv,
    nei_send,
    nei_recv,
    wq_send,
    wq_recv,
    wo_send,
    wo_recv,
    pair_send,
    pair_recv,
    swap_send,
    swap_recv,
    load_sem,
    store_sem,
):
    place = Place()
    x, y = place.x, place.y
    tokens, width = dq_ref.shape
    groups, cap, piece_rows, _ = came.shape
    inst = nei.shape[2] // piece_rows
    own = [
        pltpu.make_async_copy(hid_ref, hid.at[x, place.member], load_sem.at[0]),
        pltpu.make_async_copy(cot_ref, cot.at[x, place.member], load_sem.at[1]),
    ]
    mine = pl.ds(2 * place.set, 2)
    left = pl.ds(0, width)
    weights = [
        pltpu.make_async_copy(wq_ref.at[:, mine], wq.at[:, :, :, left], load_sem.at[2]),
        pltpu.make_async_copy(wo_ref.at[:, mine], wo.at[:, :, :, left], load_sem.at[3]),
        pltpu.make_async_copy(wk_ref, wkv.at[:, pl.ds(0, width)], load_sem.at[4]),
        pltpu.make_async_copy(wv_ref, wkv.at[:, pl.ds(width, width)], load_sem.at[5]),
    ]
    for copy in own:
        copy.start()
    greet(place)
    for copy in own:
        copy.wait()
    pair = [
        SetGather(place, hid, hid_send, hid_recv),
        SetGather(place, cot, cot_send, cot_recv),
    ]
    near = Gather(place, nei, nei_send, nei_recv)
    spreads = [
        Spread(place, wq_ref, wq, wq_send, wq_recv),
        Spread(place, wo_ref, wo, wo_send, wo_recv),
    ]
    hid_set, cot_set = pair

    group = lax.axis_index("wide")
    stored = table_ref.shape[0]

    def stored_at(g, i):
        return map_ref[nbr_ref[i % NEIGH, g * (inst // NEIGH) + i // NEIGH]]

    def offer():
        def one(g, carry):
            count = jnp.int32(0)
            chosen = [jnp.int32(0)] * cap
            for i in range(inst):
                at = stored_at(g, i) - group * stored
                hit = (at >= 0) & (at < stored)
                chosen = [
                    jnp.where(hit & (count == r), at, old) for r, old in enumerate(chosen)
                ]
                count = count + hit.astype(jnp.int32)
            for r in range(cap):
                pick_ref[g * cap + r] = chosen[r]
                going[g, r] = table_ref[chosen[r]]
            return carry

        lax.fori_loop(0, groups, one, 0)
        return exchange(going, came, swap_send, swap_recv, load_sem.at[6])

    def places():
        owners = [lax.div(stored_at(group, i), stored) for i in range(inst)]
        slots = [
            owner * cap + sum((owners[j] == owner).astype(jnp.int32) for j in range(i))
            for i, owner in enumerate(owners)
        ]
        for i in range(inst):
            slot_ref[i] = slots[i]

        def one(slot, carry):
            inst_ref[slot] = sum(jnp.where(slot_ref[i] == slot, i, 0) for i in range(inst))
            return carry

        lax.fori_loop(0, inst, one, 0)

    def accept(swaps):
        for copy in swaps:
            copy.wait()
        for i in range(inst):
            slot = slot_ref[i]
            nei[x, y, pl.ds(i * piece_rows, piece_rows), :] = came[
                slot // cap, lax.rem(slot, cap)
            ]

    def set_forward(gather):
        gather.forward(0)
        gather.across(1).start()
        gather.across(3).start()

    def set_other(gather):
        gather.across(4, True).wait_recv()
        gather.begin(2)

    def set_finish(gather):
        gather.finish(0)
        gather.across(2).start()

    def add_products(gather, half, bx):
        rows = pl.ds(half * (tokens // 2), tokens // 2)
        total, weight, precision = (
            (q_two, wq, HIGH) if gather is hid_set else (da_two, wo, MID)
        )

        def column(member, carry):
            total[rows, :] += jnp.dot(
                gather.buf[bx, member, rows, :], weight[bx, member], precision=precision,
                preferred_element_type=jnp.float32,
            )
            return carry

        lax.fori_loop(0, 2, column, 0)

    def project(gather, half):
        if half == 0:
            for turn in (0, 1, 3, 2):
                gather.across(turn, True).wait_recv()
                add_products(gather, 0, wrap(x + turn))
            return
        gather.finish(1)
        gather.finish(2)

        def block(bx, carry):
            add_products(gather, 1, bx)
            return carry

        lax.fori_loop(0, SIDE, block, 0)

    def half_copy(gather, half):
        rows = pl.ds(half * (tokens // 2), tokens // 2)
        total, came_ref = (q_two, q_came) if gather is hid_set else (da_two, da_came)
        sem = half + 2 * int(gather is cot_set)
        return partner_copy(
            place,
            total.at[rows, pl.ds(width, width)],
            came_ref.at[rows],
            pair_send.at[sem],
            pair_recv.at[sem],
        )

    def add_half(gather, half):
        half_copy(gather, half).wait_recv()
        rows = pl.ds(half * (tokens // 2), tokens // 2)
        total, came_ref = (q_two, q_came) if gather is hid_set else (da_two, da_came)
        came_ref[rows, :] += total[rows, :width]

    def near_keep(half, turn):
        first = wrap(place.own(half)[0] + turn - 1)
        rows = pl.ds(half * (nei.shape[2] // 2), nei.shape[2] // 2)
        at = (first, slice(None), rows) if half == 0 else (slice(None), first, rows)
        return pltpu.make_async_copy(nei.at[at], nei_out.at[at], store_sem.at[2 + half * 5 + turn])

    def near_project(half, turn):
        near.finish(half, turn)
        near_keep(half, turn).start()
        first = wrap(place.own(half)[0] + turn - 1)
        few = nei.shape[2] // 2
        rows = pl.ds(half * few, few)
        if half == 0:
            blocks = nei[first, :, rows, :]
        else:
            blocks = nei[:, first, rows, :]
        both = jnp.dot(
            blocks.reshape(SIDE * few, nei.shape[3]), wkv[...], precision=HIGH,
            preferred_element_type=jnp.float32,
        ).reshape(SIDE, few, 2 * width)
        if half == 0:
            keys_ref[first, :, rows, :] = both[:, :, :width]
            values_ref[first, :, rows, :] = both[:, :, width:]
        else:
            keys_ref[:, first, rows, :] = both[:, :, :width]
            values_ref[:, first, rows, :] = both[:, :, width:]

    def near_begin(turn):
        for half in (0, 1):
            near.begin(half, turn)

    attended = (q_came, da_came, keys_ref, values_ref, att_ref, dq_ref, dk_ref, dv_ref)

    cot_set.begin(0)
    for spread in spreads:
        spread.first().start()
    cot_set.across(0).start()
    cot_set.begin(1)
    cot_set.across(4).start()
    swaps = offer()
    places()
    for copy in weights:
        copy.start()
    q_two[...] = jnp.zeros_like(q_two)
    da_two[...] = jnp.zeros_like(da_two)
    accept(swaps)
    set_forward(cot_set)
    set_other(cot_set)
    near_begin(0)
    hid_set.across(4).start()
    for spread in spreads:
        spread.spread()
    near_begin(1)
    hid_set.begin(0)
    for half in (0, 1):
        near.forward(half, 0)
    near_begin(2)
    near_begin(4)
    hid_set.begin(1)
    set_other(hid_set)
    set_forward(hid_set)
    for spread in spreads:
        spread.pass_on()
    cot_set.forward(2)
    cot_set.forward(1)
    near.forward(0, 1)
    near.forward(0, 4)
    near.forward(1, 1)
    for copy in weights:
        copy.wait()
    near_project(0, 4)
    set_finish(cot_set)
    near.forward(0, 2)
    near_project(0, 1)
    hid_set.forward(1)
    for spread in spreads:
        spread.finish()
    keep_weights = pltpu.make_async_copy(wq, wq_out, load_sem.at[7])
    keep_weights.start()
    hid_set.forward(2)
    for half in (0, 1):
        near.finish(half, 0)
    near_begin(3)
    near.forward(1, 4)
    project(cot_set, 0)
    hid_set.across(0).start()
    half_copy(cot_set, 0).start()
    project(cot_set, 1)
    half_copy(cot_set, 1).start()
    keep_cot = pltpu.make_async_copy(cot, cot_out, store_sem.at[1])
    keep_cot.start()
    near_project(1, 1)
    set_finish(hid_set)
    near_project(0, 2)
    project(hid_set, 1)
    half_copy(hid_set, 1).start()
    near.forward(1, 2)
    project(hid_set, 0)
    near.forward(0, 3)
    near.forward(1, 3)
    half_copy(hid_set, 0).start()
    keep_hid = pltpu.make_async_copy(hid, hid_out, store_sem.at[0])
    keep_hid.start()
    near_project(1, 4)
    near_project(1, 2)
    add_half(cot_set, 1)
    near_project(1, 3)
    add_half(cot_set, 0)
    add_half(hid_set, 1)
    attend(1, *attended)
    near_project(0, 3)
    add_half(hid_set, 0)
    attend(0, *attended)
    for target in (*pair, near, *spreads):
        target.drain()
    for gather in pair:
        for half in (0, 1):
            half_copy(gather, half).wait_send()
    for copy in (keep_weights, keep_hid, keep_cot):
        copy.wait()
    for half in (0, 1):
        for turn in range(1, SIDE + 1):
            near_keep(half, turn).wait()


class Reduce:
    def __init__(self, place, part, whole_in, quarter_in, send, recv):
        self.place, self.part = place, part
        self.whole_in, self.quarter_in = whole_in, quarter_in
        self.send, self.recv = send, recv
        self.rows = part.shape[2]

    def at(self, half, turn, shift):
        first, second = self.place.own(half)
        if isinstance(turn, int) and turn == 0:
            return wrap(first + shift), second
        return wrap(first + turn - 1), wrap(second + shift)

    def piece(self, half, block, kind):
        rows = self.rows // 2 if kind < 2 else self.rows // 4
        start = half * (self.rows // 2) + (self.rows // 4 if kind == 3 else 0)
        bx, by = self.place.block(half, *block)
        return bx, by, pl.ds(start, rows)

    def copy(self, half, turn, kind):
        ahead = (1, -1, 1, -1)[kind]
        shift = (1, -1, 2, 2)[kind]
        slot = (half * 5 + turn) * 2 + kind % 2
        landing = (self.whole_in if kind < 2 else self.quarter_in).at[slot]
        bx, by, rows = self.piece(half, self.at(half, turn, shift), kind)
        sem = (half * 5 + turn) * 4 + kind
        return pltpu.make_async_remote_copy(
            src_ref=self.part.at[bx, by, rows],
            dst_ref=landing,
            send_sem=self.send.at[sem],
            recv_sem=self.recv.at[sem],
            device_id=self.place.device(half, *self.place.line(half, turn, ahead)),
            device_id_type=MESH,
        )

    def begin(self, half, turn):
        for kind in (2, 3):
            self.copy(half, turn, kind).start()

    def middle(self, half, turn):
        for kind in (2, 3):
            self.copy(half, turn, kind).wait_recv()
            slot = (half * 5 + turn) * 2 + kind % 2
            shift = 1 if kind == 2 else -1
            bx, by, rows = self.piece(half, self.at(half, turn, shift), kind)
            self.part[bx, by, rows, :] += self.quarter_in[slot]
            self.copy(half, turn, kind - 2).start()

    def finish(self, half, turn):
        for kind in (0, 1):
            self.copy(half, turn, kind).wait_recv()
        slot = (half * 5 + turn) * 2
        bx, by, rows = self.piece(half, self.at(half, turn, 0), 0)
        self.part[bx, by, rows, :] += self.whole_in[slot] + self.whole_in[slot + 1]

    def drain(self):
        for half in (0, 1):
            for turn in range(5):
                for kind in range(4):
                    self.copy(half, turn, kind).wait_send()


class Ring:
    def __init__(self, w, near_in, whole_in, half_in, send, recv, keep):
        group = lax.axis_index("wide")
        self.z, self.core, self.keep = group // 2, lax.rem(group, 2), keep
        self.w, self.near_in, self.whole_in, self.half_in = w, near_in, whole_in, half_in
        self.send, self.recv = send, recv
        self.half_rows = w.shape[2] // 2

    def swap(self, turn, shift):
        to = wrap(self.z + shift)
        return pltpu.make_async_remote_copy(
            src_ref=self.w.at[1 - self.keep, to],
            dst_ref=self.near_in.at[to],
            send_sem=self.send.at[4 + turn],
            recv_sem=self.recv.at[4 + turn],
            device_id={"wide": self.z * 2 + 1 - self.core},
            device_id_type=MESH,
        )

    def take(self, turn, shift):
        self.swap(turn, shift).wait_recv()
        to = wrap(self.z + shift)
        self.w[self.keep, to] += self.near_in[to]

    def copy(self, kind):
        ahead = (1, -1, 1, -1)[kind]
        shift = (1, -1, 2, 2)[kind]
        source = self.w.at[self.keep, wrap(self.z + shift)]
        landing = self.whole_in
        if kind >= 2:
            source = source.at[pl.ds((kind - 2) * self.half_rows, self.half_rows)]
            landing = self.half_in
        return pltpu.make_async_remote_copy(
            src_ref=source,
            dst_ref=landing.at[kind % 2],
            send_sem=self.send.at[kind],
            recv_sem=self.recv.at[kind],
            device_id={"wide": wrap(self.z + ahead) * 2 + self.core},
            device_id_type=MESH,
        )

    def begin(self):
        self.take(0, 2)
        for kind in (2, 3):
            self.copy(kind).start()

    def middle(self):
        for kind in (2, 3):
            shift = 1 if kind == 2 else -1
            self.take(kind - 1, shift)
            self.copy(kind).wait_recv()
            rows = pl.ds((kind - 2) * self.half_rows, self.half_rows)
            self.w[self.keep, wrap(self.z + shift), rows, :] += self.half_in[kind - 2]
            self.copy(kind - 2).start()
        self.take(3, 0)

    def finish(self):
        for kind in (0, 1):
            self.copy(kind).wait_recv()
        return self.w[self.keep, self.z] + self.whole_in[0] + self.whole_in[1]

    def drain(self):
        for kind in range(4):
            self.copy(kind).wait_send()
        for turn, shift in enumerate((2, 1, 3, 0)):
            self.swap(turn, shift).wait_send()


TURNS = (3, 2, 4, 1)


def shift_of(step):
    return 2 - step + 3 * (step // 2) - 2 * (step // 3)


def stream(count, loads, work):
    for copy in loads(0, 0):
        copy.start()

    def one(i, carry):
        slot = lax.rem(i, 2)

        @pl.when(i + 1 < count)
        def _():
            for copy in loads(i + 1, 1 - slot):
                copy.start()

        for copy in loads(i, slot):
            copy.wait()
        work(i, slot)
        return carry

    lax.fori_loop(0, count, one, 0)


def reduce_kernel(
    dq_ref,
    att_ref,
    inst_ref,
    dk_hbm,
    dv_hbm,
    hid_hbm,
    cot_hbm,
    nei_hbm,
    wq_hbm,
    wk_hbm,
    wv_hbm,
    gh_ref,
    came_ref,
    gq_ref,
    go_ref,
    gk_ref,
    gv_ref,
    dq_two,
    att_two,
    gpart,
    dpart,
    ghalf,
    gquarter,
    gacross,
    dhalf,
    dquarter,
    w_tile,
    tile,
    near_tile,
    dk_tile,
    dv_tile,
    wk,
    wv,
    going,
    mine,
    out_w,
    out_near,
    out_whole,
    out_half,
    in_w,
    in_near,
    in_whole,
    in_half,
    kv_w,
    kv_near,
    kv_whole,
    kv_half,
    gq_done,
    go_done,
    g_send,
    g_recv,
    d_send,
    d_recv,
    out_send,
    out_recv,
    in_send,
    in_recv,
    kv_send,
    kv_recv,
    pair_send,
    pair_recv,
    swap_send,
    swap_recv,
    load_sem,
    tile_sem,
    near_sem,
):
    place = Place()
    x, y = place.x, place.y
    width = dq_ref.shape[1]
    piece_rows = going.shape[2]
    groups, cap = going.shape[:2]
    rows, enc = dpart.shape[2:]
    weights = [
        pltpu.make_async_copy(wk_hbm, wk, load_sem.at[1]),
        pltpu.make_async_copy(wv_hbm, wv, load_sem.at[2]),
    ]
    for copy in weights:
        copy.start()
    right = pl.ds(width, width)
    halves = [
        partner_copy(place, dq_ref, dq_two.at[:, right], pair_send.at[0], pair_recv.at[0]),
        partner_copy(place, att_ref, att_two.at[:, right], pair_send.at[1], pair_recv.at[1]),
    ]
    greet(place, True)
    for copy in halves:
        copy.start()
    dq_two[:, :width] = dq_ref[...]
    att_two[:, :width] = att_ref[...]
    core = lax.rem(lax.axis_index("wide"), 2)
    keep = lax.rem(core + place.set, 2)
    wide_sum = SetReduce(place, gpart, ghalf, gquarter, gacross, g_send, g_recv)
    near_sum = Reduce(place, dpart, dhalf, dquarter, d_send, d_recv)
    out_ring = Ring(out_w, out_near, out_whole, out_half, out_send, out_recv, keep)
    in_ring = Ring(in_w, in_near, in_whole, in_half, in_send, in_recv, keep)
    kv_ring = Ring(kv_w, kv_near, kv_whole, kv_half, kv_send, kv_recv, core)

    def dot(a, b, ca, cb):
        return lax.dot_general(
            a, b, (((ca,), (cb,)), ((), ())), precision=MID, preferred_element_type=jnp.float32
        )

    def g_load(i, slot):
        block = wq_hbm.at[wrap(x + shift_of(i // 2)), lax.rem(i, 2)]
        return [pltpu.make_async_copy(block, w_tile.at[slot], tile_sem.at[slot])]

    def g_work(i, slot):
        shift = shift_of(i // 2)
        gpart[wrap(x + shift), lax.rem(i, 2)] = dot(dq_two[...], w_tile[slot], 1, 1)

        @pl.when(i == 1)
        def _():
            wide_sum.begin(1)
            wide_sum.begin(2)

        @pl.when(lax.rem(i, 2) == 1)
        def _():
            wide_sum.across(shift).start()

    def weight_grad(source, two_ref, ring):
        def load(i, slot):
            block = source.at[wrap(ring.z + shift_of(i // 2)), lax.rem(i, 2)]
            return [pltpu.make_async_copy(block, tile.at[slot], tile_sem.at[slot])]

        def work(i, slot):
            shift, u = shift_of(i // 2), lax.rem(i, 2)
            part = pl.ds(pl.multiple_of(u * width, width), width)
            both = dot(tile[slot], two_ref[...], 0, 0)
            ring.w[0, wrap(ring.z + shift), part, :] = both[:, :width]
            ring.w[1, wrap(ring.z + shift), part, :] = both[:, width:]

            @pl.when(u == 1)
            def _():
                ring.swap(i // 2, shift).start()

        stream(2 * SIDE, load, work)

    def handed(which, done, out_ref):
        return partner_copy(
            place, done, out_ref, pair_send.at[2 + which], pair_recv.at[2 + which], True
        )

    def deliver(which, ring, done, out_ref):
        done[...] = ring.finish()

        @pl.when(keep == 0)
        def _():
            out_ref[...] = done[...]

        @pl.when(keep == 1)
        def _():
            handed(which, done, out_ref).start()

    def delivered(which, done, out_ref):
        @pl.when(keep == 1)
        def _():
            handed(which, done, out_ref).wait()

    def near_load(sources):
        def load(i, slot):
            at = (wrap(x + shift_of(i // 2)), pl.ds(2 * lax.rem(i, 2), 2))
            return [
                pltpu.make_async_copy(source.at[at], buf.at[slot], near_sem.at[2 * which + slot])
                for which, (source, buf) in enumerate(sources)
            ]

        return load

    def d_work(i, slot):
        shift = shift_of(i // 2)
        bx, by = wrap(x + shift), 2 * lax.rem(i, 2)
        dk = dk_tile[slot].reshape(2 * rows, width)
        dv = dv_tile[slot].reshape(2 * rows, width)
        dpart[bx, pl.ds(by, 2)] = (dot(dk, wk[...], 1, 1) + dot(dv, wv[...], 1, 1)).reshape(
            2, rows, enc
        )

        @pl.when(i == 1)
        def _():
            for turn in TURNS:
                near_sum.begin(1, turn)

        @pl.when(lax.rem(i, 2) == 1)
        def _():
            near_sum.begin(0, shift + 1)

    def neighbour_grad():
        for copy in weights:
            copy.wait()
        stream(2 * SIDE, near_load(((dk_hbm, dk_tile), (dv_hbm, dv_tile))), d_work)

    def kv_work(i, slot):
        dk = dk_tile[slot].reshape(2 * rows, width)
        dv = dv_tile[slot].reshape(2 * rows, width)
        near = near_tile[slot].reshape(2 * rows, enc)
        pair = dot(near, jnp.concatenate([dk, dv], axis=1), 0, 0)
        for group in range(groups):
            share = pair[group * kv_w.shape[2] : (group + 1) * kv_w.shape[2]]
            kv_w[group % 2, group // 2] += share

    def kv_grad():
        kv_w[...] = jnp.zeros_like(kv_w)
        stream(
            2 * SIDE, near_load(((dk_hbm, dk_tile), (dv_hbm, dv_tile), (nei_hbm, near_tile))), kv_work
        )
        for turn, shift in enumerate((2, 1, 3, 0)):
            kv_ring.swap(turn, shift).start()

    def near_middle(turn):
        for half in (0, 1):
            near_sum.middle(half, turn)

    def near_finish(turn):
        for half in (0, 1):
            near_sum.finish(half, turn)
        if turn == 3:
            for half in (0, 1):
                near_sum.begin(half, 0)

    neighbour_grad()
    halves[0].wait()
    stream(2 * SIDE, g_load, g_work)
    weight_grad(hid_hbm, dq_two, in_ring)
    wide_sum.middle(1)
    wide_sum.take(2)
    wide_sum.begin(0)
    in_ring.begin()
    halves[1].wait()
    weight_grad(cot_hbm, att_two, out_ring)
    near_middle(3)
    near_middle(4)
    near_middle(2)
    out_ring.begin()
    in_ring.middle()
    kv_grad()
    near_finish(3)
    kv_ring.begin()
    wide_sum.middle(2)
    near_middle(1)
    out_ring.middle()
    near_finish(4)
    deliver(0, in_ring, gq_done, gq_ref)
    near_finish(2)
    near_middle(0)
    wide_sum.take(1)
    wide_sum.take(3)
    kv_ring.middle()
    wide_sum.finish(2)
    wide_sum.across(4).start()
    wide_sum.finish(1)
    near_finish(1)
    deliver(1, out_ring, go_done, go_ref)
    wide_sum.middle(0)
    near_finish(0)
    for i in range(groups * cap):
        mine[i] = dpart[x, y, pl.ds(i * piece_rows, piece_rows), :]
    for slot in range(groups * cap):
        going[slot // cap, slot % cap] = mine[inst_ref[slot]]
    swaps = exchange(going, came_ref, swap_send, swap_recv, load_sem.at[3])
    wide_sum.take(0)
    pair = kv_ring.finish()
    gk_ref[...] = pair[:, :width]
    gv_ref[...] = pair[:, width:]
    wide_sum.take(4)
    wide_sum.finish(0)
    gh_ref[...] = gpart[x, place.member]
    delivered(0, gq_done, gq_ref)
    delivered(1, go_done, go_ref)
    for copy in swaps:
        copy.wait()
    for target in (wide_sum, near_sum, out_ring, in_ring, kv_ring):
        target.drain()


def result_kernel(slot_ref, came_ref, *refs):
    sources, table_ref, results, sems = refs[:5], refs[5], refs[6:11], refs[11]
    copies = [
        pltpu.make_async_copy(source, result, sems.at[i])
        for i, (source, result) in enumerate(zip(sources, results))
    ]
    for copy in copies:
        copy.start()
    table_ref[...] = jnp.zeros_like(table_ref)
    cap = came_ref.shape[1]
    for i in range(came_ref.shape[0] * cap):
        slot = slot_ref[i]
        table_ref[slot] += came_ref[i // cap, i % cap]
    for copy in copies:
        copy.wait()


def vmem(n):
    return [pl.BlockSpec(memory_space=pltpu.VMEM)] * n


def hbm(n):
    return [pl.BlockSpec(memory_space=pl.ANY)] * n


def smem(n):
    return [pl.BlockSpec(memory_space=pltpu.SMEM)] * n


def f32(*shape):
    return jax.ShapeDtypeStruct(shape, jnp.float32)


def gather_call(hidden, cotangent, table, nbr_ids, owner_map, wq, wo, wk, wv, groups):
    tokens, width = hidden.shape
    _, piece_rows, enc = table.shape
    inst = nbr_ids.size // groups
    going = (groups, inst // groups, piece_rows, enc)
    rows = inst * piece_rows
    places = jax.ShapeDtypeStruct((inst,), jnp.int32)
    dma = pltpu.SemaphoreType.DMA
    blocks = (SIDE, 2, tokens, width)
    pairs = (SIDE, 2, width, 2 * width)
    out_shape = [
        f32(*blocks),
        f32(*blocks),
        f32(SIDE, SIDE, rows, enc),
        f32(*pairs),
        places,
        places,
        places,
        f32(tokens, width),
        f32(tokens, width),
        f32(SIDE, SIDE, rows, width),
        f32(SIDE, SIDE, rows, width),
    ]
    scratch = [
        pltpu.VMEM((tokens, 2 * width), jnp.float32),
        pltpu.VMEM((tokens, 2 * width), jnp.float32),
        pltpu.VMEM((tokens, width), jnp.float32),
        pltpu.VMEM((tokens, width), jnp.float32),
        pltpu.VMEM((SIDE, SIDE, rows, width), jnp.float32),
        pltpu.VMEM((SIDE, SIDE, rows, width), jnp.float32),
        pltpu.VMEM(blocks, jnp.float32),
        pltpu.VMEM(blocks, jnp.float32),
        pltpu.VMEM((SIDE, SIDE, rows, enc), jnp.float32),
        pltpu.VMEM(pairs, jnp.float32),
        pltpu.VMEM(pairs, jnp.float32),
        pltpu.VMEM((enc, 2 * width), jnp.float32),
        pltpu.VMEM(going, jnp.float32),
        pltpu.VMEM(going, jnp.float32),
    ]
    scratch += [dma((17,))] * 4 + [dma((40,))] * 2 + [dma((8,))] * 4 + [dma((4,))] * 2
    scratch += [dma((groups,))] * 2 + [dma((8,)), dma((12,))]
    return pl.pallas_call(
        gather_kernel,
        out_shape=out_shape,
        in_specs=hbm(2) + vmem(1) + smem(2) + hbm(4),
        out_specs=hbm(4) + smem(3) + vmem(4),
        scratch_shapes=scratch,
        compiler_params=pltpu.CompilerParams(
            collective_id=0, has_side_effects=True, vmem_limit_bytes=VMEM_LIMIT
        ),
        cost_estimate=pl.CostEstimate(flops=24_000_000_000, bytes_accessed=60_000_000, transcendentals=0),
    )(hidden, cotangent, table, nbr_ids, owner_map, wq, wo, wk, wv)


def reduce_call(dq, att, inst_of, dk, dv, hid, cot, nei, wq, wk, wv, groups):
    tokens, width = dq.shape
    rows = dk.shape[2]
    enc = wk.shape[0]
    slots = inst_of.shape[0]
    cap = slots // groups
    piece_rows = rows // slots
    dma = pltpu.SemaphoreType.DMA
    going = (groups, cap, piece_rows, enc)
    out_rows, enc_rows = 2 * width, enc // groups

    def ring(rows, cols):
        return [
            pltpu.VMEM((*n, r, cols), jnp.float32)
            for n, r in (((2, SIDE), rows), ((SIDE,), rows), ((2,), rows), ((2,), rows // 2))
        ]

    scratch = [
        pltpu.VMEM((tokens, 2 * width), jnp.float32),
        pltpu.VMEM((tokens, 2 * width), jnp.float32),
        pltpu.VMEM((SIDE, 2, tokens, width), jnp.float32),
        pltpu.VMEM((SIDE, SIDE, rows, enc), jnp.float32),
        pltpu.VMEM((6, tokens // 2, width), jnp.float32),
        pltpu.VMEM((6, tokens // 4, width), jnp.float32),
        pltpu.VMEM((5, tokens // 2, width), jnp.float32),
        pltpu.VMEM((20, rows // 2, enc), jnp.float32),
        pltpu.VMEM((20, rows // 4, enc), jnp.float32),
        pltpu.VMEM((2, width, 2 * width), jnp.float32),
        pltpu.VMEM((2, tokens, width), jnp.float32),
        pltpu.VMEM((2, 2, rows, enc), jnp.float32),
        pltpu.VMEM((2, 2, rows, width), jnp.float32),
        pltpu.VMEM((2, 2, rows, width), jnp.float32),
        pltpu.VMEM(wk.shape, jnp.float32),
        pltpu.VMEM(wv.shape, jnp.float32),
        pltpu.VMEM(going, jnp.float32),
        pltpu.VMEM((slots, piece_rows, enc), jnp.float32),
    ]
    scratch += ring(out_rows, width) + ring(out_rows, width) + ring(enc_rows, 2 * width)
    scratch += [pltpu.VMEM((out_rows, width), jnp.float32)] * 2
    scratch += [dma((17,))] * 2 + [dma((40,))] * 2 + [dma((8,))] * 6 + [dma((4,))] * 2
    scratch += [dma((groups,))] * 2 + [dma((4,)), dma((2,)), dma((6,))]
    return pl.pallas_call(
        reduce_kernel,
        out_shape=[
            f32(tokens, width),
            f32(*going),
            f32(out_rows, width),
            f32(out_rows, width),
            f32(enc_rows, width),
            f32(enc_rows, width),
        ],
        in_specs=vmem(2) + smem(1) + hbm(8),
        out_specs=vmem(6),
        scratch_shapes=scratch,
        compiler_params=pltpu.CompilerParams(
            collective_id=1, has_side_effects=True, vmem_limit_bytes=REDUCE_LIMIT
        ),
        cost_estimate=pl.CostEstimate(flops=50_000_000_000, bytes_accessed=60_000_000, transcendentals=0),
    )(dq, att, inst_of, dk, dv, hid, cot, nei, wq, wk, wv)


def body(
    hidden_states, out_cotangent, enc_table, nbr_ids, owner_map, w_query, w_key, w_value, w_out
):
    groups = lax.axis_size("wide")
    width = hidden_states.shape[1]
    query_blocks = w_query.reshape(SIDE, SIDE, width, width)
    out_blocks = w_out.reshape(SIDE, SIDE, width, width)
    hid, cot, nei, query_pair, picks, _, inst_of, attended, d_query, d_keys, d_values = gather_call(
        hidden_states, out_cotangent, enc_table, nbr_ids.T, owner_map, query_blocks, out_blocks,
        w_key, w_value, groups,
    )
    grad_hidden, arrived, grad_query, grad_out, grad_key, grad_value = reduce_call(
        d_query, attended, inst_of, d_keys, d_values, hid, cot, nei, query_pair, w_key, w_value,
        groups,
    )
    sums = (grad_hidden, grad_query, grad_key, grad_value, grad_out)
    grad_table, *sums = pl.pallas_call(
        result_kernel,
        out_shape=[f32(*enc_table.shape)] + [f32(*t.shape) for t in sums],
        in_specs=smem(1) + vmem(1) + hbm(5),
        out_specs=vmem(1) + hbm(5),
        scratch_shapes=[pltpu.SemaphoreType.DMA((5,))],
    )(picks, arrived, *sums)
    return (*sums, grad_table)


def solution(mesh):
    placed = (
        P("wide", "narrow"),
        P("wide", "narrow"),
        P("wide", "narrow", None),
        P(),
        P(),
        P(None, "narrow"),
        P(None, "narrow"),
        P(None, "narrow"),
        P(None, "narrow"),
    )
    return jax.shard_map(
        body,
        mesh=mesh,
        in_specs=placed,
        out_specs=(
            P("wide", "narrow"),
            P("wide", "narrow"),
            P("wide", "narrow"),
            P("wide", "narrow"),
            P("wide", "narrow"),
            P("wide", "narrow", None),
        ),
        check_vma=False,
    )
```

```python
import functools

import jax
import jax.numpy as jnp
from jax import lax
from jax.experimental import pallas as pl
from jax.experimental.pallas import tpu as pltpu
from jax.sharding import PartitionSpec as P

HEAD_DIM = 128
SPAN = 64
NEIGH = 2
SIDE = 4
VMEM_LIMIT = 60 * 1024 * 1024
REDUCE_LIMIT = 63 * 1024 * 1024

HIGH = lax.Precision.HIGHEST
MID = lax.Precision.HIGH
MESH = pl.DeviceIdType.MESH


def wrap(value):
    return lax.rem(value + 2 * SIDE, SIDE)


class Place:
    def __init__(self):
        me = lax.axis_index("narrow")
        self.x = me // SIDE
        self.y = lax.rem(me, SIDE)
        self.set = self.y // 2
        self.member = lax.rem(self.y, 2)

    def at(self, dx, dy):
        return {"narrow": wrap(self.x + dx) * SIDE + wrap(self.y + dy)}

    def mate(self):
        return {"narrow": self.x * SIDE + self.y + 1 - 2 * self.member}

    def partner(self):
        return {"narrow": self.x * SIDE + SIDE - 1 - self.y}

    def own(self, half):
        return (self.x, self.y) if half == 0 else (self.y, self.x)

    @staticmethod
    def block(half, first, second):
        return (first, second) if half == 0 else (second, first)

    def device(self, half, first, second):
        bx, by = self.block(half, first, second)
        return {"narrow": bx * SIDE + by}

    def line(self, half, turn, shift):
        first, second = self.own(half)
        if isinstance(turn, int) and turn == 0:
            return wrap(first + shift), second
        return first, wrap(second + shift)


class SetGather:
    def __init__(self, place, buf, send, recv):
        self.place, self.buf, self.send, self.recv = place, buf, send, recv
        self.rows = buf.shape[2] // 2

    def copy(self, slot, bx, member, start, rows, device):
        piece = self.buf.at[bx, member, pl.ds(start, rows)]
        return pltpu.make_async_remote_copy(
            src_ref=piece,
            dst_ref=piece,
            send_sem=self.send.at[slot],
            recv_sem=self.recv.at[slot],
            device_id=device,
            device_id_type=MESH,
        )

    def ring(self, which, kind, arriving=False):
        place = self.place
        member = place.member if which < 2 else 1 - place.member
        ahead = (1, -1, 1, -1)[kind]
        shift = (0, 0, -1, 1)[kind] - (ahead if arriving else 0)
        start = self.rows * (which > 0) + (self.rows // 2 if kind == 3 else 0)
        rows = self.rows if kind < 2 else self.rows // 2
        return self.copy(
            which * 4 + kind, wrap(place.x + shift), member, start, rows, place.at(ahead, 0)
        )

    def across(self, turn, arriving=False):
        place = self.place
        member = 1 - place.member if arriving else place.member
        bx = wrap(place.x + turn)
        start = self.rows if turn == 4 else 0
        return self.copy(12 + turn, bx, member, start, self.rows, place.mate())

    def begin(self, which):
        for kind in (0, 1):
            self.ring(which, kind).start()

    def forward(self, which):
        for kind in (0, 1):
            self.ring(which, kind, True).wait_recv()
            self.ring(which, kind + 2).start()

    def finish(self, which):
        for kind in (2, 3):
            self.ring(which, kind, True).wait_recv()

    def drain(self):
        for which in range(3):
            for kind in range(4):
                self.ring(which, kind).wait_send()
        for turn in range(5):
            self.across(turn).wait_send()


class SetReduce:
    def __init__(self, place, part, whole_in, quarter_in, across_in, send, recv):
        self.place, self.part = place, part
        self.whole_in, self.quarter_in, self.across_in = whole_in, quarter_in, across_in
        self.send, self.recv = send, recv
        self.rows = part.shape[2] // 2

    def ring(self, which, kind):
        place = self.place
        member = place.member if which < 2 else 1 - place.member
        ahead = (1, -1, 1, -1)[kind]
        shift = (1, -1, 2, 2)[kind]
        start = self.rows * (which > 0) + (self.rows // 2 if kind == 3 else 0)
        rows = self.rows if kind < 2 else self.rows // 2
        landing = self.whole_in if kind < 2 else self.quarter_in
        slot = which * 4 + kind
        return pltpu.make_async_remote_copy(
            src_ref=self.part.at[wrap(place.x + shift), member, pl.ds(start, rows)],
            dst_ref=landing.at[which * 2 + kind % 2],
            send_sem=self.send.at[slot],
            recv_sem=self.recv.at[slot],
            device_id=place.at(ahead, 0),
            device_id_type=MESH,
        )

    def across(self, turn):
        place = self.place
        start = self.rows if isinstance(turn, int) and turn == 4 else 0
        return pltpu.make_async_remote_copy(
            src_ref=self.part.at[
                wrap(place.x + turn), 1 - place.member, pl.ds(start, self.rows)
            ],
            dst_ref=self.across_in.at[turn],
            send_sem=self.send.at[12 + turn],
            recv_sem=self.recv.at[12 + turn],
            device_id=place.mate(),
            device_id_type=MESH,
        )

    def take(self, turn):
        self.across(turn).wait_recv()
        rows = pl.ds(self.rows if turn == 4 else 0, self.rows)
        self.part[wrap(self.place.x + turn), self.place.member, rows, :] += self.across_in[turn]

    def begin(self, which):
        for kind in (2, 3):
            self.ring(which, kind).start()

    def middle(self, which):
        member = self.place.member if which < 2 else 1 - self.place.member
        for kind in (2, 3):
            self.ring(which, kind).wait_recv()
            start = self.rows * (which > 0) + (self.rows // 2 if kind == 3 else 0)
            bx = wrap(self.place.x + (1 if kind == 2 else -1))
            self.part[bx, member, pl.ds(start, self.rows // 2), :] += self.quarter_in[
                which * 2 + kind % 2
            ]
            self.ring(which, kind - 2).start()

    def finish(self, which):
        member = self.place.member if which < 2 else 1 - self.place.member
        for kind in (0, 1):
            self.ring(which, kind).wait_recv()
        rows = pl.ds(self.rows * (which > 0), self.rows)
        self.part[self.place.x, member, rows, :] += (
            self.whole_in[which * 2] + self.whole_in[which * 2 + 1]
        )

    def drain(self):
        for which in range(3):
            for kind in range(4):
                self.ring(which, kind).wait_send()
        for turn in range(5):
            self.across(turn).wait_send()


def partner_copy(place, src, dst, send, recv, other_core=False):
    device = place.partner()
    if other_core:
        group = lax.axis_index("wide")
        device = {"wide": group + 1 - 2 * lax.rem(group, 2), **device}
    return pltpu.make_async_remote_copy(
        src_ref=src,
        dst_ref=dst,
        send_sem=send,
        recv_sem=recv,
        device_id=device,
        device_id_type=MESH,
    )


def greet(place, diagonal=False):
    groups = lax.axis_size("wide")
    group = lax.axis_index("wide")
    barrier = pltpu.get_barrier_semaphore()
    for half in (0, 1):
        for shift in (1, -1):
            pl.semaphore_signal(
                barrier,
                inc=1,
                device_id=place.device(half, *place.line(half, 0, shift)),
                device_id_type=MESH,
            )
    for step in range(1, groups):
        pl.semaphore_signal(
            barrier,
            inc=1,
            device_id={"wide": lax.rem(group + step, groups)},
            device_id_type=MESH,
        )
    if diagonal:
        pl.semaphore_signal(
            barrier,
            inc=1,
            device_id={"wide": group + 1 - 2 * lax.rem(group, 2), **place.partner()},
            device_id_type=MESH,
        )
    pl.semaphore_wait(barrier, 4 + groups - 1 + int(diagonal))


def exchange(out_ref, in_ref, send, recv, local):
    groups = lax.axis_size("wide")
    group = lax.axis_index("wide")
    copies = []
    for step in range(1, groups):
        peer = lax.rem(group + step, groups)
        copy = pltpu.make_async_remote_copy(
            src_ref=out_ref.at[peer],
            dst_ref=in_ref.at[group],
            send_sem=send.at[step],
            recv_sem=recv.at[step],
            device_id={"wide": peer},
            device_id_type=MESH,
        )
        copy.start()
        copies.append(copy)
    mine = pltpu.make_async_copy(out_ref.at[group], in_ref.at[group], local)
    mine.start()
    copies.append(mine)
    return copies


class Gather:
    def __init__(self, place, buf, send, recv):
        self.place, self.buf, self.send, self.recv = place, buf, send, recv
        self.rows = buf.shape[2]

    def copy(self, half, turn, kind, block, dest):
        rows = self.rows // 2 if kind < 2 else self.rows // 4
        start = half * (self.rows // 2) + (self.rows // 4 if kind == 3 else 0)
        bx, by = self.place.block(half, *block)
        piece = self.buf.at[bx, by, pl.ds(start, rows)]
        slot = (half * 5 + turn) * 4 + kind
        return pltpu.make_async_remote_copy(
            src_ref=piece,
            dst_ref=piece,
            send_sem=self.send.at[slot],
            recv_sem=self.recv.at[slot],
            device_id=self.place.device(half, *dest),
            device_id_type=MESH,
        )

    def at(self, half, turn, shift):
        first, second = self.place.own(half)
        if isinstance(turn, int) and turn == 0:
            return wrap(first + shift), second
        return wrap(first + turn - 1), wrap(second + shift)

    def along_y(self, half, turn):
        return half == 1 if isinstance(turn, int) and turn == 0 else half == 0

    def describe(self, half, turn, kind):
        shift = (0, 0, -1, 1)[kind]
        ahead = (1, -1, 1, -1)[kind]
        if kind >= 2 and self.along_y(half, turn):
            ahead = 2 * self.place.member - 1
            shift = -ahead
        return self.copy(
            half, turn, kind, self.at(half, turn, shift), self.place.line(half, turn, ahead)
        )

    def arrival(self, half, turn, kind):
        shift = (-1, 1, 2, 2)[kind]
        ahead = (1, -1, 1, -1)[kind]
        return self.copy(
            half, turn, kind, self.at(half, turn, shift), self.place.line(half, turn, ahead)
        )

    def begin(self, half, turn):
        self.describe(half, turn, 0).start()
        self.describe(half, turn, 1).start()

    def forward(self, half, turn):
        if self.along_y(half, turn):
            for kind in (0, 1):
                self.arrival(half, turn, kind).wait_recv()
            for kind in (2, 3):
                self.describe(half, turn, kind).start()
            return
        for kind in (0, 1):
            self.arrival(half, turn, kind).wait_recv()
            self.describe(half, turn, kind + 2).start()

    def finish(self, half, turn):
        for kind in (2, 3):
            self.arrival(half, turn, kind).wait_recv()

    def drain(self):
        for half in (0, 1):
            for turn in range(5):
                for kind in range(4):
                    self.describe(half, turn, kind).wait_send()


def attend(half, q_ref, da_ref, keys_ref, values_ref, att_ref, dq_ref, dk_ref, dv_ref):
    scale = HEAD_DIM ** (-0.5)
    heads = q_ref.shape[1] // HEAD_DIM
    spans = q_ref.shape[0] // SPAN
    few = keys_ref.shape[2] // spans
    near = SIDE * SIDE * few

    def dot(a, b, ca, cb, precision=MID):
        return lax.dot_general(
            a, b, (((ca,), (cb,)), ((), ())), precision=precision,
            preferred_element_type=jnp.float32,
        )

    def span(c, carry):
        rows = pl.ds(pl.multiple_of(c * SPAN, SPAN), SPAN)
        pieces = pl.ds(pl.multiple_of(c * few, few), few)
        for head in range(heads):
            cols = pl.ds(head * HEAD_DIM, HEAD_DIM)
            q = q_ref[rows, cols]
            da = da_ref[rows, cols]
            k = keys_ref[:, :, pieces, cols].reshape(near, HEAD_DIM)
            v = values_ref[:, :, pieces, cols].reshape(near, HEAD_DIM)
            scores = dot(q, k, 1, 1, HIGH) * scale
            dp = dot(da, v, 1, 1)
            top = jnp.max(scores, axis=-1, keepdims=True)
            e = jnp.exp(scores - top)
            probs = e / jnp.sum(e, axis=-1, keepdims=True)
            ds = probs * (dp - jnp.sum(dp * probs, axis=-1, keepdims=True)) * scale
            att_ref[rows, cols] = dot(probs, v, 1, 0)
            dq_ref[rows, cols] = dot(ds, k, 1, 0)
            shape = (SIDE, SIDE, few, HEAD_DIM)
            dk_ref[:, :, pieces, cols] = dot(ds, q, 0, 0).reshape(shape)
            dv_ref[:, :, pieces, cols] = dot(probs, da, 0, 0).reshape(shape)
        return carry

    lax.fori_loop(half * spans // 2, (half + 1) * spans // 2, span, 0)


class Spread:
    def __init__(self, place, source, wide_w, send, recv):
        self.place, self.source, self.w = place, source, wide_w
        self.send, self.recv = send, recv
        self.group = lax.axis_index("wide")
        self.z, self.core = self.group // 2, lax.rem(self.group, 2)
        self.width = source.shape[3]

    def slot(self, group):
        return self.w.at[group // 2, lax.rem(group, 2), :, pl.ds(self.width, self.width)]

    def first(self):
        block = self.source.at[self.z, 2 * (1 - self.place.set) + self.core]
        return partner_copy(
            self.place, block, self.slot(self.group), self.send.at[0], self.recv.at[0]
        )

    def to(self, index, group, target):
        return pltpu.make_async_remote_copy(
            src_ref=self.slot(group),
            dst_ref=self.slot(group),
            send_sem=self.send.at[index],
            recv_sem=self.recv.at[index],
            device_id={"wide": target},
            device_id_type=MESH,
        )

    def along(self, step, arriving=False):
        there = wrap(self.z + step) * 2 + self.core
        back = wrap(self.z - step) * 2 + self.core
        return self.to(step, back if arriving else self.group, there)

    def beside(self, step, arriving=False):
        core = 1 - self.core if arriving else self.core
        other = self.z * 2 + 1 - self.core
        return self.to(4 + step, wrap(self.z - step) * 2 + core, other)

    def spread(self):
        self.first().wait_recv()
        for step in (1, 3, 2):
            self.along(step).start()
        self.beside(0).start()

    def pass_on(self):
        for step in (1, 3, 2):
            self.along(step, True).wait_recv()
            self.beside(step).start()

    def finish(self):
        for step in range(SIDE):
            self.beside(step, True).wait_recv()

    def drain(self):
        self.first().wait_send()
        for step in (1, 2, 3):
            self.along(step).wait_send()
        for step in range(SIDE):
            self.beside(step).wait_send()


def gather_kernel(
    hid_ref,
    cot_ref,
    table_ref,
    nbr_ref,
    map_ref,
    wq_ref,
    wo_ref,
    wk_ref,
    wv_ref,
    hid_out,
    cot_out,
    nei_out,
    wq_out,
    pick_ref,
    slot_ref,
    inst_ref,
    att_ref,
    dq_ref,
    dk_ref,
    dv_ref,
    q_two,
    da_two,
    q_came,
    da_came,
    keys_ref,
    values_ref,
    hid,
    cot,
    nei,
    wq,
    wo,
    wkv,
    going,
    came,
    hid_send,
    hid_recv,
    cot_send,
    cot_recv,
    nei_send,
    nei_recv,
    wq_send,
    wq_recv,
    wo_send,
    wo_recv,
    pair_send,
    pair_recv,
    swap_send,
    swap_recv,
    load_sem,
    store_sem,
):
    place = Place()
    x, y = place.x, place.y
    tokens, width = dq_ref.shape
    groups, cap, piece_rows, _ = came.shape
    inst = nei.shape[2] // piece_rows
    own = [
        pltpu.make_async_copy(hid_ref, hid.at[x, place.member], load_sem.at[0]),
        pltpu.make_async_copy(cot_ref, cot.at[x, place.member], load_sem.at[1]),
    ]
    mine = pl.ds(2 * place.set, 2)
    left = pl.ds(0, width)
    weights = [
        pltpu.make_async_copy(wq_ref.at[:, mine], wq.at[:, :, :, left], load_sem.at[2]),
        pltpu.make_async_copy(wo_ref.at[:, mine], wo.at[:, :, :, left], load_sem.at[3]),
        pltpu.make_async_copy(wk_ref, wkv.at[:, pl.ds(0, width)], load_sem.at[4]),
        pltpu.make_async_copy(wv_ref, wkv.at[:, pl.ds(width, width)], load_sem.at[5]),
    ]
    for copy in own:
        copy.start()
    greet(place)
    for copy in own:
        copy.wait()
    pair = [
        SetGather(place, hid, hid_send, hid_recv),
        SetGather(place, cot, cot_send, cot_recv),
    ]
    near = Gather(place, nei, nei_send, nei_recv)
    spreads = [
        Spread(place, wq_ref, wq, wq_send, wq_recv),
        Spread(place, wo_ref, wo, wo_send, wo_recv),
    ]
    hid_set, cot_set = pair

    group = lax.axis_index("wide")
    stored = table_ref.shape[0]

    def stored_at(g, i):
        return map_ref[nbr_ref[i % NEIGH, g * (inst // NEIGH) + i // NEIGH]]

    def offer():
        def one(g, carry):
            count = jnp.int32(0)
            chosen = [jnp.int32(0)] * cap
            for i in range(inst):
                at = stored_at(g, i) - group * stored
                hit = (at >= 0) & (at < stored)
                chosen = [
                    jnp.where(hit & (count == r), at, old) for r, old in enumerate(chosen)
                ]
                count = count + hit.astype(jnp.int32)
            for r in range(cap):
                pick_ref[g * cap + r] = chosen[r]
                going[g, r] = table_ref[chosen[r]]
            return carry

        lax.fori_loop(0, groups, one, 0)
        return exchange(going, came, swap_send, swap_recv, load_sem.at[6])

    def places():
        owners = [lax.div(stored_at(group, i), stored) for i in range(inst)]
        slots = [
            owner * cap + sum((owners[j] == owner).astype(jnp.int32) for j in range(i))
            for i, owner in enumerate(owners)
        ]
        for i in range(inst):
            slot_ref[i] = slots[i]

        def one(slot, carry):
            inst_ref[slot] = sum(jnp.where(slot_ref[i] == slot, i, 0) for i in range(inst))
            return carry

        lax.fori_loop(0, inst, one, 0)

    def accept(swaps):
        for copy in swaps:
            copy.wait()
        for i in range(inst):
            slot = slot_ref[i]
            nei[x, y, pl.ds(i * piece_rows, piece_rows), :] = came[
                slot // cap, lax.rem(slot, cap)
            ]

    def set_forward(gather):
        gather.forward(0)
        gather.across(1).start()
        gather.across(3).start()

    def set_other(gather):
        gather.across(4, True).wait_recv()
        gather.begin(2)

    def set_finish(gather):
        gather.finish(0)
        gather.across(2).start()

    def add_products(gather, half, bx):
        rows = pl.ds(half * (tokens // 2), tokens // 2)
        total, weight, precision = (
            (q_two, wq, HIGH) if gather is hid_set else (da_two, wo, MID)
        )

        def column(member, carry):
            total[rows, :] += jnp.dot(
                gather.buf[bx, member, rows, :], weight[bx, member], precision=precision,
                preferred_element_type=jnp.float32,
            )
            return carry

        lax.fori_loop(0, 2, column, 0)

    def project(gather, half):
        if half == 0:
            for turn in (0, 1, 3, 2):
                gather.across(turn, True).wait_recv()
                add_products(gather, 0, wrap(x + turn))
            return
        gather.finish(1)
        gather.finish(2)

        def block(bx, carry):
            add_products(gather, 1, bx)
            return carry

        lax.fori_loop(0, SIDE, block, 0)

    def half_copy(gather, half):
        rows = pl.ds(half * (tokens // 2), tokens // 2)
        total, came_ref = (q_two, q_came) if gather is hid_set else (da_two, da_came)
        sem = half + 2 * int(gather is cot_set)
        return partner_copy(
            place,
            total.at[rows, pl.ds(width, width)],
            came_ref.at[rows],
            pair_send.at[sem],
            pair_recv.at[sem],
        )

    def add_half(gather, half):
        half_copy(gather, half).wait_recv()
        rows = pl.ds(half * (tokens // 2), tokens // 2)
        total, came_ref = (q_two, q_came) if gather is hid_set else (da_two, da_came)
        came_ref[rows, :] += total[rows, :width]

    def near_keep(half, turn):
        first = wrap(place.own(half)[0] + turn - 1)
        rows = pl.ds(half * (nei.shape[2] // 2), nei.shape[2] // 2)
        at = (first, slice(None), rows) if half == 0 else (slice(None), first, rows)
        return pltpu.make_async_copy(nei.at[at], nei_out.at[at], store_sem.at[2 + half * 5 + turn])

    def near_project(half, turn):
        near.finish(half, turn)
        near_keep(half, turn).start()
        first = wrap(place.own(half)[0] + turn - 1)
        few = nei.shape[2] // 2
        rows = pl.ds(half * few, few)
        if half == 0:
            blocks = nei[first, :, rows, :]
        else:
            blocks = nei[:, first, rows, :]
        both = jnp.dot(
            blocks.reshape(SIDE * few, nei.shape[3]), wkv[...], precision=HIGH,
            preferred_element_type=jnp.float32,
        ).reshape(SIDE, few, 2 * width)
        if half == 0:
            keys_ref[first, :, rows, :] = both[:, :, :width]
            values_ref[first, :, rows, :] = both[:, :, width:]
        else:
            keys_ref[:, first, rows, :] = both[:, :, :width]
            values_ref[:, first, rows, :] = both[:, :, width:]

    def near_begin(turn):
        for half in (0, 1):
            near.begin(half, turn)

    attended = (q_came, da_came, keys_ref, values_ref, att_ref, dq_ref, dk_ref, dv_ref)

    cot_set.begin(0)
    for spread in spreads:
        spread.first().start()
    cot_set.across(0).start()
    cot_set.begin(1)
    cot_set.across(4).start()
    swaps = offer()
    places()
    for copy in weights:
        copy.start()
    q_two[...] = jnp.zeros_like(q_two)
    da_two[...] = jnp.zeros_like(da_two)
    accept(swaps)
    set_forward(cot_set)
    set_other(cot_set)
    near_begin(0)
    hid_set.across(4).start()
    for spread in spreads:
        spread.spread()
    near_begin(1)
    hid_set.begin(0)
    for half in (0, 1):
        near.forward(half, 0)
    near_begin(2)
    near_begin(4)
    hid_set.begin(1)
    set_other(hid_set)
    set_forward(hid_set)
    for spread in spreads:
        spread.pass_on()
    cot_set.forward(2)
    cot_set.forward(1)
    near.forward(0, 1)
    near.forward(0, 4)
    near.forward(1, 1)
    for copy in weights:
        copy.wait()
    near_project(0, 4)
    set_finish(cot_set)
    near.forward(0, 2)
    near_project(0, 1)
    hid_set.forward(1)
    for spread in spreads:
        spread.finish()
    keep_weights = pltpu.make_async_copy(wq, wq_out, load_sem.at[7])
    keep_weights.start()
    hid_set.forward(2)
    for half in (0, 1):
        near.finish(half, 0)
    near_begin(3)
    near.forward(1, 4)
    project(cot_set, 0)
    hid_set.across(0).start()
    half_copy(cot_set, 0).start()
    project(cot_set, 1)
    half_copy(cot_set, 1).start()
    keep_cot = pltpu.make_async_copy(cot, cot_out, store_sem.at[1])
    keep_cot.start()
    near_project(1, 1)
    set_finish(hid_set)
    near_project(0, 2)
    project(hid_set, 1)
    half_copy(hid_set, 1).start()
    near.forward(1, 2)
    project(hid_set, 0)
    near.forward(0, 3)
    near.forward(1, 3)
    half_copy(hid_set, 0).start()
    keep_hid = pltpu.make_async_copy(hid, hid_out, store_sem.at[0])
    keep_hid.start()
    near_project(1, 4)
    near_project(1, 2)
    add_half(cot_set, 1)
    near_project(1, 3)
    add_half(cot_set, 0)
    add_half(hid_set, 1)
    attend(1, *attended)
    near_project(0, 3)
    add_half(hid_set, 0)
    attend(0, *attended)
    for target in (*pair, near, *spreads):
        target.drain()
    for gather in pair:
        for half in (0, 1):
            half_copy(gather, half).wait_send()
    for copy in (keep_weights, keep_hid, keep_cot):
        copy.wait()
    for half in (0, 1):
        for turn in range(1, SIDE + 1):
            near_keep(half, turn).wait()


class Reduce:
    def __init__(self, place, part, whole_in, quarter_in, send, recv):
        self.place, self.part = place, part
        self.whole_in, self.quarter_in = whole_in, quarter_in
        self.send, self.recv = send, recv
        self.rows = part.shape[2]

    def at(self, half, turn, shift):
        first, second = self.place.own(half)
        if isinstance(turn, int) and turn == 0:
            return wrap(first + shift), second
        return wrap(first + turn - 1), wrap(second + shift)

    def piece(self, half, block, kind):
        rows = self.rows // 2 if kind < 2 else self.rows // 4
        start = half * (self.rows // 2) + (self.rows // 4 if kind == 3 else 0)
        bx, by = self.place.block(half, *block)
        return bx, by, pl.ds(start, rows)

    def copy(self, half, turn, kind):
        ahead = (1, -1, 1, -1)[kind]
        shift = (1, -1, 2, 2)[kind]
        slot = (half * 5 + turn) * 2 + kind % 2
        landing = (self.whole_in if kind < 2 else self.quarter_in).at[slot]
        bx, by, rows = self.piece(half, self.at(half, turn, shift), kind)
        sem = (half * 5 + turn) * 4 + kind
        return pltpu.make_async_remote_copy(
            src_ref=self.part.at[bx, by, rows],
            dst_ref=landing,
            send_sem=self.send.at[sem],
            recv_sem=self.recv.at[sem],
            device_id=self.place.device(half, *self.place.line(half, turn, ahead)),
            device_id_type=MESH,
        )

    def begin(self, half, turn):
        for kind in (2, 3):
            self.copy(half, turn, kind).start()

    def middle(self, half, turn):
        for kind in (2, 3):
            self.copy(half, turn, kind).wait_recv()
            slot = (half * 5 + turn) * 2 + kind % 2
            shift = 1 if kind == 2 else -1
            bx, by, rows = self.piece(half, self.at(half, turn, shift), kind)
            self.part[bx, by, rows, :] += self.quarter_in[slot]
            self.copy(half, turn, kind - 2).start()

    def finish(self, half, turn):
        for kind in (0, 1):
            self.copy(half, turn, kind).wait_recv()
        slot = (half * 5 + turn) * 2
        bx, by, rows = self.piece(half, self.at(half, turn, 0), 0)
        self.part[bx, by, rows, :] += self.whole_in[slot] + self.whole_in[slot + 1]

    def drain(self):
        for half in (0, 1):
            for turn in range(5):
                for kind in range(4):
                    self.copy(half, turn, kind).wait_send()


class Ring:
    def __init__(self, w, near_in, whole_in, half_in, send, recv, keep):
        group = lax.axis_index("wide")
        self.z, self.core, self.keep = group // 2, lax.rem(group, 2), keep
        self.w, self.near_in, self.whole_in, self.half_in = w, near_in, whole_in, half_in
        self.send, self.recv = send, recv
        self.half_rows = w.shape[2] // 2

    def swap(self, turn, shift):
        to = wrap(self.z + shift)
        return pltpu.make_async_remote_copy(
            src_ref=self.w.at[1 - self.keep, to],
            dst_ref=self.near_in.at[to],
            send_sem=self.send.at[4 + turn],
            recv_sem=self.recv.at[4 + turn],
            device_id={"wide": self.z * 2 + 1 - self.core},
            device_id_type=MESH,
        )

    def take(self, turn, shift):
        self.swap(turn, shift).wait_recv()
        to = wrap(self.z + shift)
        self.w[self.keep, to] += self.near_in[to]

    def copy(self, kind):
        ahead = (1, -1, 1, -1)[kind]
        shift = (1, -1, 2, 2)[kind]
        source = self.w.at[self.keep, wrap(self.z + shift)]
        landing = self.whole_in
        if kind >= 2:
            source = source.at[pl.ds((kind - 2) * self.half_rows, self.half_rows)]
            landing = self.half_in
        return pltpu.make_async_remote_copy(
            src_ref=source,
            dst_ref=landing.at[kind % 2],
            send_sem=self.send.at[kind],
            recv_sem=self.recv.at[kind],
            device_id={"wide": wrap(self.z + ahead) * 2 + self.core},
            device_id_type=MESH,
        )

    def begin(self):
        self.take(0, 2)
        for kind in (2, 3):
            self.copy(kind).start()

    def middle(self):
        for kind in (2, 3):
            shift = 1 if kind == 2 else -1
            self.take(kind - 1, shift)
            self.copy(kind).wait_recv()
            rows = pl.ds((kind - 2) * self.half_rows, self.half_rows)
            self.w[self.keep, wrap(self.z + shift), rows, :] += self.half_in[kind - 2]
            self.copy(kind - 2).start()
        self.take(3, 0)

    def finish(self):
        for kind in (0, 1):
            self.copy(kind).wait_recv()
        return self.w[self.keep, self.z] + self.whole_in[0] + self.whole_in[1]

    def drain(self):
        for kind in range(4):
            self.copy(kind).wait_send()
        for turn, shift in enumerate((2, 1, 3, 0)):
            self.swap(turn, shift).wait_send()


TURNS = (3, 2, 4, 1)


def shift_of(step):
    return 2 - step + 3 * (step // 2) - 2 * (step // 3)


def stream(count, loads, work):
    for copy in loads(0, 0):
        copy.start()

    def one(i, carry):
        slot = lax.rem(i, 2)

        @pl.when(i + 1 < count)
        def _():
            for copy in loads(i + 1, 1 - slot):
                copy.start()

        for copy in loads(i, slot):
            copy.wait()
        work(i, slot)
        return carry

    lax.fori_loop(0, count, one, 0)


def reduce_kernel(
    dq_ref,
    att_ref,
    inst_ref,
    dk_hbm,
    dv_hbm,
    hid_hbm,
    cot_hbm,
    nei_hbm,
    wq_hbm,
    wk_hbm,
    wv_hbm,
    gh_ref,
    came_ref,
    gq_ref,
    go_ref,
    gk_ref,
    gv_ref,
    dq_two,
    att_two,
    gpart,
    dpart,
    ghalf,
    gquarter,
    gacross,
    dhalf,
    dquarter,
    w_tile,
    tile,
    near_tile,
    dk_tile,
    dv_tile,
    wk,
    wv,
    going,
    mine,
    out_w,
    out_near,
    out_whole,
    out_half,
    in_w,
    in_near,
    in_whole,
    in_half,
    kv_w,
    kv_near,
    kv_whole,
    kv_half,
    gq_done,
    go_done,
    g_send,
    g_recv,
    d_send,
    d_recv,
    out_send,
    out_recv,
    in_send,
    in_recv,
    kv_send,
    kv_recv,
    pair_send,
    pair_recv,
    swap_send,
    swap_recv,
    load_sem,
    tile_sem,
    near_sem,
):
    place = Place()
    x, y = place.x, place.y
    width = dq_ref.shape[1]
    piece_rows = going.shape[2]
    groups, cap = going.shape[:2]
    rows, enc = dpart.shape[2:]
    weights = [
        pltpu.make_async_copy(wk_hbm, wk, load_sem.at[1]),
        pltpu.make_async_copy(wv_hbm, wv, load_sem.at[2]),
    ]
    for copy in weights:
        copy.start()
    right = pl.ds(width, width)
    halves = [
        partner_copy(place, dq_ref, dq_two.at[:, right], pair_send.at[0], pair_recv.at[0]),
        partner_copy(place, att_ref, att_two.at[:, right], pair_send.at[1], pair_recv.at[1]),
    ]
    greet(place, True)
    for copy in halves:
        copy.start()
    dq_two[:, :width] = dq_ref[...]
    att_two[:, :width] = att_ref[...]
    core = lax.rem(lax.axis_index("wide"), 2)
    keep = lax.rem(core + place.set, 2)
    wide_sum = SetReduce(place, gpart, ghalf, gquarter, gacross, g_send, g_recv)
    near_sum = Reduce(place, dpart, dhalf, dquarter, d_send, d_recv)
    out_ring = Ring(out_w, out_near, out_whole, out_half, out_send, out_recv, keep)
    in_ring = Ring(in_w, in_near, in_whole, in_half, in_send, in_recv, keep)
    kv_ring = Ring(kv_w, kv_near, kv_whole, kv_half, kv_send, kv_recv, core)

    def dot(a, b, ca, cb):
        return lax.dot_general(
            a, b, (((ca,), (cb,)), ((), ())), precision=MID, preferred_element_type=jnp.float32
        )

    def g_load(i, slot):
        block = wq_hbm.at[wrap(x + shift_of(i // 2)), lax.rem(i, 2)]
        return [pltpu.make_async_copy(block, w_tile.at[slot], tile_sem.at[slot])]

    def g_work(i, slot):
        shift = shift_of(i // 2)
        gpart[wrap(x + shift), lax.rem(i, 2)] = dot(dq_two[...], w_tile[slot], 1, 1)

        @pl.when(i == 1)
        def _():
            wide_sum.begin(1)
            wide_sum.begin(2)

        @pl.when(lax.rem(i, 2) == 1)
        def _():
            wide_sum.across(shift).start()

    def weight_grad(source, two_ref, ring):
        def load(i, slot):
            block = source.at[wrap(ring.z + shift_of(i // 2)), lax.rem(i, 2)]
            return [pltpu.make_async_copy(block, tile.at[slot], tile_sem.at[slot])]

        def work(i, slot):
            shift, u = shift_of(i // 2), lax.rem(i, 2)
            part = pl.ds(pl.multiple_of(u * width, width), width)
            both = dot(tile[slot], two_ref[...], 0, 0)
            ring.w[0, wrap(ring.z + shift), part, :] = both[:, :width]
            ring.w[1, wrap(ring.z + shift), part, :] = both[:, width:]

            @pl.when(u == 1)
            def _():
                ring.swap(i // 2, shift).start()

        stream(2 * SIDE, load, work)

    def handed(which, done, out_ref):
        return partner_copy(
            place, done, out_ref, pair_send.at[2 + which], pair_recv.at[2 + which], True
        )

    def deliver(which, ring, done, out_ref):
        done[...] = ring.finish()

        @pl.when(keep == 0)
        def _():
            out_ref[...] = done[...]

        @pl.when(keep == 1)
        def _():
            handed(which, done, out_ref).start()

    def delivered(which, done, out_ref):
        @pl.when(keep == 1)
        def _():
            handed(which, done, out_ref).wait()

    def near_load(sources):
        def load(i, slot):
            at = (wrap(x + shift_of(i // 2)), pl.ds(2 * lax.rem(i, 2), 2))
            return [
                pltpu.make_async_copy(source.at[at], buf.at[slot], near_sem.at[2 * which + slot])
                for which, (source, buf) in enumerate(sources)
            ]

        return load

    def d_work(i, slot):
        shift = shift_of(i // 2)
        bx, by = wrap(x + shift), 2 * lax.rem(i, 2)
        dk = dk_tile[slot].reshape(2 * rows, width)
        dv = dv_tile[slot].reshape(2 * rows, width)
        dpart[bx, pl.ds(by, 2)] = (dot(dk, wk[...], 1, 1) + dot(dv, wv[...], 1, 1)).reshape(
            2, rows, enc
        )

        @pl.when(i == 1)
        def _():
            for turn in TURNS:
                near_sum.begin(1, turn)

        @pl.when(lax.rem(i, 2) == 1)
        def _():
            near_sum.begin(0, shift + 1)

    def neighbour_grad():
        for copy in weights:
            copy.wait()
        stream(2 * SIDE, near_load(((dk_hbm, dk_tile), (dv_hbm, dv_tile))), d_work)

    def kv_work(i, slot):
        dk = dk_tile[slot].reshape(2 * rows, width)
        dv = dv_tile[slot].reshape(2 * rows, width)
        near = near_tile[slot].reshape(2 * rows, enc)
        pair = dot(near, jnp.concatenate([dk, dv], axis=1), 0, 0)
        for group in range(groups):
            share = pair[group * kv_w.shape[2] : (group + 1) * kv_w.shape[2]]
            kv_w[group % 2, group // 2] += share

    def kv_grad():
        kv_w[...] = jnp.zeros_like(kv_w)
        stream(
            2 * SIDE, near_load(((dk_hbm, dk_tile), (dv_hbm, dv_tile), (nei_hbm, near_tile))), kv_work
        )
        for turn, shift in enumerate((2, 1, 3, 0)):
            kv_ring.swap(turn, shift).start()

    def near_middle(turn):
        for half in (0, 1):
            near_sum.middle(half, turn)

    def near_finish(turn):
        for half in (0, 1):
            near_sum.finish(half, turn)
        if turn == 3:
            for half in (0, 1):
                near_sum.begin(half, 0)

    neighbour_grad()
    halves[0].wait()
    stream(2 * SIDE, g_load, g_work)
    weight_grad(hid_hbm, dq_two, in_ring)
    wide_sum.middle(1)
    wide_sum.take(2)
    wide_sum.begin(0)
    in_ring.begin()
    halves[1].wait()
    weight_grad(cot_hbm, att_two, out_ring)
    near_middle(3)
    near_middle(4)
    near_middle(2)
    out_ring.begin()
    in_ring.middle()
    kv_grad()
    near_finish(3)
    kv_ring.begin()
    wide_sum.middle(2)
    near_middle(1)
    out_ring.middle()
    near_finish(4)
    deliver(0, in_ring, gq_done, gq_ref)
    near_finish(2)
    near_middle(0)
    wide_sum.take(1)
    wide_sum.take(3)
    kv_ring.middle()
    wide_sum.finish(2)
    wide_sum.across(4).start()
    wide_sum.finish(1)
    near_finish(1)
    deliver(1, out_ring, go_done, go_ref)
    wide_sum.middle(0)
    near_finish(0)
    for i in range(groups * cap):
        mine[i] = dpart[x, y, pl.ds(i * piece_rows, piece_rows), :]
    for slot in range(groups * cap):
        going[slot // cap, slot % cap] = mine[inst_ref[slot]]
    swaps = exchange(going, came_ref, swap_send, swap_recv, load_sem.at[3])
    wide_sum.take(0)
    pair = kv_ring.finish()
    gk_ref[...] = pair[:, :width]
    gv_ref[...] = pair[:, width:]
    wide_sum.take(4)
    wide_sum.finish(0)
    gh_ref[...] = gpart[x, place.member]
    delivered(0, gq_done, gq_ref)
    delivered(1, go_done, go_ref)
    for copy in swaps:
        copy.wait()
    for target in (wide_sum, near_sum, out_ring, in_ring, kv_ring):
        target.drain()


def result_kernel(slot_ref, came_ref, *refs):
    sources, table_ref, results = refs[:5], refs[5], refs[6:]
    for source, result in zip(sources, results):
        result[...] = source[...]
    table_ref[...] = jnp.zeros_like(table_ref)
    cap = came_ref.shape[1]
    for i in range(came_ref.shape[0] * cap):
        slot = slot_ref[i]
        table_ref[slot] += came_ref[i // cap, i % cap]


def vmem(n):
    return [pl.BlockSpec(memory_space=pltpu.VMEM)] * n


def hbm(n):
    return [pl.BlockSpec(memory_space=pl.ANY)] * n


def smem(n):
    return [pl.BlockSpec(memory_space=pltpu.SMEM)] * n


def f32(*shape):
    return jax.ShapeDtypeStruct(shape, jnp.float32)


def gather_call(hidden, cotangent, table, nbr_ids, owner_map, wq, wo, wk, wv, groups):
    tokens, width = hidden.shape
    _, piece_rows, enc = table.shape
    inst = nbr_ids.size // groups
    going = (groups, inst // groups, piece_rows, enc)
    rows = inst * piece_rows
    places = jax.ShapeDtypeStruct((inst,), jnp.int32)
    dma = pltpu.SemaphoreType.DMA
    blocks = (SIDE, 2, tokens, width)
    pairs = (SIDE, 2, width, 2 * width)
    out_shape = [
        f32(*blocks),
        f32(*blocks),
        f32(SIDE, SIDE, rows, enc),
        f32(*pairs),
        places,
        places,
        places,
        f32(tokens, width),
        f32(tokens, width),
        f32(SIDE, SIDE, rows, width),
        f32(SIDE, SIDE, rows, width),
    ]
    scratch = [
        pltpu.VMEM((tokens, 2 * width), jnp.float32),
        pltpu.VMEM((tokens, 2 * width), jnp.float32),
        pltpu.VMEM((tokens, width), jnp.float32),
        pltpu.VMEM((tokens, width), jnp.float32),
        pltpu.VMEM((SIDE, SIDE, rows, width), jnp.float32),
        pltpu.VMEM((SIDE, SIDE, rows, width), jnp.float32),
        pltpu.VMEM(blocks, jnp.float32),
        pltpu.VMEM(blocks, jnp.float32),
        pltpu.VMEM((SIDE, SIDE, rows, enc), jnp.float32),
        pltpu.VMEM(pairs, jnp.float32),
        pltpu.VMEM(pairs, jnp.float32),
        pltpu.VMEM((enc, 2 * width), jnp.float32),
        pltpu.VMEM(going, jnp.float32),
        pltpu.VMEM(going, jnp.float32),
    ]
    scratch += [dma((17,))] * 4 + [dma((40,))] * 2 + [dma((8,))] * 4 + [dma((4,))] * 2
    scratch += [dma((groups,))] * 2 + [dma((8,)), dma((12,))]
    return pl.pallas_call(
        gather_kernel,
        out_shape=out_shape,
        in_specs=hbm(2) + vmem(1) + smem(2) + hbm(4),
        out_specs=hbm(4) + smem(3) + vmem(4),
        scratch_shapes=scratch,
        compiler_params=pltpu.CompilerParams(
            collective_id=0, has_side_effects=True, vmem_limit_bytes=VMEM_LIMIT
        ),
        cost_estimate=pl.CostEstimate(flops=24_000_000_000, bytes_accessed=60_000_000, transcendentals=0),
    )(hidden, cotangent, table, nbr_ids, owner_map, wq, wo, wk, wv)


def reduce_call(dq, att, inst_of, dk, dv, hid, cot, nei, wq, wk, wv, groups):
    tokens, width = dq.shape
    rows = dk.shape[2]
    enc = wk.shape[0]
    slots = inst_of.shape[0]
    cap = slots // groups
    piece_rows = rows // slots
    dma = pltpu.SemaphoreType.DMA
    going = (groups, cap, piece_rows, enc)
    out_rows, enc_rows = 2 * width, enc // groups

    def ring(rows, cols):
        return [
            pltpu.VMEM((*n, r, cols), jnp.float32)
            for n, r in (((2, SIDE), rows), ((SIDE,), rows), ((2,), rows), ((2,), rows // 2))
        ]

    scratch = [
        pltpu.VMEM((tokens, 2 * width), jnp.float32),
        pltpu.VMEM((tokens, 2 * width), jnp.float32),
        pltpu.VMEM((SIDE, 2, tokens, width), jnp.float32),
        pltpu.VMEM((SIDE, SIDE, rows, enc), jnp.float32),
        pltpu.VMEM((6, tokens // 2, width), jnp.float32),
        pltpu.VMEM((6, tokens // 4, width), jnp.float32),
        pltpu.VMEM((5, tokens // 2, width), jnp.float32),
        pltpu.VMEM((20, rows // 2, enc), jnp.float32),
        pltpu.VMEM((20, rows // 4, enc), jnp.float32),
        pltpu.VMEM((2, width, 2 * width), jnp.float32),
        pltpu.VMEM((2, tokens, width), jnp.float32),
        pltpu.VMEM((2, 2, rows, enc), jnp.float32),
        pltpu.VMEM((2, 2, rows, width), jnp.float32),
        pltpu.VMEM((2, 2, rows, width), jnp.float32),
        pltpu.VMEM(wk.shape, jnp.float32),
        pltpu.VMEM(wv.shape, jnp.float32),
        pltpu.VMEM(going, jnp.float32),
        pltpu.VMEM((slots, piece_rows, enc), jnp.float32),
    ]
    scratch += ring(out_rows, width) + ring(out_rows, width) + ring(enc_rows, 2 * width)
    scratch += [pltpu.VMEM((out_rows, width), jnp.float32)] * 2
    scratch += [dma((17,))] * 2 + [dma((40,))] * 2 + [dma((8,))] * 6 + [dma((4,))] * 2
    scratch += [dma((groups,))] * 2 + [dma((4,)), dma((2,)), dma((6,))]
    return pl.pallas_call(
        reduce_kernel,
        out_shape=[
            f32(tokens, width),
            f32(*going),
            f32(out_rows, width),
            f32(out_rows, width),
            f32(enc_rows, width),
            f32(enc_rows, width),
        ],
        in_specs=vmem(2) + smem(1) + hbm(8),
        out_specs=vmem(6),
        scratch_shapes=scratch,
        compiler_params=pltpu.CompilerParams(
            collective_id=1, has_side_effects=True, vmem_limit_bytes=REDUCE_LIMIT
        ),
        cost_estimate=pl.CostEstimate(flops=50_000_000_000, bytes_accessed=60_000_000, transcendentals=0),
    )(dq, att, inst_of, dk, dv, hid, cot, nei, wq, wk, wv)


def body(
    hidden_states, out_cotangent, enc_table, nbr_ids, owner_map, w_query, w_key, w_value, w_out
):
    groups = lax.axis_size("wide")
    width = hidden_states.shape[1]
    query_blocks = w_query.reshape(SIDE, SIDE, width, width)
    out_blocks = w_out.reshape(SIDE, SIDE, width, width)
    hid, cot, nei, query_pair, picks, _, inst_of, attended, d_query, d_keys, d_values = gather_call(
        hidden_states, out_cotangent, enc_table, nbr_ids.T, owner_map, query_blocks, out_blocks,
        w_key, w_value, groups,
    )
    grad_hidden, arrived, grad_query, grad_out, grad_key, grad_value = reduce_call(
        d_query, attended, inst_of, d_keys, d_values, hid, cot, nei, query_pair, w_key, w_value,
        groups,
    )
    sums = (grad_hidden, grad_query, grad_key, grad_value, grad_out)
    grad_table, *sums = pl.pallas_call(
        result_kernel,
        out_shape=[f32(*enc_table.shape)] + [f32(*t.shape) for t in sums],
        in_specs=smem(1) + vmem(6),
        out_specs=vmem(6),
    )(picks, arrived, *sums)
    return (*sums, grad_table)


def solution(mesh):
    placed = (
        P("wide", "narrow"),
        P("wide", "narrow"),
        P("wide", "narrow", None),
        P(),
        P(),
        P(None, "narrow"),
        P(None, "narrow"),
        P(None, "narrow"),
        P(None, "narrow"),
    )
    return jax.shard_map(
        body,
        mesh=mesh,
        in_specs=placed,
        out_specs=(
            P("wide", "narrow"),
            P("wide", "narrow"),
            P("wide", "narrow"),
            P("wide", "narrow"),
            P("wide", "narrow"),
            P("wide", "narrow", None),
        ),
        check_vma=False,
    )
```

```python
import functools

import jax
import jax.numpy as jnp
from jax import lax
from jax.experimental import pallas as pl
from jax.experimental.pallas import tpu as pltpu
from jax.sharding import PartitionSpec as P

HEAD_DIM = 128
SPAN = 64
NEIGH = 2
SIDE = 4
VMEM_LIMIT = 60 * 1024 * 1024
REDUCE_LIMIT = 63 * 1024 * 1024

HIGH = lax.Precision.HIGHEST
MID = lax.Precision.HIGH
MESH = pl.DeviceIdType.MESH


def wrap(value):
    return lax.rem(value + 2 * SIDE, SIDE)


class Place:
    def __init__(self):
        me = lax.axis_index("narrow")
        self.x = me // SIDE
        self.y = lax.rem(me, SIDE)
        self.set = self.y // 2
        self.member = lax.rem(self.y, 2)

    def at(self, dx, dy):
        return {"narrow": wrap(self.x + dx) * SIDE + wrap(self.y + dy)}

    def mate(self):
        return {"narrow": self.x * SIDE + self.y + 1 - 2 * self.member}

    def partner(self):
        return {"narrow": self.x * SIDE + SIDE - 1 - self.y}

    def own(self, half):
        return (self.x, self.y) if half == 0 else (self.y, self.x)

    @staticmethod
    def block(half, first, second):
        return (first, second) if half == 0 else (second, first)

    def device(self, half, first, second):
        bx, by = self.block(half, first, second)
        return {"narrow": bx * SIDE + by}

    def line(self, half, turn, shift):
        first, second = self.own(half)
        if isinstance(turn, int) and turn == 0:
            return wrap(first + shift), second
        return first, wrap(second + shift)


class SetGather:
    def __init__(self, place, buf, send, recv):
        self.place, self.buf, self.send, self.recv = place, buf, send, recv
        self.rows = buf.shape[2] // 2

    def copy(self, slot, bx, member, start, rows, device):
        piece = self.buf.at[bx, member, pl.ds(start, rows)]
        return pltpu.make_async_remote_copy(
            src_ref=piece,
            dst_ref=piece,
            send_sem=self.send.at[slot],
            recv_sem=self.recv.at[slot],
            device_id=device,
            device_id_type=MESH,
        )

    def ring(self, which, kind, arriving=False):
        place = self.place
        member = place.member if which < 2 else 1 - place.member
        ahead = (1, -1, 1, -1)[kind]
        shift = (0, 0, -1, 1)[kind] - (ahead if arriving else 0)
        start = self.rows * (which > 0) + (self.rows // 2 if kind == 3 else 0)
        rows = self.rows if kind < 2 else self.rows // 2
        return self.copy(
            which * 4 + kind, wrap(place.x + shift), member, start, rows, place.at(ahead, 0)
        )

    def across(self, turn, arriving=False):
        place = self.place
        member = 1 - place.member if arriving else place.member
        bx = wrap(place.x + turn)
        start = self.rows if turn == 4 else 0
        return self.copy(12 + turn, bx, member, start, self.rows, place.mate())

    def begin(self, which):
        for kind in (0, 1):
            self.ring(which, kind).start()

    def forward(self, which):
        for kind in (0, 1):
            self.ring(which, kind, True).wait_recv()
            self.ring(which, kind + 2).start()

    def finish(self, which):
        for kind in (2, 3):
            self.ring(which, kind, True).wait_recv()

    def drain(self):
        for which in range(3):
            for kind in range(4):
                self.ring(which, kind).wait_send()
        for turn in range(5):
            self.across(turn).wait_send()


class SetReduce:
    def __init__(self, place, part, whole_in, quarter_in, across_in, send, recv):
        self.place, self.part = place, part
        self.whole_in, self.quarter_in, self.across_in = whole_in, quarter_in, across_in
        self.send, self.recv = send, recv
        self.rows = part.shape[2] // 2

    def ring(self, which, kind):
        place = self.place
        member = place.member if which < 2 else 1 - place.member
        ahead = (1, -1, 1, -1)[kind]
        shift = (1, -1, 2, 2)[kind]
        start = self.rows * (which > 0) + (self.rows // 2 if kind == 3 else 0)
        rows = self.rows if kind < 2 else self.rows // 2
        landing = self.whole_in if kind < 2 else self.quarter_in
        slot = which * 4 + kind
        return pltpu.make_async_remote_copy(
            src_ref=self.part.at[wrap(place.x + shift), member, pl.ds(start, rows)],
            dst_ref=landing.at[which * 2 + kind % 2],
            send_sem=self.send.at[slot],
            recv_sem=self.recv.at[slot],
            device_id=place.at(ahead, 0),
            device_id_type=MESH,
        )

    def across(self, turn):
        place = self.place
        start = self.rows if isinstance(turn, int) and turn == 4 else 0
        return pltpu.make_async_remote_copy(
            src_ref=self.part.at[
                wrap(place.x + turn), 1 - place.member, pl.ds(start, self.rows)
            ],
            dst_ref=self.across_in.at[turn],
            send_sem=self.send.at[12 + turn],
            recv_sem=self.recv.at[12 + turn],
            device_id=place.mate(),
            device_id_type=MESH,
        )

    def take(self, turn):
        self.across(turn).wait_recv()
        rows = pl.ds(self.rows if turn == 4 else 0, self.rows)
        self.part[wrap(self.place.x + turn), self.place.member, rows, :] += self.across_in[turn]

    def begin(self, which):
        for kind in (2, 3):
            self.ring(which, kind).start()

    def middle(self, which):
        member = self.place.member if which < 2 else 1 - self.place.member
        for kind in (2, 3):
            self.ring(which, kind).wait_recv()
            start = self.rows * (which > 0) + (self.rows // 2 if kind == 3 else 0)
            bx = wrap(self.place.x + (1 if kind == 2 else -1))
            self.part[bx, member, pl.ds(start, self.rows // 2), :] += self.quarter_in[
                which * 2 + kind % 2
            ]
            self.ring(which, kind - 2).start()

    def finish(self, which):
        member = self.place.member if which < 2 else 1 - self.place.member
        for kind in (0, 1):
            self.ring(which, kind).wait_recv()
        rows = pl.ds(self.rows * (which > 0), self.rows)
        self.part[self.place.x, member, rows, :] += (
            self.whole_in[which * 2] + self.whole_in[which * 2 + 1]
        )

    def drain(self):
        for which in range(3):
            for kind in range(4):
                self.ring(which, kind).wait_send()
        for turn in range(5):
            self.across(turn).wait_send()


def partner_copy(place, src, dst, send, recv, other_core=False):
    device = place.partner()
    if other_core:
        group = lax.axis_index("wide")
        device = {"wide": group + 1 - 2 * lax.rem(group, 2), **device}
    return pltpu.make_async_remote_copy(
        src_ref=src,
        dst_ref=dst,
        send_sem=send,
        recv_sem=recv,
        device_id=device,
        device_id_type=MESH,
    )


def greet(place, diagonal=False):
    groups = lax.axis_size("wide")
    group = lax.axis_index("wide")
    barrier = pltpu.get_barrier_semaphore()
    for half in (0, 1):
        for shift in (1, -1):
            pl.semaphore_signal(
                barrier,
                inc=1,
                device_id=place.device(half, *place.line(half, 0, shift)),
                device_id_type=MESH,
            )
    for step in range(1, groups):
        pl.semaphore_signal(
            barrier,
            inc=1,
            device_id={"wide": lax.rem(group + step, groups)},
            device_id_type=MESH,
        )
    if diagonal:
        pl.semaphore_signal(
            barrier,
            inc=1,
            device_id={"wide": group + 1 - 2 * lax.rem(group, 2), **place.partner()},
            device_id_type=MESH,
        )
    pl.semaphore_wait(barrier, 4 + groups - 1 + int(diagonal))


def exchange(out_ref, in_ref, send, recv, local):
    groups = lax.axis_size("wide")
    group = lax.axis_index("wide")
    copies = []
    for step in range(1, groups):
        peer = lax.rem(group + step, groups)
        copy = pltpu.make_async_remote_copy(
            src_ref=out_ref.at[peer],
            dst_ref=in_ref.at[group],
            send_sem=send.at[step],
            recv_sem=recv.at[step],
            device_id={"wide": peer},
            device_id_type=MESH,
        )
        copy.start()
        copies.append(copy)
    mine = pltpu.make_async_copy(out_ref.at[group], in_ref.at[group], local)
    mine.start()
    copies.append(mine)
    return copies


class Gather:
    def __init__(self, place, buf, send, recv):
        self.place, self.buf, self.send, self.recv = place, buf, send, recv
        self.rows = buf.shape[2]

    def copy(self, half, turn, kind, block, dest):
        rows = self.rows // 2 if kind < 2 else self.rows // 4
        start = half * (self.rows // 2) + (self.rows // 4 if kind == 3 else 0)
        bx, by = self.place.block(half, *block)
        piece = self.buf.at[bx, by, pl.ds(start, rows)]
        slot = (half * 5 + turn) * 4 + kind
        return pltpu.make_async_remote_copy(
            src_ref=piece,
            dst_ref=piece,
            send_sem=self.send.at[slot],
            recv_sem=self.recv.at[slot],
            device_id=self.place.device(half, *dest),
            device_id_type=MESH,
        )

    def at(self, half, turn, shift):
        first, second = self.place.own(half)
        if isinstance(turn, int) and turn == 0:
            return wrap(first + shift), second
        return wrap(first + turn - 1), wrap(second + shift)

    def along_y(self, half, turn):
        return half == 1 if isinstance(turn, int) and turn == 0 else half == 0

    def describe(self, half, turn, kind):
        shift = (0, 0, -1, 1)[kind]
        ahead = (1, -1, 1, -1)[kind]
        if kind >= 2 and self.along_y(half, turn):
            ahead = 2 * self.place.member - 1
            shift = -ahead
        return self.copy(
            half, turn, kind, self.at(half, turn, shift), self.place.line(half, turn, ahead)
        )

    def arrival(self, half, turn, kind):
        shift = (-1, 1, 2, 2)[kind]
        ahead = (1, -1, 1, -1)[kind]
        return self.copy(
            half, turn, kind, self.at(half, turn, shift), self.place.line(half, turn, ahead)
        )

    def begin(self, half, turn):
        self.describe(half, turn, 0).start()
        self.describe(half, turn, 1).start()

    def forward(self, half, turn):
        if self.along_y(half, turn):
            for kind in (0, 1):
                self.arrival(half, turn, kind).wait_recv()
            for kind in (2, 3):
                self.describe(half, turn, kind).start()
            return
        for kind in (0, 1):
            self.arrival(half, turn, kind).wait_recv()
            self.describe(half, turn, kind + 2).start()

    def finish(self, half, turn):
        for kind in (2, 3):
            self.arrival(half, turn, kind).wait_recv()

    def drain(self):
        for half in (0, 1):
            for turn in range(5):
                for kind in range(4):
                    self.describe(half, turn, kind).wait_send()


def attend(half, q_ref, da_ref, keys_ref, values_ref, att_ref, dq_ref, dk_ref, dv_ref):
    scale = HEAD_DIM ** (-0.5)
    heads = q_ref.shape[1] // HEAD_DIM
    spans = q_ref.shape[0] // SPAN
    few = keys_ref.shape[2] // spans
    near = SIDE * SIDE * few

    def dot(a, b, ca, cb, precision=MID):
        return lax.dot_general(
            a, b, (((ca,), (cb,)), ((), ())), precision=precision,
            preferred_element_type=jnp.float32,
        )

    def span(c, carry):
        rows = pl.ds(pl.multiple_of(c * SPAN, SPAN), SPAN)
        pieces = pl.ds(pl.multiple_of(c * few, few), few)
        for head in range(heads):
            cols = pl.ds(head * HEAD_DIM, HEAD_DIM)
            q = q_ref[rows, cols]
            da = da_ref[rows, cols]
            k = keys_ref[:, :, pieces, cols].reshape(near, HEAD_DIM)
            v = values_ref[:, :, pieces, cols].reshape(near, HEAD_DIM)
            scores = dot(q, k, 1, 1, HIGH) * scale
            dp = dot(da, v, 1, 1)
            top = jnp.max(scores, axis=-1, keepdims=True)
            e = jnp.exp(scores - top)
            probs = e / jnp.sum(e, axis=-1, keepdims=True)
            ds = probs * (dp - jnp.sum(dp * probs, axis=-1, keepdims=True)) * scale
            att_ref[rows, cols] = dot(probs, v, 1, 0)
            dq_ref[rows, cols] = dot(ds, k, 1, 0)
            shape = (SIDE, SIDE, few, HEAD_DIM)
            dk_ref[:, :, pieces, cols] = dot(ds, q, 0, 0).reshape(shape)
            dv_ref[:, :, pieces, cols] = dot(probs, da, 0, 0).reshape(shape)
        return carry

    lax.fori_loop(half * spans // 2, (half + 1) * spans // 2, span, 0)


class Spread:
    def __init__(self, place, source, wide_w, send, recv):
        self.place, self.source, self.w = place, source, wide_w
        self.send, self.recv = send, recv
        self.group = lax.axis_index("wide")
        self.z, self.core = self.group // 2, lax.rem(self.group, 2)
        self.width = source.shape[3]

    def slot(self, group):
        return self.w.at[group // 2, lax.rem(group, 2), :, pl.ds(self.width, self.width)]

    def first(self):
        block = self.source.at[self.z, 2 * (1 - self.place.set) + self.core]
        return partner_copy(
            self.place, block, self.slot(self.group), self.send.at[0], self.recv.at[0]
        )

    def to(self, index, group, target):
        return pltpu.make_async_remote_copy(
            src_ref=self.slot(group),
            dst_ref=self.slot(group),
            send_sem=self.send.at[index],
            recv_sem=self.recv.at[index],
            device_id={"wide": target},
            device_id_type=MESH,
        )

    def along(self, step, arriving=False):
        there = wrap(self.z + step) * 2 + self.core
        back = wrap(self.z - step) * 2 + self.core
        return self.to(step, back if arriving else self.group, there)

    def beside(self, step, arriving=False):
        core = 1 - self.core if arriving else self.core
        other = self.z * 2 + 1 - self.core
        return self.to(4 + step, wrap(self.z - step) * 2 + core, other)

    def spread(self):
        self.first().wait_recv()
        for step in (1, 3, 2):
            self.along(step).start()
        self.beside(0).start()

    def pass_on(self):
        for step in (1, 3, 2):
            self.along(step, True).wait_recv()
            self.beside(step).start()

    def finish(self):
        for step in range(SIDE):
            self.beside(step, True).wait_recv()

    def drain(self):
        self.first().wait_send()
        for step in (1, 2, 3):
            self.along(step).wait_send()
        for step in range(SIDE):
            self.beside(step).wait_send()


def gather_kernel(
    hid_ref,
    cot_ref,
    table_ref,
    nbr_ref,
    map_ref,
    wq_ref,
    wo_ref,
    wk_ref,
    wv_ref,
    hid_out,
    cot_out,
    nei_out,
    wq_out,
    pick_ref,
    slot_ref,
    inst_ref,
    att_ref,
    dq_ref,
    dk_ref,
    dv_ref,
    q_two,
    da_two,
    q_came,
    da_came,
    keys_ref,
    values_ref,
    hid,
    cot,
    nei,
    wq,
    wo,
    wkv,
    going,
    came,
    hid_send,
    hid_recv,
    cot_send,
    cot_recv,
    nei_send,
    nei_recv,
    wq_send,
    wq_recv,
    wo_send,
    wo_recv,
    pair_send,
    pair_recv,
    swap_send,
    swap_recv,
    load_sem,
    store_sem,
):
    place = Place()
    x, y = place.x, place.y
    tokens, width = dq_ref.shape
    groups, cap, piece_rows, _ = came.shape
    inst = nei.shape[2] // piece_rows
    own = [
        pltpu.make_async_copy(hid_ref, hid.at[x, place.member], load_sem.at[0]),
        pltpu.make_async_copy(cot_ref, cot.at[x, place.member], load_sem.at[1]),
    ]
    mine = pl.ds(2 * place.set, 2)
    left = pl.ds(0, width)
    weights = [
        pltpu.make_async_copy(wq_ref.at[:, mine], wq.at[:, :, :, left], load_sem.at[2]),
        pltpu.make_async_copy(wo_ref.at[:, mine], wo.at[:, :, :, left], load_sem.at[3]),
        pltpu.make_async_copy(wk_ref, wkv.at[:, pl.ds(0, width)], load_sem.at[4]),
        pltpu.make_async_copy(wv_ref, wkv.at[:, pl.ds(width, width)], load_sem.at[5]),
    ]
    for copy in own:
        copy.start()
    greet(place)
    for copy in own:
        copy.wait()
    pair = [
        SetGather(place, hid, hid_send, hid_recv),
        SetGather(place, cot, cot_send, cot_recv),
    ]
    near = Gather(place, nei, nei_send, nei_recv)
    spreads = [
        Spread(place, wq_ref, wq, wq_send, wq_recv),
        Spread(place, wo_ref, wo, wo_send, wo_recv),
    ]
    hid_set, cot_set = pair

    group = lax.axis_index("wide")
    stored = table_ref.shape[0]

    def stored_at(g, i):
        return map_ref[nbr_ref[i % NEIGH, g * (inst // NEIGH) + i // NEIGH]]

    def offer():
        def one(g, carry):
            count = jnp.int32(0)
            chosen = [jnp.int32(0)] * cap
            for i in range(inst):
                at = stored_at(g, i) - group * stored
                hit = (at >= 0) & (at < stored)
                chosen = [
                    jnp.where(hit & (count == r), at, old) for r, old in enumerate(chosen)
                ]
                count = count + hit.astype(jnp.int32)
            for r in range(cap):
                pick_ref[g * cap + r] = chosen[r]
                going[g, r] = table_ref[chosen[r]]
            return carry

        lax.fori_loop(0, groups, one, 0)
        return exchange(going, came, swap_send, swap_recv, load_sem.at[6])

    def places():
        owners = [lax.div(stored_at(group, i), stored) for i in range(inst)]
        slots = [
            owner * cap + sum((owners[j] == owner).astype(jnp.int32) for j in range(i))
            for i, owner in enumerate(owners)
        ]
        for i in range(inst):
            slot_ref[i] = slots[i]

        def one(slot, carry):
            inst_ref[slot] = sum(jnp.where(slot_ref[i] == slot, i, 0) for i in range(inst))
            return carry

        lax.fori_loop(0, inst, one, 0)

    def accept(swaps):
        for copy in swaps:
            copy.wait()
        for i in range(inst):
            slot = slot_ref[i]
            nei[x, y, pl.ds(i * piece_rows, piece_rows), :] = came[
                slot // cap, lax.rem(slot, cap)
            ]

    def set_forward(gather):
        gather.forward(0)
        gather.across(1).start()
        gather.across(3).start()

    def set_other(gather):
        gather.across(4, True).wait_recv()
        gather.begin(2)

    def set_finish(gather):
        gather.finish(0)
        gather.across(2).start()

    def add_products(gather, half, bx):
        rows = pl.ds(half * (tokens // 2), tokens // 2)
        total, weight, precision = (
            (q_two, wq, HIGH) if gather is hid_set else (da_two, wo, MID)
        )

        def column(member, carry):
            total[rows, :] += jnp.dot(
                gather.buf[bx, member, rows, :], weight[bx, member], precision=precision,
                preferred_element_type=jnp.float32,
            )
            return carry

        lax.fori_loop(0, 2, column, 0)

    def project(gather, half):
        if half == 0:
            for turn in (0, 1, 3, 2):
                gather.across(turn, True).wait_recv()
                add_products(gather, 0, wrap(x + turn))
            return
        gather.finish(1)
        gather.finish(2)

        def block(bx, carry):
            add_products(gather, 1, bx)
            return carry

        lax.fori_loop(0, SIDE, block, 0)

    def half_copy(gather, half):
        rows = pl.ds(half * (tokens // 2), tokens // 2)
        total, came_ref = (q_two, q_came) if gather is hid_set else (da_two, da_came)
        sem = half + 2 * int(gather is cot_set)
        return partner_copy(
            place,
            total.at[rows, pl.ds(width, width)],
            came_ref.at[rows],
            pair_send.at[sem],
            pair_recv.at[sem],
        )

    def add_half(gather, half):
        half_copy(gather, half).wait_recv()
        rows = pl.ds(half * (tokens // 2), tokens // 2)
        total, came_ref = (q_two, q_came) if gather is hid_set else (da_two, da_came)
        came_ref[rows, :] += total[rows, :width]

    def near_keep(half, turn):
        first = wrap(place.own(half)[0] + turn - 1)
        rows = pl.ds(half * (nei.shape[2] // 2), nei.shape[2] // 2)
        at = (first, slice(None), rows) if half == 0 else (slice(None), first, rows)
        return pltpu.make_async_copy(nei.at[at], nei_out.at[at], store_sem.at[2 + half * 5 + turn])

    def near_project(half, turn):
        near.finish(half, turn)
        near_keep(half, turn).start()
        first = wrap(place.own(half)[0] + turn - 1)
        few = nei.shape[2] // 2
        rows = pl.ds(half * few, few)
        if half == 0:
            blocks = nei[first, :, rows, :]
        else:
            blocks = nei[:, first, rows, :]
        flat = blocks.reshape(SIDE * few, nei.shape[3])
        keys = jnp.dot(
            flat, wkv[:, :width], precision=HIGH, preferred_element_type=jnp.float32
        ).reshape(SIDE, few, width)
        values = jnp.dot(
            flat, wkv[:, width:], precision=MID, preferred_element_type=jnp.float32
        ).reshape(SIDE, few, width)
        if half == 0:
            keys_ref[first, :, rows, :] = keys
            values_ref[first, :, rows, :] = values
        else:
            keys_ref[:, first, rows, :] = keys
            values_ref[:, first, rows, :] = values

    def near_begin(turn):
        for half in (0, 1):
            near.begin(half, turn)

    attended = (q_came, da_came, keys_ref, values_ref, att_ref, dq_ref, dk_ref, dv_ref)

    cot_set.begin(0)
    for spread in spreads:
        spread.first().start()
    cot_set.across(0).start()
    cot_set.begin(1)
    cot_set.across(4).start()
    swaps = offer()
    places()
    for copy in weights:
        copy.start()
    q_two[...] = jnp.zeros_like(q_two)
    da_two[...] = jnp.zeros_like(da_two)
    accept(swaps)
    set_forward(cot_set)
    set_other(cot_set)
    near_begin(0)
    hid_set.across(4).start()
    for spread in spreads:
        spread.spread()
    near_begin(1)
    hid_set.begin(0)
    for half in (0, 1):
        near.forward(half, 0)
    near_begin(2)
    near_begin(4)
    hid_set.begin(1)
    set_other(hid_set)
    set_forward(hid_set)
    for spread in spreads:
        spread.pass_on()
    cot_set.forward(2)
    cot_set.forward(1)
    near.forward(0, 1)
    near.forward(0, 4)
    near.forward(1, 1)
    for copy in weights:
        copy.wait()
    near_project(0, 4)
    set_finish(cot_set)
    near.forward(0, 2)
    near_project(0, 1)
    hid_set.forward(1)
    for spread in spreads:
        spread.finish()
    keep_weights = pltpu.make_async_copy(wq, wq_out, load_sem.at[7])
    keep_weights.start()
    hid_set.forward(2)
    for half in (0, 1):
        near.finish(half, 0)
    near_begin(3)
    near.forward(1, 4)
    project(cot_set, 0)
    hid_set.across(0).start()
    half_copy(cot_set, 0).start()
    project(cot_set, 1)
    half_copy(cot_set, 1).start()
    keep_cot = pltpu.make_async_copy(cot, cot_out, store_sem.at[1])
    keep_cot.start()
    near_project(1, 1)
    set_finish(hid_set)
    near_project(0, 2)
    project(hid_set, 1)
    half_copy(hid_set, 1).start()
    near.forward(1, 2)
    project(hid_set, 0)
    near.forward(0, 3)
    near.forward(1, 3)
    half_copy(hid_set, 0).start()
    keep_hid = pltpu.make_async_copy(hid, hid_out, store_sem.at[0])
    keep_hid.start()
    near_project(1, 4)
    near_project(1, 2)
    add_half(cot_set, 1)
    near_project(1, 3)
    add_half(cot_set, 0)
    add_half(hid_set, 1)
    attend(1, *attended)
    near_project(0, 3)
    add_half(hid_set, 0)
    attend(0, *attended)
    for target in (*pair, near, *spreads):
        target.drain()
    for gather in pair:
        for half in (0, 1):
            half_copy(gather, half).wait_send()
    for copy in (keep_weights, keep_hid, keep_cot):
        copy.wait()
    for half in (0, 1):
        for turn in range(1, SIDE + 1):
            near_keep(half, turn).wait()


class Reduce:
    def __init__(self, place, part, whole_in, quarter_in, send, recv):
        self.place, self.part = place, part
        self.whole_in, self.quarter_in = whole_in, quarter_in
        self.send, self.recv = send, recv
        self.rows = part.shape[2]

    def at(self, half, turn, shift):
        first, second = self.place.own(half)
        if isinstance(turn, int) and turn == 0:
            return wrap(first + shift), second
        return wrap(first + turn - 1), wrap(second + shift)

    def piece(self, half, block, kind):
        rows = self.rows // 2 if kind < 2 else self.rows // 4
        start = half * (self.rows // 2) + (self.rows // 4 if kind == 3 else 0)
        bx, by = self.place.block(half, *block)
        return bx, by, pl.ds(start, rows)

    def copy(self, half, turn, kind):
        ahead = (1, -1, 1, -1)[kind]
        shift = (1, -1, 2, 2)[kind]
        slot = (half * 5 + turn) * 2 + kind % 2
        landing = (self.whole_in if kind < 2 else self.quarter_in).at[slot]
        bx, by, rows = self.piece(half, self.at(half, turn, shift), kind)
        sem = (half * 5 + turn) * 4 + kind
        return pltpu.make_async_remote_copy(
            src_ref=self.part.at[bx, by, rows],
            dst_ref=landing,
            send_sem=self.send.at[sem],
            recv_sem=self.recv.at[sem],
            device_id=self.place.device(half, *self.place.line(half, turn, ahead)),
            device_id_type=MESH,
        )

    def begin(self, half, turn):
        for kind in (2, 3):
            self.copy(half, turn, kind).start()

    def middle(self, half, turn):
        for kind in (2, 3):
            self.copy(half, turn, kind).wait_recv()
            slot = (half * 5 + turn) * 2 + kind % 2
            shift = 1 if kind == 2 else -1
            bx, by, rows = self.piece(half, self.at(half, turn, shift), kind)
            self.part[bx, by, rows, :] += self.quarter_in[slot]
            self.copy(half, turn, kind - 2).start()

    def finish(self, half, turn):
        for kind in (0, 1):
            self.copy(half, turn, kind).wait_recv()
        slot = (half * 5 + turn) * 2
        bx, by, rows = self.piece(half, self.at(half, turn, 0), 0)
        self.part[bx, by, rows, :] += self.whole_in[slot] + self.whole_in[slot + 1]

    def drain(self):
        for half in (0, 1):
            for turn in range(5):
                for kind in range(4):
                    self.copy(half, turn, kind).wait_send()


class Ring:
    def __init__(self, w, near_in, whole_in, half_in, send, recv, keep):
        group = lax.axis_index("wide")
        self.z, self.core, self.keep = group // 2, lax.rem(group, 2), keep
        self.w, self.near_in, self.whole_in, self.half_in = w, near_in, whole_in, half_in
        self.send, self.recv = send, recv
        self.half_rows = w.shape[2] // 2

    def swap(self, turn, shift):
        to = wrap(self.z + shift)
        return pltpu.make_async_remote_copy(
            src_ref=self.w.at[1 - self.keep, to],
            dst_ref=self.near_in.at[to],
            send_sem=self.send.at[4 + turn],
            recv_sem=self.recv.at[4 + turn],
            device_id={"wide": self.z * 2 + 1 - self.core},
            device_id_type=MESH,
        )

    def take(self, turn, shift):
        self.swap(turn, shift).wait_recv()
        to = wrap(self.z + shift)
        self.w[self.keep, to] += self.near_in[to]

    def copy(self, kind):
        ahead = (1, -1, 1, -1)[kind]
        shift = (1, -1, 2, 2)[kind]
        source = self.w.at[self.keep, wrap(self.z + shift)]
        landing = self.whole_in
        if kind >= 2:
            source = source.at[pl.ds((kind - 2) * self.half_rows, self.half_rows)]
            landing = self.half_in
        return pltpu.make_async_remote_copy(
            src_ref=source,
            dst_ref=landing.at[kind % 2],
            send_sem=self.send.at[kind],
            recv_sem=self.recv.at[kind],
            device_id={"wide": wrap(self.z + ahead) * 2 + self.core},
            device_id_type=MESH,
        )

    def begin(self):
        self.take(0, 2)
        for kind in (2, 3):
            self.copy(kind).start()

    def middle(self):
        for kind in (2, 3):
            shift = 1 if kind == 2 else -1
            self.take(kind - 1, shift)
            self.copy(kind).wait_recv()
            rows = pl.ds((kind - 2) * self.half_rows, self.half_rows)
            self.w[self.keep, wrap(self.z + shift), rows, :] += self.half_in[kind - 2]
            self.copy(kind - 2).start()
        self.take(3, 0)

    def finish(self):
        for kind in (0, 1):
            self.copy(kind).wait_recv()
        return self.w[self.keep, self.z] + self.whole_in[0] + self.whole_in[1]

    def drain(self):
        for kind in range(4):
            self.copy(kind).wait_send()
        for turn, shift in enumerate((2, 1, 3, 0)):
            self.swap(turn, shift).wait_send()


TURNS = (3, 2, 4, 1)


def shift_of(step):
    return 2 - step + 3 * (step // 2) - 2 * (step // 3)


def stream(count, loads, work):
    for copy in loads(0, 0):
        copy.start()

    def one(i, carry):
        slot = lax.rem(i, 2)

        @pl.when(i + 1 < count)
        def _():
            for copy in loads(i + 1, 1 - slot):
                copy.start()

        for copy in loads(i, slot):
            copy.wait()
        work(i, slot)
        return carry

    lax.fori_loop(0, count, one, 0)


def reduce_kernel(
    dq_ref,
    att_ref,
    inst_ref,
    dk_hbm,
    dv_hbm,
    hid_hbm,
    cot_hbm,
    nei_hbm,
    wq_hbm,
    wk_hbm,
    wv_hbm,
    gh_ref,
    came_ref,
    gq_ref,
    go_ref,
    gk_ref,
    gv_ref,
    dq_two,
    att_two,
    gpart,
    dpart,
    ghalf,
    gquarter,
    gacross,
    dhalf,
    dquarter,
    w_tile,
    tile,
    near_tile,
    dk_tile,
    dv_tile,
    wk,
    wv,
    going,
    mine,
    out_w,
    out_near,
    out_whole,
    out_half,
    in_w,
    in_near,
    in_whole,
    in_half,
    kv_w,
    kv_near,
    kv_whole,
    kv_half,
    gq_done,
    go_done,
    g_send,
    g_recv,
    d_send,
    d_recv,
    out_send,
    out_recv,
    in_send,
    in_recv,
    kv_send,
    kv_recv,
    pair_send,
    pair_recv,
    swap_send,
    swap_recv,
    load_sem,
    tile_sem,
    near_sem,
):
    place = Place()
    x, y = place.x, place.y
    width = dq_ref.shape[1]
    piece_rows = going.shape[2]
    groups, cap = going.shape[:2]
    rows, enc = dpart.shape[2:]
    weights = [
        pltpu.make_async_copy(wk_hbm, wk, load_sem.at[1]),
        pltpu.make_async_copy(wv_hbm, wv, load_sem.at[2]),
    ]
    for copy in weights:
        copy.start()
    right = pl.ds(width, width)
    halves = [
        partner_copy(place, dq_ref, dq_two.at[:, right], pair_send.at[0], pair_recv.at[0]),
        partner_copy(place, att_ref, att_two.at[:, right], pair_send.at[1], pair_recv.at[1]),
    ]
    greet(place, True)
    for copy in halves:
        copy.start()
    dq_two[:, :width] = dq_ref[...]
    att_two[:, :width] = att_ref[...]
    core = lax.rem(lax.axis_index("wide"), 2)
    keep = lax.rem(core + place.set, 2)
    wide_sum = SetReduce(place, gpart, ghalf, gquarter, gacross, g_send, g_recv)
    near_sum = Reduce(place, dpart, dhalf, dquarter, d_send, d_recv)
    out_ring = Ring(out_w, out_near, out_whole, out_half, out_send, out_recv, keep)
    in_ring = Ring(in_w, in_near, in_whole, in_half, in_send, in_recv, keep)
    kv_ring = Ring(kv_w, kv_near, kv_whole, kv_half, kv_send, kv_recv, core)

    def dot(a, b, ca, cb):
        return lax.dot_general(
            a, b, (((ca,), (cb,)), ((), ())), precision=MID, preferred_element_type=jnp.float32
        )

    def g_load(i, slot):
        block = wq_hbm.at[wrap(x + shift_of(i // 2)), lax.rem(i, 2)]
        return [pltpu.make_async_copy(block, w_tile.at[slot], tile_sem.at[slot])]

    def g_work(i, slot):
        shift = shift_of(i // 2)
        gpart[wrap(x + shift), lax.rem(i, 2)] = dot(dq_two[...], w_tile[slot], 1, 1)

        @pl.when(i == 1)
        def _():
            wide_sum.begin(1)
            wide_sum.begin(2)

        @pl.when(lax.rem(i, 2) == 1)
        def _():
            wide_sum.across(shift).start()

    def weight_grad(source, two_ref, ring):
        def load(i, slot):
            block = source.at[wrap(ring.z + shift_of(i // 2)), lax.rem(i, 2)]
            return [pltpu.make_async_copy(block, tile.at[slot], tile_sem.at[slot])]

        def work(i, slot):
            shift, u = shift_of(i // 2), lax.rem(i, 2)
            part = pl.ds(pl.multiple_of(u * width, width), width)
            both = dot(tile[slot], two_ref[...], 0, 0)
            ring.w[0, wrap(ring.z + shift), part, :] = both[:, :width]
            ring.w[1, wrap(ring.z + shift), part, :] = both[:, width:]

            @pl.when(u == 1)
            def _():
                ring.swap(i // 2, shift).start()

        stream(2 * SIDE, load, work)

    def handed(which, done, out_ref):
        return partner_copy(
            place, done, out_ref, pair_send.at[2 + which], pair_recv.at[2 + which], True
        )

    def deliver(which, ring, done, out_ref):
        done[...] = ring.finish()

        @pl.when(keep == 0)
        def _():
            out_ref[...] = done[...]

        @pl.when(keep == 1)
        def _():
            handed(which, done, out_ref).start()

    def delivered(which, done, out_ref):
        @pl.when(keep == 1)
        def _():
            handed(which, done, out_ref).wait()

    def near_load(sources):
        def load(i, slot):
            at = (wrap(x + shift_of(i // 2)), pl.ds(2 * lax.rem(i, 2), 2))
            return [
                pltpu.make_async_copy(source.at[at], buf.at[slot], near_sem.at[2 * which + slot])
                for which, (source, buf) in enumerate(sources)
            ]

        return load

    def d_work(i, slot):
        shift = shift_of(i // 2)
        bx, by = wrap(x + shift), 2 * lax.rem(i, 2)
        dk = dk_tile[slot].reshape(2 * rows, width)
        dv = dv_tile[slot].reshape(2 * rows, width)
        dpart[bx, pl.ds(by, 2)] = (dot(dk, wk[...], 1, 1) + dot(dv, wv[...], 1, 1)).reshape(
            2, rows, enc
        )

        @pl.when(i == 1)
        def _():
            for turn in TURNS:
                near_sum.begin(1, turn)

        @pl.when(lax.rem(i, 2) == 1)
        def _():
            near_sum.begin(0, shift + 1)

    def neighbour_grad():
        for copy in weights:
            copy.wait()
        stream(2 * SIDE, near_load(((dk_hbm, dk_tile), (dv_hbm, dv_tile))), d_work)

    def kv_work(i, slot):
        dk = dk_tile[slot].reshape(2 * rows, width)
        dv = dv_tile[slot].reshape(2 * rows, width)
        near = near_tile[slot].reshape(2 * rows, enc)
        pair = dot(near, jnp.concatenate([dk, dv], axis=1), 0, 0)
        for group in range(groups):
            share = pair[group * kv_w.shape[2] : (group + 1) * kv_w.shape[2]]
            kv_w[group % 2, group // 2] += share

    def kv_grad():
        kv_w[...] = jnp.zeros_like(kv_w)
        stream(
            2 * SIDE, near_load(((dk_hbm, dk_tile), (dv_hbm, dv_tile), (nei_hbm, near_tile))), kv_work
        )
        for turn, shift in enumerate((2, 1, 3, 0)):
            kv_ring.swap(turn, shift).start()

    def near_middle(turn):
        for half in (0, 1):
            near_sum.middle(half, turn)

    def near_finish(turn):
        for half in (0, 1):
            near_sum.finish(half, turn)
        if turn == 3:
            for half in (0, 1):
                near_sum.begin(half, 0)

    neighbour_grad()
    halves[0].wait()
    stream(2 * SIDE, g_load, g_work)
    weight_grad(hid_hbm, dq_two, in_ring)
    wide_sum.middle(1)
    wide_sum.take(2)
    wide_sum.begin(0)
    in_ring.begin()
    halves[1].wait()
    weight_grad(cot_hbm, att_two, out_ring)
    near_middle(3)
    near_middle(4)
    near_middle(2)
    out_ring.begin()
    in_ring.middle()
    kv_grad()
    near_finish(3)
    kv_ring.begin()
    wide_sum.middle(2)
    near_middle(1)
    out_ring.middle()
    near_finish(4)
    deliver(0, in_ring, gq_done, gq_ref)
    near_finish(2)
    near_middle(0)
    wide_sum.take(1)
    wide_sum.take(3)
    kv_ring.middle()
    wide_sum.finish(2)
    wide_sum.across(4).start()
    wide_sum.finish(1)
    near_finish(1)
    deliver(1, out_ring, go_done, go_ref)
    wide_sum.middle(0)
    near_finish(0)
    for i in range(groups * cap):
        mine[i] = dpart[x, y, pl.ds(i * piece_rows, piece_rows), :]
    for slot in range(groups * cap):
        going[slot // cap, slot % cap] = mine[inst_ref[slot]]
    swaps = exchange(going, came_ref, swap_send, swap_recv, load_sem.at[3])
    wide_sum.take(0)
    pair = kv_ring.finish()
    gk_ref[...] = pair[:, :width]
    gv_ref[...] = pair[:, width:]
    wide_sum.take(4)
    wide_sum.finish(0)
    gh_ref[...] = gpart[x, place.member]
    delivered(0, gq_done, gq_ref)
    delivered(1, go_done, go_ref)
    for copy in swaps:
        copy.wait()
    for target in (wide_sum, near_sum, out_ring, in_ring, kv_ring):
        target.drain()


def result_kernel(slot_ref, came_ref, *refs):
    sources, table_ref, results = refs[:5], refs[5], refs[6:]
    for source, result in zip(sources, results):
        result[...] = source[...]
    table_ref[...] = jnp.zeros_like(table_ref)
    cap = came_ref.shape[1]
    for i in range(came_ref.shape[0] * cap):
        slot = slot_ref[i]
        table_ref[slot] += came_ref[i // cap, i % cap]


def vmem(n):
    return [pl.BlockSpec(memory_space=pltpu.VMEM)] * n


def hbm(n):
    return [pl.BlockSpec(memory_space=pl.ANY)] * n


def smem(n):
    return [pl.BlockSpec(memory_space=pltpu.SMEM)] * n


def f32(*shape):
    return jax.ShapeDtypeStruct(shape, jnp.float32)


def gather_call(hidden, cotangent, table, nbr_ids, owner_map, wq, wo, wk, wv, groups):
    tokens, width = hidden.shape
    _, piece_rows, enc = table.shape
    inst = nbr_ids.size // groups
    going = (groups, inst // groups, piece_rows, enc)
    rows = inst * piece_rows
    places = jax.ShapeDtypeStruct((inst,), jnp.int32)
    dma = pltpu.SemaphoreType.DMA
    blocks = (SIDE, 2, tokens, width)
    pairs = (SIDE, 2, width, 2 * width)
    out_shape = [
        f32(*blocks),
        f32(*blocks),
        f32(SIDE, SIDE, rows, enc),
        f32(*pairs),
        places,
        places,
        places,
        f32(tokens, width),
        f32(tokens, width),
        f32(SIDE, SIDE, rows, width),
        f32(SIDE, SIDE, rows, width),
    ]
    scratch = [
        pltpu.VMEM((tokens, 2 * width), jnp.float32),
        pltpu.VMEM((tokens, 2 * width), jnp.float32),
        pltpu.VMEM((tokens, width), jnp.float32),
        pltpu.VMEM((tokens, width), jnp.float32),
        pltpu.VMEM((SIDE, SIDE, rows, width), jnp.float32),
        pltpu.VMEM((SIDE, SIDE, rows, width), jnp.float32),
        pltpu.VMEM(blocks, jnp.float32),
        pltpu.VMEM(blocks, jnp.float32),
        pltpu.VMEM((SIDE, SIDE, rows, enc), jnp.float32),
        pltpu.VMEM(pairs, jnp.float32),
        pltpu.VMEM(pairs, jnp.float32),
        pltpu.VMEM((enc, 2 * width), jnp.float32),
        pltpu.VMEM(going, jnp.float32),
        pltpu.VMEM(going, jnp.float32),
    ]
    scratch += [dma((17,))] * 4 + [dma((40,))] * 2 + [dma((8,))] * 4 + [dma((4,))] * 2
    scratch += [dma((groups,))] * 2 + [dma((8,)), dma((12,))]
    return pl.pallas_call(
        gather_kernel,
        out_shape=out_shape,
        in_specs=hbm(2) + vmem(1) + smem(2) + hbm(4),
        out_specs=hbm(4) + smem(3) + vmem(4),
        scratch_shapes=scratch,
        compiler_params=pltpu.CompilerParams(
            collective_id=0, has_side_effects=True, vmem_limit_bytes=VMEM_LIMIT
        ),
        cost_estimate=pl.CostEstimate(flops=24_000_000_000, bytes_accessed=60_000_000, transcendentals=0),
    )(hidden, cotangent, table, nbr_ids, owner_map, wq, wo, wk, wv)


def reduce_call(dq, att, inst_of, dk, dv, hid, cot, nei, wq, wk, wv, groups):
    tokens, width = dq.shape
    rows = dk.shape[2]
    enc = wk.shape[0]
    slots = inst_of.shape[0]
    cap = slots // groups
    piece_rows = rows // slots
    dma = pltpu.SemaphoreType.DMA
    going = (groups, cap, piece_rows, enc)
    out_rows, enc_rows = 2 * width, enc // groups

    def ring(rows, cols):
        return [
            pltpu.VMEM((*n, r, cols), jnp.float32)
            for n, r in (((2, SIDE), rows), ((SIDE,), rows), ((2,), rows), ((2,), rows // 2))
        ]

    scratch = [
        pltpu.VMEM((tokens, 2 * width), jnp.float32),
        pltpu.VMEM((tokens, 2 * width), jnp.float32),
        pltpu.VMEM((SIDE, 2, tokens, width), jnp.float32),
        pltpu.VMEM((SIDE, SIDE, rows, enc), jnp.float32),
        pltpu.VMEM((6, tokens // 2, width), jnp.float32),
        pltpu.VMEM((6, tokens // 4, width), jnp.float32),
        pltpu.VMEM((5, tokens // 2, width), jnp.float32),
        pltpu.VMEM((20, rows // 2, enc), jnp.float32),
        pltpu.VMEM((20, rows // 4, enc), jnp.float32),
        pltpu.VMEM((2, width, 2 * width), jnp.float32),
        pltpu.VMEM((2, tokens, width), jnp.float32),
        pltpu.VMEM((2, 2, rows, enc), jnp.float32),
        pltpu.VMEM((2, 2, rows, width), jnp.float32),
        pltpu.VMEM((2, 2, rows, width), jnp.float32),
        pltpu.VMEM(wk.shape, jnp.float32),
        pltpu.VMEM(wv.shape, jnp.float32),
        pltpu.VMEM(going, jnp.float32),
        pltpu.VMEM((slots, piece_rows, enc), jnp.float32),
    ]
    scratch += ring(out_rows, width) + ring(out_rows, width) + ring(enc_rows, 2 * width)
    scratch += [pltpu.VMEM((out_rows, width), jnp.float32)] * 2
    scratch += [dma((17,))] * 2 + [dma((40,))] * 2 + [dma((8,))] * 6 + [dma((4,))] * 2
    scratch += [dma((groups,))] * 2 + [dma((4,)), dma((2,)), dma((6,))]
    return pl.pallas_call(
        reduce_kernel,
        out_shape=[
            f32(tokens, width),
            f32(*going),
            f32(out_rows, width),
            f32(out_rows, width),
            f32(enc_rows, width),
            f32(enc_rows, width),
        ],
        in_specs=vmem(2) + smem(1) + hbm(8),
        out_specs=vmem(6),
        scratch_shapes=scratch,
        compiler_params=pltpu.CompilerParams(
            collective_id=1, has_side_effects=True, vmem_limit_bytes=REDUCE_LIMIT
        ),
        cost_estimate=pl.CostEstimate(flops=50_000_000_000, bytes_accessed=60_000_000, transcendentals=0),
    )(dq, att, inst_of, dk, dv, hid, cot, nei, wq, wk, wv)


def body(
    hidden_states, out_cotangent, enc_table, nbr_ids, owner_map, w_query, w_key, w_value, w_out
):
    groups = lax.axis_size("wide")
    width = hidden_states.shape[1]
    query_blocks = w_query.reshape(SIDE, SIDE, width, width)
    out_blocks = w_out.reshape(SIDE, SIDE, width, width)
    hid, cot, nei, query_pair, picks, _, inst_of, attended, d_query, d_keys, d_values = gather_call(
        hidden_states, out_cotangent, enc_table, nbr_ids.T, owner_map, query_blocks, out_blocks,
        w_key, w_value, groups,
    )
    grad_hidden, arrived, grad_query, grad_out, grad_key, grad_value = reduce_call(
        d_query, attended, inst_of, d_keys, d_values, hid, cot, nei, query_pair, w_key, w_value,
        groups,
    )
    sums = (grad_hidden, grad_query, grad_key, grad_value, grad_out)
    grad_table, *sums = pl.pallas_call(
        result_kernel,
        out_shape=[f32(*enc_table.shape)] + [f32(*t.shape) for t in sums],
        in_specs=smem(1) + vmem(6),
        out_specs=vmem(6),
    )(picks, arrived, *sums)
    return (*sums, grad_table)


def solution(mesh):
    placed = (
        P("wide", "narrow"),
        P("wide", "narrow"),
        P("wide", "narrow", None),
        P(),
        P(),
        P(None, "narrow"),
        P(None, "narrow"),
        P(None, "narrow"),
        P(None, "narrow"),
    )
    return jax.shard_map(
        body,
        mesh=mesh,
        in_specs=placed,
        out_specs=(
            P("wide", "narrow"),
            P("wide", "narrow"),
            P("wide", "narrow"),
            P("wide", "narrow"),
            P("wide", "narrow"),
            P("wide", "narrow", None),
        ),
        check_vma=False,
    )
```
